32 devices in a mesh: expert: 8 (over y, x, core), feat: 4 (over z).
Axes of the slice: x: 2, y: 2, z: 4, core: 2. Of those that a mesh axis runs over, the one named last changes fastest.
Arguments:
- tokens: bfloat16 [512, 2304], P('expert'), may hold values from -6 to 6
- expert_ids: int32 [512, 8], P(('expert', 'feat')), may hold values from 0 to 31, all different within a row; in each aligned block of 16 rows (0 to 15, 16 to 31, ...) at most 8 rows name the same one
- gate_weights: float32 [512, 8], P(('expert', 'feat')), may hold values from 0.1 to 0.6
- expert_gate: bfloat16 [32, 2304, 1024], P(('expert', 'feat')), may hold values from -0.125 to 0.125
- expert_up: bfloat16 [32, 2304, 1024], P(('expert', 'feat')), may hold values from -0.125 to 0.125
- expert_down: bfloat16 [32, 1024, 2304], P(('expert', 'feat')), may hold values from -0.1875 to 0.1875
- shared_gate: bfloat16 [2304, 1024], P(None, 'feat'), may hold values from -0.125 to 0.125
- shared_up: bfloat16 [2304, 1024], P(None, 'feat'), may hold values from -0.125 to 0.125
- shared_down: bfloat16 [1024, 2304], P('feat'), may hold values from -0.1875 to 0.1875
- encoder: bfloat16 [2304, 16384], P(None, ('expert', 'feat')), may hold values from -0.125 to 0.125
- encoder_bias: float32 [16384], P(('expert', 'feat')), may hold values from -0.6 to 0.2
- decoder: bfloat16 [16384, 2304], P(('expert', 'feat')), may hold values from -0.046875 to 0.046875
- decoder_bias: float32 [2304], replicated, may hold values from -3 to 3
Outputs:
- features: bfloat16 [512, 16384], P(None, ('expert', 'feat'))
- reconstruction: float32 [512, 2304], P(('expert', 'feat'))
The draws below stay inside these ranges and needn't reach their ends.
Inputs may be any that keep to these rules, and one draw needn't show every extreme that they name: `expert_ids`: each row names 8 different experts. Within each aligned block of 16 rows (the rows of one device) no expert is named by more than 8 rows, a bound that some block reaches.
All inputs are finite; a program needn't handle non-finite values.
Results may differ from the reference program's by a relative error of at most 0.012.
Values may be sent and summed in bfloat16 or wider, within the bound.
No kernel may reach another device: no remote copies, remote signals or barrier semaphores. Data moves between devices by JAX's collectives and lax.ppermute only.
A program may use at most 128 MiB of HBM per device.

```python
import math
import jax
import jax.numpy as jnp
import numpy as np
from jax import lax

D = 2304
HID = 1024
SHARED = 1024
TOP = 8
TOK_DEV = 16
EXPERTS = 32
FEATURES = 16384
TOKENS = 512
CAP = 8
N_EXPERT = 8
N_FEAT = 4


def levels(stream_key, dims, cuts, low, largest):
    factor_of, own = 1.0, jax.random.fold_in(stream_key, 6)
    for dim, blocks in cuts:
        steps = jnp.exp(jax.random.uniform(jax.random.fold_in(own, dim), (blocks,), jnp.float32, low / len(cuts), largest / len(cuts)))
        factor_of = factor_of * jnp.repeat(steps, dims[dim] // blocks).reshape([-1 if axis == dim else 1 for axis in range(len(dims))])
    return factor_of


def deal_out(own_key, own, number, rows, number_of, top, most, skew):
    sequence = jax.random.permutation(own_key, number_of)
    heavy_load, common = load_shares(number_of, rows * top, most, skew, True), load_shares(number_of, rows * top, most, skew, False)
    places = jnp.arange(number_of)

    def named(sizes, turn):
        used = int((sizes > 0).sum())
        fixed = max(1, used // 4)
        moved = fixed + (places - fixed + turn * (used - fixed)) % max(1, number_of - fixed)
        return jnp.zeros((number_of,), jnp.int32).at[sequence[jnp.where(places < fixed, places, moved)]].set(jnp.asarray(sizes, jnp.int32))

    sizes = jnp.where(number % 4 == 0, named(heavy_load, number // 4), named(common, number - number // 4 - 1))
    mixed = jax.random.permutation(jax.random.fold_in(own, 3), number_of)
    donor, sink = mixed[0:number_of // 2 * 2:2], mixed[1:number_of // 2 * 2:2]
    room = jnp.minimum(sizes[donor] - 1, most - sizes[sink]) // 2
    room = jnp.where((donor == sequence[0]) | (sink == sequence[0]) | (sizes[sink] == 0), 0, jnp.maximum(room, 0))
    moved = jax.random.randint(jax.random.fold_in(own, 4), (number_of // 2,), 0, 1 << 20) % (room + 1)
    sizes = sizes.at[donor].add(-moved).at[sink].add(moved)
    members = jnp.searchsorted(jnp.cumsum(sizes), jnp.arange(rows * top), side="right").astype(jnp.int32)
    table = members.reshape(top, rows).T
    table = table[jax.random.permutation(jax.random.fold_in(own, 1), rows)]
    turn = jax.random.randint(jax.random.fold_in(own, 2), (rows, 1), 0, top)
    return jnp.take_along_axis(table, (jnp.arange(top)[None, :] + turn) % top, axis=1)


def load_shares(amount, total, most, skew, full):
    portions = [(1 << 20) // math.isqrt(grade ** skew) + 1 for grade in range(1, amount + 1)]
    largest = most if full else min(most, max(-(-total // amount), total * portions[0] // sum(portions)))
    least = 1 if total - largest >= amount - 1 else 0
    given, surplus = [largest] + [least] * (amount - 1), total - largest - least * (amount - 1)
    while surplus > 0:
        free = [i for i in range(1, amount) if given[i] < largest] or [i for i in range(1, amount) if given[i] < most]
        pool, remaining = sum([portions[i] for i in free]), surplus
        for i in free:
            addition = min(most - given[i], max(1, remaining * portions[i] // pool), surplus)
            given[i] = given[i] + addition
            surplus = surplus - addition
    return np.array(given)


def noise(own_key, dims, width, most, split=(), held_as=jnp.bfloat16):
    drawn = width * jax.random.normal(own_key, dims, jnp.float32)
    if split:
        drawn = drawn * levels(own_key, dims, split, -0.22, 0.18)
    return jnp.clip(drawn, -most, most).astype(held_as)


def setup_inputs(seed: int = 0) -> dict:
    splits = jax.random.split(jax.random.key(seed), 14)
    tokens = noise(splits[0], (TOKENS, D), 1.0, 6.0, ((0, 8),))
    expert_ids_keys = jax.random.split(jax.random.fold_in(splits[1], 1), TOKENS // TOK_DEV)
    expert_ids_turns = jax.random.permutation(jax.random.fold_in(splits[1], 3), TOKENS // TOK_DEV)
    expert_ids = jax.vmap(lambda own, number: deal_out(jax.random.fold_in(splits[1], 2), own, number, TOK_DEV, EXPERTS, TOP, CAP, 2))(expert_ids_keys, expert_ids_turns).reshape((TOKENS, TOP))
    gate_weights = jnp.clip(0.1 + 0.5 * jax.random.uniform(splits[2], (TOKENS, TOP), jnp.float32) ** levels(splits[2], (TOKENS, TOP), ((0, 32),), -0.2, 0.2), 0.1, 0.6)
    expert_gate = noise(splits[3], (EXPERTS, D, HID), D ** -0.5, 0.125, ((0, 32),))
    expert_up = noise(splits[4], (EXPERTS, D, HID), D ** -0.5, 0.125, ((0, 32),))
    expert_down = noise(splits[5], (EXPERTS, HID, D), HID ** -0.5, 0.1875, ((0, 32),))
    shared_gate = noise(splits[6], (D, SHARED), D ** -0.5, 0.125, ((1, 4),))
    shared_up = noise(splits[7], (D, SHARED), D ** -0.5, 0.125, ((1, 4),))
    shared_down = noise(splits[8], (SHARED, D), SHARED ** -0.5, 0.1875, ((0, 4),))
    encoder = noise(splits[9], (D, FEATURES), D ** -0.5, 0.125, ((1, 32),))
    encoder_bias = jnp.clip(-0.6 + 0.8 * jax.random.uniform(splits[10], (FEATURES,), jnp.float32) ** levels(splits[10], (FEATURES,), ((0, 32),), -0.2, 0.2), -0.6, 0.2)
    decoder = noise(splits[11], (FEATURES, D), FEATURES ** -0.5, 0.046875, ((0, 32),))
    decoder_bias = noise(splits[12], (D,), 0.5, 3.0, (), jnp.float32)
    return dict(tokens=tokens, expert_ids=expert_ids, gate_weights=gate_weights, expert_gate=expert_gate, expert_up=expert_up, expert_down=expert_down, shared_gate=shared_gate, shared_up=shared_up, shared_down=shared_down, encoder=encoder, encoder_bias=encoder_bias, decoder=decoder, decoder_bias=decoder_bias)


def swiglu_block(row_block, weight_gate, weight_up, weight_down):
    gate_proj = jnp.dot(row_block, weight_gate, preferred_element_type=jnp.float32)
    up_proj = jnp.dot(row_block, weight_up, preferred_element_type=jnp.float32)
    hidden = (jax.nn.silu(gate_proj) * up_proj).astype(jnp.bfloat16)
    return jnp.dot(hidden, weight_down, preferred_element_type=jnp.float32).astype(jnp.bfloat16)


def reference(tokens, expert_ids, gate_weights, expert_gate, expert_up, expert_down, shared_gate, shared_up, shared_down, encoder, encoder_bias, decoder, decoder_bias):
    devices = N_EXPERT * N_FEAT
    pair_count = TOK_DEV * TOP
    blocks = expert_ids.reshape(devices, pair_count).astype(jnp.int32)
    onehot = (blocks[:, :, None] == jnp.arange(EXPERTS, dtype=jnp.int32)[None, None, :]).astype(jnp.int32)
    earlier = (jnp.cumsum(onehot, axis=1) - onehot).astype(jnp.int32)
    slot_index = jnp.sum(earlier * onehot, axis=2).astype(jnp.int32)
    source = jnp.arange(devices, dtype=jnp.int32)[:, None]
    row_place = ((blocks * devices + source) * CAP + slot_index).reshape(-1).astype(jnp.int32)
    token_index = jnp.repeat(jnp.arange(TOKENS, dtype=jnp.int32), TOP)
    token_table = jnp.full((EXPERTS * devices * CAP,), TOKENS, jnp.int32).at[row_place].set(token_index)
    padded = jnp.concatenate([tokens, jnp.zeros((1, D), tokens.dtype)], axis=0)

    def one_expert(operands):
        index_rows, weight_gate, weight_up, weight_down = operands
        return swiglu_block(padded[index_rows], weight_gate, weight_up, weight_down)

    outputs = lax.map(one_expert, (token_table.reshape(EXPERTS, devices * CAP), expert_gate, expert_up, expert_down))
    gathered = outputs.reshape(-1, D)[row_place].reshape(TOKENS, TOP, D)
    routed = jnp.einsum("tk,tkd->td", gate_weights.astype(jnp.float32), gathered.astype(jnp.float32), precision=lax.Precision.HIGHEST).astype(jnp.bfloat16)
    shared = swiglu_block(tokens, shared_gate, shared_up, shared_down)
    moe_out = (routed.astype(jnp.float32) + shared.astype(jnp.float32)).astype(jnp.bfloat16)
    features = jax.nn.relu(jnp.dot(moe_out, encoder, preferred_element_type=jnp.float32) + encoder_bias[None, :]).astype(jnp.bfloat16)
    reconstruction = jnp.dot(features, decoder, preferred_element_type=jnp.float32) + decoder_bias[None, :]
    return features, reconstruction
```

```python
import jax
import jax.numpy as jnp
from jax import lax
from jax.sharding import PartitionSpec as P


def swap(value, axis, bit):
    count = lax.axis_size(axis)
    return lax.ppermute(value, axis, [(i, i ^ bit) for i in range(count)])


def bits_of(axis):
    count = lax.axis_size(axis)
    assert count & (count - 1) == 0
    return [(axis, 1 << b) for b in range(count.bit_length() - 1)]


def gather(value, held, order, dims):
    held = list(held)
    for bit in order:
        held = [d for d in dims if d in held or d == bit]
        value = jnp.stack([value, swap(value, *bit)], axis=held.index(bit))
    return value


def reduce_bits(value, held, order):
    held = list(held)
    for bit in order:
        place = held.index(bit)
        sent = lax.index_in_dim(value, 1, place, keepdims=False).astype(jnp.bfloat16)
        kept = lax.index_in_dim(value, 0, place, keepdims=False)
        value = kept + swap(sent, *bit).astype(jnp.float32)
        held.remove(bit)
    return value


def relative(value, axis):
    me = lax.axis_index(axis)
    blocks = [lax.dynamic_index_in_dim(value, i ^ me, 0) for i in range(value.shape[0])]
    return jnp.concatenate(blocks, axis=0)


def dot(a, b):
    return jnp.dot(a, b, preferred_element_type=jnp.float32)


def shards(
    tokens,
    expert_ids,
    gate_weights,
    expert_gate,
    expert_up,
    expert_down,
    shared_gate,
    shared_up,
    shared_down,
    encoder,
    encoder_bias,
    decoder,
    decoder_bias,
):
    own, top = expert_ids.shape
    width = tokens.shape[1]
    e_bits, f_bits = bits_of("expert"), bits_of("feat")
    devices = lax.axis_size(("expert", "feat"))
    dims = e_bits + f_bits[::-1]
    feat_dims = f_bits[::-1]
    first, plane = e_bits[0], e_bits[1:]
    half = (width // 2 + 127) // 128 * 128
    streams = [(slice(0, half), plane), (slice(half, width), plane[::-1])]
    local_experts = expert_gate.shape[0]
    me = lax.axis_index(("expert", "feat"))

    table = jnp.concatenate([expert_ids.astype(jnp.float32), gate_weights], axis=1)
    table = gather(table, [], f_bits + plane + [first], dims).reshape(-1, 2 * top)
    ids, weights = table[:, :top].astype(jnp.int32), table[:, top:]

    mine = relative(tokens.reshape(-1, own, width), "feat")
    mine = mine.reshape((2,) * len(f_bits) + (own, width))
    parts = [gather(mine[..., cols], feat_dims, order, dims) for cols, order in streams]
    near = jnp.concatenate(parts, axis=-1).reshape(-1, width)
    far = swap(near, *first)

    def expert(rows):
        out = []
        for j in range(local_experts):
            hidden = (
                jax.nn.silu(dot(rows, expert_gate[j])) * dot(rows, expert_up[j])
            ).astype(jnp.bfloat16)
            out.append(hidden)
        return out

    n = near.shape[0]
    hidden_near, hidden_far = expert(near), expert(far)
    shared_rows = mine.reshape(-1, width)
    shared_rows = (
        jax.nn.silu(dot(shared_rows, shared_gate)) * dot(shared_rows, shared_up)
    ).astype(jnp.bfloat16)
    scale = [
        jnp.sum(jnp.where(ids == me * local_experts + j, weights, 0.0), axis=1)[:, None]
        for j in range(local_experts)
    ]
    moe = []
    rest = [d for d in dims if d != first]
    for cols, order in streams:
        far_out = sum(
            dot(hidden_far[j], expert_down[j][:, cols]) * scale[j][n:] for j in range(local_experts)
        )
        far_out = swap(far_out.astype(jnp.bfloat16), *first)
        near_out = sum(
            dot(hidden_near[j], expert_down[j][:, cols]) * scale[j][:n] for j in range(local_experts)
        )
        total = near_out + far_out.astype(jnp.float32)
        total = total.reshape((2,) * len(rest) + (own, -1))
        total = reduce_bits(total, rest, order)
        shared_out = dot(shared_rows, shared_down[:, cols])
        total = total + shared_out.reshape(total.shape)
        total = reduce_bits(total, feat_dims, f_bits)
        out = total.astype(jnp.bfloat16)
        out = gather(out, [], f_bits[::-1] + order[::-1], dims)
        moe.append(out)
    near = jnp.concatenate(moe, axis=-1).reshape(-1, width)
    far = swap(near, *first)

    features_near = jax.nn.relu(dot(near, encoder) + encoder_bias[None, :]).astype(jnp.bfloat16)
    features_far = jax.nn.relu(dot(far, encoder) + encoder_bias[None, :]).astype(jnp.bfloat16)

    recon = []
    for cols, order in streams:
        far_out = swap(dot(features_far, decoder[:, cols]).astype(jnp.bfloat16), *first)
        total = dot(features_near, decoder[:, cols]) + far_out.astype(jnp.float32)
        total = total.reshape((2,) * len(rest) + (own, -1))
        recon.append(reduce_bits(total, rest, order + f_bits))
    reconstruction = jnp.concatenate(recon, axis=-1) + decoder_bias[None, :]

    features = jnp.concatenate([features_near, features_far], axis=0)
    features = features.reshape((2,) * len(dims) + (own, -1))
    wanted = e_bits[::-1] + f_bits[::-1]
    features = jnp.transpose(
        features, [dims.index(d) for d in wanted] + [len(dims), len(dims) + 1]
    ).reshape(devices, own, -1)
    features = relative(features, ("expert", "feat")).reshape(devices * own, -1)
    return (features, reconstruction)


def solution(mesh):
    return jax.shard_map(
        shards,
        mesh=mesh,
        in_specs=(
            P("expert", None),
            P(("expert", "feat"), None),
            P(("expert", "feat"), None),
            P(("expert", "feat"), None, None),
            P(("expert", "feat"), None, None),
            P(("expert", "feat"), None, None),
            P(None, "feat"),
            P(None, "feat"),
            P("feat", None),
            P(None, ("expert", "feat")),
            P(("expert", "feat")),
            P(("expert", "feat"), None),
            P(),
        ),
        out_specs=(P(None, ("expert", "feat")), P(("expert", "feat"), None)),
        check_vma=False,
    )
```

```python
import jax
import jax.numpy as jnp
from jax import lax
from jax.sharding import PartitionSpec as P

CHUNKS = 2


def swap(value, axis, r):
    return lax.ppermute(value, axis, [(i, i ^ r) for i in range(lax.axis_size(axis))])


def dot(a, b):
    return jnp.dot(a, b, preferred_element_type=jnp.float32)


def half(value):
    return value.astype(jnp.bfloat16)


def full(value):
    return value.astype(jnp.float32)


def routing_table(expert_ids, gate_weights, planes, feats):
    own, top = expert_ids.shape
    high = half(gate_weights)
    low = half(gate_weights - full(high))
    row = jnp.concatenate([half(expert_ids), high, low], axis=1)
    row = jnp.pad(row, ((0, 0), (0, 128 - 3 * top)))
    mine = jnp.arange(feats, dtype=jnp.int32)[:, None, None] == lax.axis_index("feat")
    table = jnp.where(mine, row[None], jnp.zeros_like(row)[None])
    bit = 1
    while bit < feats:
        table = table + swap(table, "feat", bit)
        bit *= 2
    table = table[None]
    bit = 1
    while bit < planes:
        table = jnp.concatenate([table, swap(table, "expert", 2 * bit)], axis=0)
        bit *= 2
    return table, swap(table, "expert", 1)


def chunk_rows(value, planes, feats):
    own = value.shape[2]
    value = value.reshape(planes, feats, CHUNKS, own // CHUNKS, value.shape[-1])
    return value.transpose(2, 0, 1, 3, 4).reshape(-1, value.shape[-1])


def shards(
    tokens,
    expert_ids,
    gate_weights,
    expert_gate,
    expert_up,
    expert_down,
    shared_gate,
    shared_up,
    shared_down,
    encoder,
    encoder_bias,
    decoder,
    decoder_bias,
):
    own, top = expert_ids.shape
    width = tokens.shape[1]
    feats = lax.axis_size("feat")
    planes = lax.axis_size("expert") // 2
    devices = 2 * planes * feats
    local_experts = expert_gate.shape[0]
    me = lax.axis_index(("expert", "feat"))
    my_feat = lax.axis_index("feat")
    step = own // CHUNKS
    rows = planes * feats * step

    table_near, table_far = routing_table(expert_ids, gate_weights, planes, feats)

    pieces = [tokens] + [swap(tokens, "expert", 2 * p) for p in range(1, planes)]
    near = chunk_rows(jnp.stack(pieces).reshape(planes, feats, own, width), planes, feats)
    far = swap(near, "expert", 1)

    def scales(table):
        table = chunk_rows(table, planes, feats)
        ids = table[:, :top].astype(jnp.int32)
        weights = full(table[:, top : 2 * top]) + full(table[:, 2 * top : 3 * top])
        return [
            jnp.sum(jnp.where(ids == me * local_experts + j, weights, 0.0), axis=1)[:, None]
            for j in range(local_experts)
        ]

    def swiglu(x, gate, up):
        return half(jax.nn.silu(dot(x, gate)) * dot(x, up))

    def expert_hidden(x):
        return [swiglu(x, expert_gate[j], expert_up[j]) for j in range(local_experts)]

    def expert_out(hidden, scale, c):
        cut = slice(c * rows, (c + 1) * rows)
        return sum(
            dot(hidden[j][cut], expert_down[j]) * scale[j][cut] for j in range(local_experts)
        )

    hidden_near = expert_hidden(near)
    scale_near, scale_far = scales(table_near), scales(table_far)
    received = [
        swap(half(expert_out(hidden_near, scale_near, c)), "expert", 1) for c in range(CHUNKS)
    ]
    hidden_far = expert_hidden(far)
    shared_rows = far.reshape(CHUNKS, planes, feats * step, width)[:, 0]
    shared_rows = shared_rows.reshape(CHUNKS * feats * step, width)
    shared_out = dot(swiglu(shared_rows, shared_gate, shared_up), shared_down)
    shared_out = shared_out.reshape(CHUNKS, feats, step, width)

    near_rows = []
    for c in range(CHUNKS):
        total = expert_out(hidden_far, scale_far, c) + full(received[c])
        total = total.reshape(planes, feats, step, width)
        arrived = [swap(half(total[p]), "expert", 2 * p) for p in range(1, planes)]
        total = total[0] + shared_out[c] + sum(full(a) for a in arrived)
        block = [lax.dynamic_index_in_dim(total, my_feat ^ r, 0, False) for r in range(feats)]
        arrived = [swap(half(block[r]), "feat", r) for r in range(1, feats)]
        moe_out = half(block[0] + sum(full(a) for a in arrived))
        pieces = jnp.stack([moe_out] + [swap(moe_out, "feat", r) for r in range(1, feats)])
        pieces = [pieces] + [swap(pieces, "expert", 2 * p) for p in range(1, planes)]
        near_rows.append(jnp.stack(pieces).reshape(rows, width))

    def encode(x):
        return half(jax.nn.relu(dot(x, encoder) + encoder_bias[None, :]))

    features, reconstruction = [], []
    for c in range(CHUNKS):
        near, far = near_rows[c], swap(near_rows[c], "expert", 1)
        features_near = encode(near)
        arrived = swap(half(dot(features_near, decoder)), "expert", 1)
        features_far = encode(far)
        total = dot(features_far, decoder) + full(arrived)
        total = total.reshape(planes, feats, step, width)
        arrived = [swap(half(total[p]), "expert", 2 * p) for p in range(1, planes)]
        total = total[0] + sum(full(a) for a in arrived)
        arrived = [swap(half(total[r]), "feat", r) for r in range(1, feats)]
        reconstruction.append(total[0] + sum(full(a) for a in arrived) + decoder_bias[None, :])
        both = jnp.stack([features_far, features_near])
        features.append(both.reshape(2, planes, feats, step, -1))
    reconstruction = jnp.concatenate(reconstruction, axis=0)

    features = jnp.stack(features).transpose(2, 1, 3, 0, 4, 5).reshape(devices, own, -1)
    blocks = [lax.dynamic_index_in_dim(features, i ^ me, 0) for i in range(devices)]
    features = jnp.concatenate(blocks, axis=0).reshape(devices * own, -1)
    return (features, reconstruction)


def solution(mesh):
    return jax.shard_map(
        shards,
        mesh=mesh,
        in_specs=(
            P("expert", None),
            P(("expert", "feat"), None),
            P(("expert", "feat"), None),
            P(("expert", "feat"), None, None),
            P(("expert", "feat"), None, None),
            P(("expert", "feat"), None, None),
            P(None, "feat"),
            P(None, "feat"),
            P("feat", None),
            P(None, ("expert", "feat")),
            P(("expert", "feat")),
            P(("expert", "feat"), None),
            P(),
        ),
        out_specs=(P(None, ("expert", "feat")), P(("expert", "feat"), None)),
        check_vma=False,
    )
```

```python
import jax
import jax.numpy as jnp
from jax import lax
from jax.sharding import PartitionSpec as P

CHUNKS = 2


def pair_swap(value):
    return lax.ppermute(value, "expert", [(i, i ^ 1) for i in range(lax.axis_size("expert"))])


def exchange_pairs(blocks):
    count = lax.axis_size("expert")
    groups = [list(range(parity, count, 2)) for parity in range(2)]
    return lax.all_to_all(
        blocks, "expert", split_axis=0, concat_axis=0, axis_index_groups=groups, tiled=True
    )


def exchange_feats(blocks):
    return lax.all_to_all(blocks, "feat", split_axis=0, concat_axis=0, tiled=True)


def copies(value, count):
    return jnp.broadcast_to(value[None], (count,) + value.shape)


def dot(a, b):
    return jnp.dot(a, b, preferred_element_type=jnp.float32)


def half(value):
    return value.astype(jnp.bfloat16)


def full(value):
    return value.astype(jnp.float32)


def shards(
    tokens,
    expert_ids,
    gate_weights,
    expert_gate,
    expert_up,
    expert_down,
    shared_gate,
    shared_up,
    shared_down,
    encoder,
    encoder_bias,
    decoder,
    decoder_bias,
):
    own, top = expert_ids.shape
    width = tokens.shape[1]
    feats = lax.axis_size("feat")
    pairs = lax.axis_size("expert") // 2
    devices = 2 * pairs * feats
    local_experts = expert_gate.shape[0]
    parity = lax.axis_index("expert") % 2
    step = own // CHUNKS
    rows = pairs * feats * step

    names = jnp.arange(devices * local_experts, dtype=jnp.int32)
    weights = jnp.sum(
        jnp.where(expert_ids[None] == names[:, None, None], gate_weights[None], 0.0), axis=2
    )
    weights = lax.all_to_all(
        weights.reshape(devices, local_experts, own),
        ("expert", "feat"),
        split_axis=0,
        concat_axis=0,
        tiled=True,
    )

    def chunk_rows(value):
        value = value.reshape(pairs, feats, CHUNKS, step, value.shape[-1])
        return value.transpose(2, 0, 1, 3, 4).reshape(-1, value.shape[-1])

    near = chunk_rows(exchange_pairs(copies(tokens, pairs)).reshape(pairs, feats, own, width))
    far = pair_swap(near)

    weights = weights.reshape(pairs, 2, feats, local_experts, own)
    even, odd = weights[:, 0], weights[:, 1]

    def scales(own_parity):
        value = jnp.where((parity == 0) == own_parity, even, odd)
        value = chunk_rows(value.transpose(0, 1, 3, 2))
        return [value[:, j : j + 1] for j in range(local_experts)]

    def swiglu(x, gate, up):
        return half(jax.nn.silu(dot(x, gate)) * dot(x, up))

    def expert_hidden(x):
        return [swiglu(x, expert_gate[j], expert_up[j]) for j in range(local_experts)]

    def expert_out(hidden, scale, c):
        cut = slice(c * rows, (c + 1) * rows)
        return sum(
            dot(hidden[j][cut], expert_down[j]) * scale[j][cut] for j in range(local_experts)
        )

    hidden_near = expert_hidden(near)
    scale_near, scale_far = scales(True), scales(False)
    received = [pair_swap(half(expert_out(hidden_near, scale_near, c))) for c in range(CHUNKS)]
    hidden_far = expert_hidden(far)
    my_pair = lax.axis_index("expert") // 2
    shared_rows = far.reshape(CHUNKS, pairs, feats * step, width)
    shared_rows = lax.dynamic_index_in_dim(shared_rows, my_pair, 1, False)
    shared_rows = shared_rows.reshape(CHUNKS * feats * step, width)
    shared_out = dot(swiglu(shared_rows, shared_gate, shared_up), shared_down)
    shared_out = shared_out.reshape(CHUNKS, feats, step, width)

    near_rows = []
    for c in range(CHUNKS):
        total = half(expert_out(hidden_far, scale_far, c) + full(received[c]))
        total = exchange_pairs(total.reshape(pairs, feats, step, width))
        total = half(jnp.sum(full(total), axis=0) + shared_out[c])
        moe_out = half(jnp.sum(full(exchange_feats(total)), axis=0))
        gathered = exchange_feats(copies(moe_out, feats))
        gathered = exchange_pairs(copies(gathered, pairs))
        near_rows.append(gathered.reshape(rows, width))

    def encode(x):
        return half(jax.nn.relu(dot(x, encoder) + encoder_bias[None, :]))

    features, reconstruction = [], []
    for c in range(CHUNKS):
        near, far = near_rows[c], pair_swap(near_rows[c])
        features_near = encode(near)
        arrived = pair_swap(half(dot(features_near, decoder)))
        features_far = encode(far)
        total = half(dot(features_far, decoder) + full(arrived))
        total = exchange_pairs(total.reshape(pairs, feats, step, width))
        total = exchange_feats(half(jnp.sum(full(total), axis=0)))
        reconstruction.append(jnp.sum(full(total), axis=0) + decoder_bias[None, :])
        both = [
            jnp.where(parity == 0, features_far, features_near),
            jnp.where(parity == 0, features_near, features_far),
        ]
        features.append(jnp.stack(both).reshape(2, pairs, feats, step, -1))
    reconstruction = jnp.concatenate(reconstruction, axis=0)
    features = jnp.stack(features).transpose(2, 1, 3, 0, 4, 5).reshape(devices * own, -1)
    return (features, reconstruction)


def solution(mesh):
    return jax.shard_map(
        shards,
        mesh=mesh,
        in_specs=(
            P("expert", None),
            P(("expert", "feat"), None),
            P(("expert", "feat"), None),
            P(("expert", "feat"), None, None),
            P(("expert", "feat"), None, None),
            P(("expert", "feat"), None, None),
            P(None, "feat"),
            P(None, "feat"),
            P("feat", None),
            P(None, ("expert", "feat")),
            P(("expert", "feat")),
            P(("expert", "feat"), None),
            P(),
        ),
        out_specs=(P(None, ("expert", "feat")), P(("expert", "feat"), None)),
        check_vma=False,
    )
```

```python
import jax
import jax.numpy as jnp
from jax import lax
from jax.sharding import PartitionSpec as P

CHUNKS = 2


def swap(value, axis, r):
    return lax.ppermute(value, axis, [(i, i ^ r) for i in range(lax.axis_size(axis))])


def dot(a, b):
    return jnp.dot(a, b, preferred_element_type=jnp.float32)


def half(value):
    return value.astype(jnp.bfloat16)


def full(value):
    return value.astype(jnp.float32)


def bits_of(count):
    assert count & (count - 1) == 0
    return [1 << b for b in range(count.bit_length() - 1)]


def take(value, index, dim):
    return lax.dynamic_index_in_dim(value, index, dim, keepdims=False)


def gather_pairs(value):
    pairs = lax.axis_size("expert") // 2
    return jnp.stack([value] + [swap(value, "expert", 2 * p) for p in range(1, pairs)])


def reduce_pairs(value):
    arrived = [swap(half(value[p]), "expert", 2 * p) for p in range(1, value.shape[0])]
    return value[0] + sum(full(a) for a in arrived)


def shards(
    tokens,
    expert_ids,
    gate_weights,
    expert_gate,
    expert_up,
    expert_down,
    shared_gate,
    shared_up,
    shared_down,
    encoder,
    encoder_bias,
    decoder,
    decoder_bias,
):
    own, top = expert_ids.shape
    width = tokens.shape[1]
    feats = lax.axis_size("feat")
    pairs = lax.axis_size("expert") // 2
    devices = 2 * pairs * feats
    local_experts = expert_gate.shape[0]
    me = lax.axis_index(("expert", "feat"))
    my_feat = lax.axis_index("feat")
    feat_bits = bits_of(feats)
    step = own // CHUNKS
    rows = pairs * feats * step

    high = half(gate_weights)
    low = half(gate_weights - full(high))
    row = jnp.concatenate([half(expert_ids), high, low], axis=1)
    mine = jnp.arange(feats, dtype=jnp.int32)[:, None, None] == my_feat
    table = jnp.where(mine, row[None], jnp.zeros_like(row)[None])
    table = table.reshape(feats, CHUNKS, step, 3 * top).transpose(0, 2, 1, 3)
    lanes = -(-CHUNKS * 3 * top // 128) * 128
    table = table.reshape(feats * step, CHUNKS * 3 * top)
    table = jnp.pad(table, ((0, 0), (0, lanes - table.shape[1])))
    for bit in feat_bits:
        table = table + swap(table, "feat", bit)

    parts = tokens.reshape(feats, CHUNKS, step, width)
    parts = [parts[:, c].reshape(feats * step, width) for c in range(CHUNKS)]
    parts[-1] = jnp.concatenate([parts[-1], table], axis=1)
    both = []
    for part in parts:
        near = gather_pairs(part).reshape(rows, -1)
        both.append(jnp.concatenate([near, swap(near, "expert", 1)], axis=0))
    tables = both[-1][:, width:]
    both[-1] = both[-1][:, :width]

    def scales(c):
        ids = tables[:, c * 3 * top :][:, :top].astype(jnp.int32)
        weights = full(tables[:, (c * 3 + 1) * top :][:, :top])
        weights = weights + full(tables[:, (c * 3 + 2) * top :][:, :top])
        return [
            jnp.sum(jnp.where(ids == me * local_experts + j, weights, 0.0), axis=1)[:, None]
            for j in range(local_experts)
        ]

    def swiglu(x, gate, up):
        return half(jax.nn.silu(dot(x, gate)) * dot(x, up))

    def run_experts(x, scale):
        out = 0.0
        for j in range(local_experts):
            hidden = swiglu(x, expert_gate[j], expert_up[j])
            out = out + dot(hidden, expert_down[j]) * scale[j]
        return out

    near_rows = []
    for c in range(CHUNKS):
        out = run_experts(both[c], scales(c))
        shared_rows = both[c][rows : rows + feats * step]
        shared_out = dot(swiglu(shared_rows, shared_gate, shared_up), shared_down)
        total = out[rows:] + full(swap(half(out[:rows]), "expert", 1))
        total = reduce_pairs(total.reshape(pairs, feats * step, width)) + shared_out
        total = total.reshape((2,) * len(feat_bits) + (step, width))
        place = [(my_feat // bit) % 2 for bit in feat_bits]
        for i, bit in enumerate(feat_bits[:-1]):
            dim = len(feat_bits) - 1 - i
            arrived = swap(half(take(total, 1 - place[i], dim)), "feat", bit)
            total = take(total, place[i], dim) + full(arrived)
        total = half(total)
        moe_out = half(full(total) + full(swap(total, "feat", feat_bits[-1])))
        for i, bit in reversed(list(enumerate(feat_bits[:-1]))):
            moe_out = jnp.stack([moe_out, swap(moe_out, "feat", bit)], axis=1)
        near_rows.append(gather_pairs(moe_out).reshape(rows, width))

    def encode(x):
        return half(jax.nn.relu(dot(x, encoder) + encoder_bias[None, :]))

    features, reconstruction = [], []
    for c in range(CHUNKS):
        near, far = near_rows[c], swap(near_rows[c], "expert", 1)
        features_near = encode(near)
        arrived = swap(half(dot(features_near, decoder)), "expert", 1)
        features_far = encode(far)
        total = dot(features_far, decoder) + full(arrived)
        total = reduce_pairs(total.reshape(pairs, feats * step, width))
        total = total.reshape((2,) * len(feat_bits) + (step, width))
        for bit in feat_bits[:-1]:
            dim = len(total.shape) - 3
            arrived = swap(half(lax.index_in_dim(total, 1, dim, False)), "feat", bit)
            total = lax.index_in_dim(total, 0, dim, False) + full(arrived)
        arrived = swap(half(take(total, 1 - place[-1], 0)), "feat", feat_bits[-1])
        reconstruction.append(take(total, place[-1], 0) + full(arrived) + decoder_bias[None, :])
        both = jnp.stack([features_far, features_near])
        features.append(both.reshape(2, pairs, feats, step, -1))
    reconstruction = jnp.concatenate(reconstruction, axis=0)

    features = jnp.stack(features).transpose(2, 1, 3, 0, 4, 5).reshape(devices, own, -1)
    relative = me - me % feats + my_feat % (feats // 2)
    blocks = [lax.dynamic_index_in_dim(features, i ^ relative, 0) for i in range(devices)]
    features = jnp.concatenate(blocks, axis=0).reshape(devices * own, -1)
    return (features, reconstruction)


def solution(mesh):
    return jax.shard_map(
        shards,
        mesh=mesh,
        in_specs=(
            P("expert", None),
            P(("expert", "feat"), None),
            P(("expert", "feat"), None),
            P(("expert", "feat"), None, None),
            P(("expert", "feat"), None, None),
            P(("expert", "feat"), None, None),
            P(None, "feat"),
            P(None, "feat"),
            P("feat", None),
            P(None, ("expert", "feat")),
            P(("expert", "feat")),
            P(("expert", "feat"), None),
            P(),
        ),
        out_specs=(P(None, ("expert", "feat")), P(("expert", "feat"), None)),
        check_vma=False,
    )
```

```python
import functools

import jax
import jax.numpy as jnp
from jax import lax
from jax.experimental import pallas as pl
from jax.experimental.pallas import tpu as pltpu
from jax.sharding import PartitionSpec as P

CHUNKS = 2
LANES = 128
VMEM = 24 * 1024 * 1024


def swap(value, axis, r):
    return lax.ppermute(value, axis, [(i, i ^ r) for i in range(lax.axis_size(axis))])


def dot(a, b):
    return jnp.dot(a, b, preferred_element_type=jnp.float32)


def half(value):
    return value.astype(jnp.bfloat16)


def full(value):
    return value.astype(jnp.float32)


def bits_of(count):
    assert count & (count - 1) == 0
    return [1 << b for b in range(count.bit_length() - 1)]


def take(value, index, dim):
    return lax.dynamic_index_in_dim(value, index, dim, keepdims=False)


def gather_pairs(value):
    pairs = lax.axis_size("expert") // 2
    return jnp.stack([value] + [swap(value, "expert", 2 * p) for p in range(1, pairs)])


def reduce_pairs(value):
    arrived = [swap(half(value[p]), "expert", 2 * p) for p in range(1, value.shape[0])]
    return value[0] + sum(full(a) for a in arrived)


def hidden_kernel(count, *refs):
    pieces, (gate, up, out, rows) = refs[:count], refs[count:]
    size = pieces[0].shape[0]

    @pl.when((pl.program_id(0) == 0) & (pl.program_id(1) == 0))
    def _():
        for i, piece in enumerate(pieces):
            rows[i * size : (i + 1) * size, :] = piece[...]

    value = dot(rows[...], gate[...])
    out[...] = half(value / (1.0 + jnp.exp(-value)) * dot(rows[...], up[...]))


def run_hidden(pieces, gate, up):
    count, (size, width) = len(pieces), pieces[0].shape
    experts, _, units = gate.shape
    tile = min(256, units)
    weight = pl.BlockSpec((None, width, tile), lambda e, j: (e, 0, j))
    return pl.pallas_call(
        functools.partial(hidden_kernel, count),
        grid=(experts, units // tile),
        in_specs=[pl.BlockSpec((size, width), lambda e, j: (0, 0))] * count + [weight] * 2,
        out_specs=pl.BlockSpec((None, count * size, tile), lambda e, j: (e, 0, j)),
        out_shape=jax.ShapeDtypeStruct((experts, count * size, units), jnp.bfloat16),
        scratch_shapes=[pltpu.VMEM((count * size, width), jnp.bfloat16)],
        compiler_params=pltpu.CompilerParams(vmem_limit_bytes=VMEM),
        cost_estimate=pl.CostEstimate(
            flops=4 * experts * count * size * width * units,
            bytes_accessed=4 * experts * width * units,
            transcendentals=experts * count * size * units,
        ),
    )(*pieces, gate, up)


def down_kernel(top, experts, parts, me, hidden, down, table, *refs):
    e = pl.program_id(1)
    entries = full(table[...])
    lane = lax.broadcasted_iota(jnp.int32, entries.shape, 1)
    expert = (me[0] * experts + e).astype(jnp.float32)
    chosen = jnp.where((entries == expert) & (lane < top), 1.0, 0.0)
    chosen = pltpu.roll(chosen, top, 1) + pltpu.roll(chosen, 2 * top, 1)
    scale = jnp.sum(chosen * entries, axis=1, keepdims=True)
    value = dot(hidden[...], down[...]) * scale
    if parts is None:
        outs, total = refs[:1], refs[1]
    else:
        arrived, outs, total = refs[0], refs[1:-1], refs[-1]

    @pl.when(e == 0)
    def _():
        total[...] = value if parts is None else value + full(arrived[...])

    @pl.when(e > 0)
    def _():
        total[...] += value

    @pl.when(e == experts - 1)
    def _():
        if parts is None:
            outs[0][...] = half(total[...])
        else:
            pairs, feats, step = parts
            split = total[...].reshape(pairs, feats, CHUNKS, step, -1)
            for i, out in enumerate(outs):
                block = split[i % pairs, :, i // pairs].reshape(feats * step, -1)
                out[...] = block.astype(out.dtype)


def run_down(hidden, down, table, me, top, arrived=None, parts=None):
    experts, rows, units = hidden.shape
    width = down.shape[2]
    tile = max(t for t in range(128, 769, 128) if width % t == 0)
    whole = pl.BlockSpec((rows, tile), lambda j, e: (0, j))
    in_specs = [
        pl.BlockSpec(memory_space=pltpu.SMEM),
        pl.BlockSpec((None, rows, units), lambda j, e: (e, 0, 0)),
        pl.BlockSpec((None, units, tile), lambda j, e: (e, 0, j)),
        pl.BlockSpec((rows, LANES), lambda j, e: (0, 0)),
    ]
    operands = [me.reshape(1), hidden, down, table]
    if arrived is None:
        out_specs = whole
        out_shape = jax.ShapeDtypeStruct((rows, width), jnp.bfloat16)
    else:
        in_specs.append(whole)
        operands.append(arrived)
        pairs, feats, step = parts
        out_specs = [pl.BlockSpec((feats * step, tile), lambda j, e: (0, j))] * (pairs * CHUNKS)
        out_shape = [
            jax.ShapeDtypeStruct((feats * step, width), jnp.bfloat16 if i % pairs else jnp.float32)
            for i in range(pairs * CHUNKS)
        ]
    return pl.pallas_call(
        functools.partial(down_kernel, top, experts, parts),
        grid=(width // tile, experts),
        in_specs=in_specs,
        out_specs=out_specs,
        out_shape=out_shape,
        scratch_shapes=[pltpu.VMEM((rows, tile), jnp.float32)],
        compiler_params=pltpu.CompilerParams(vmem_limit_bytes=VMEM),
        cost_estimate=pl.CostEstimate(
            flops=2 * experts * rows * width * units,
            bytes_accessed=2 * experts * width * units,
            transcendentals=0,
        ),
    )(*operands)


def shared_kernel(feats, x, gate, up, down, *outs):
    value = dot(x[...], gate[...])
    hidden = half(value / (1.0 + jnp.exp(-value)) * dot(x[...], up[...]))
    value = dot(hidden, down[...])
    rows, width = value.shape
    value = value.reshape(feats, CHUNKS, rows // feats // CHUNKS, width)
    for c, out in enumerate(outs):
        out[...] = value[:, c].reshape(rows // CHUNKS, width)


def run_shared(x, gate, up, down, feats):
    rows, width = x.shape
    return pl.pallas_call(
        functools.partial(shared_kernel, feats),
        out_shape=[jax.ShapeDtypeStruct((rows // CHUNKS, width), jnp.float32)] * CHUNKS,
        compiler_params=pltpu.CompilerParams(vmem_limit_bytes=VMEM),
        cost_estimate=pl.CostEstimate(
            flops=6 * rows * gate.size, bytes_accessed=6 * gate.size, transcendentals=0
        ),
    )(x, gate, up, down)


def sum_kernel(step, place, *refs):
    parts, (kept, sent) = refs[:-2], refs[-2:]
    total = sum(full(part[...]) for part in parts)
    rows, width = total.shape
    total = total.reshape(rows // step // 2, 2, step, width)
    low, high = total[:, 0].reshape(-1, width), total[:, 1].reshape(-1, width)
    kept[...] = jnp.where(place[0] == 0, low, high)
    sent[...] = half(jnp.where(place[0] == 0, high, low))


def run_sum(parts, place, step):
    rows, width = parts[0].shape
    vmem = pl.BlockSpec(memory_space=pltpu.VMEM)
    return pl.pallas_call(
        functools.partial(sum_kernel, step),
        in_specs=[pl.BlockSpec(memory_space=pltpu.SMEM)] + [vmem] * len(parts),
        out_shape=[
            jax.ShapeDtypeStruct((rows // 2, width), jnp.float32),
            jax.ShapeDtypeStruct((rows // 2, width), jnp.bfloat16),
        ],
        compiler_params=pltpu.CompilerParams(vmem_limit_bytes=VMEM),
        cost_estimate=pl.CostEstimate(
            flops=rows * width * len(parts), bytes_accessed=2 * rows * width, transcendentals=0
        ),
    )(place.reshape(1), *parts)


def shards(
    tokens,
    expert_ids,
    gate_weights,
    expert_gate,
    expert_up,
    expert_down,
    shared_gate,
    shared_up,
    shared_down,
    encoder,
    encoder_bias,
    decoder,
    decoder_bias,
):
    own, top = expert_ids.shape
    width = tokens.shape[1]
    feats = lax.axis_size("feat")
    pairs = lax.axis_size("expert") // 2
    devices = 2 * pairs * feats
    me = lax.axis_index(("expert", "feat"))
    my_feat = lax.axis_index("feat")
    feat_bits = bits_of(feats)
    step = own // CHUNKS
    rows = pairs * feats * step

    high = half(gate_weights)
    low = half(gate_weights - full(high))
    row = jnp.concatenate([half(expert_ids), high, low], axis=1)
    row = jnp.pad(row, ((0, 0), (0, LANES - 3 * top)))
    mine = jnp.arange(feats, dtype=jnp.int32)[:, None, None] == my_feat
    table = jnp.where(mine, row[None], jnp.zeros_like(row)[None]).reshape(-1, LANES)
    for bit in feat_bits:
        table = table + swap(table, "feat", bit)
    for bit in bits_of(pairs):
        table = jnp.concatenate([table, swap(table, "expert", 2 * bit)], axis=0)
    table_far = swap(table, "expert", 1)

    near = [tokens] + [swap(tokens, "expert", 2 * p) for p in range(1, pairs)]
    far = [swap(piece, "expert", 1) for piece in near]
    shared_out = run_shared(far[0], shared_gate, shared_up, shared_down, feats)

    hidden_near = run_hidden(near, expert_gate, expert_up)
    out_near = run_down(hidden_near, expert_down, table, me, top)
    arrived = swap(out_near, "expert", 1)
    hidden_far = run_hidden(far, expert_gate, expert_up)
    blocks = run_down(hidden_far, expert_down, table_far, me, top, arrived, (pairs, feats, step))

    near_rows = []
    place = [(my_feat // bit) % 2 for bit in feat_bits]
    for c in range(CHUNKS):
        mine = blocks[c * pairs : (c + 1) * pairs]
        arrived = [swap(mine[p], "expert", 2 * p) for p in range(1, pairs)]
        total, sent = run_sum([mine[0], shared_out[c]] + arrived, place[0], step)
        total = total + full(swap(sent, "feat", feat_bits[0]))
        total = total.reshape((2,) * (len(feat_bits) - 1) + (step, width))
        for i, bit in enumerate(feat_bits[1:-1]):
            dim = len(feat_bits) - 2 - i
            arrived = swap(half(take(total, 1 - place[i + 1], dim)), "feat", bit)
            total = take(total, place[i + 1], dim) + full(arrived)
        total = half(total)
        moe_out = half(full(total) + full(swap(total, "feat", feat_bits[-1])))
        for bit in feat_bits[-2::-1]:
            moe_out = jnp.stack([moe_out, swap(moe_out, "feat", bit)], axis=moe_out.ndim - 2)
        near_rows.append(gather_pairs(moe_out).reshape(rows, width))

    def encode(x):
        return half(jax.nn.relu(dot(x, encoder) + encoder_bias[None, :]))

    features, reconstruction = [], []
    for c in range(CHUNKS):
        near, far = near_rows[c], swap(near_rows[c], "expert", 1)
        features_near = encode(near)
        arrived = swap(half(dot(features_near, decoder)), "expert", 1)
        features_far = encode(far)
        total = dot(features_far, decoder) + full(arrived)
        total = reduce_pairs(total.reshape(pairs, feats * step, width))
        total = total.reshape((2,) * len(feat_bits) + (step, width))
        for bit in feat_bits[:-1]:
            dim = len(total.shape) - 3
            arrived = swap(half(lax.index_in_dim(total, 1, dim, False)), "feat", bit)
            total = lax.index_in_dim(total, 0, dim, False) + full(arrived)
        arrived = swap(half(take(total, 1 - place[-1], 0)), "feat", feat_bits[-1])
        reconstruction.append(take(total, place[-1], 0) + full(arrived) + decoder_bias[None, :])
        both = jnp.stack([features_far, features_near])
        features.append(both.reshape(2, pairs, feats, step, -1))
    reconstruction = jnp.concatenate(reconstruction, axis=0)

    features = jnp.stack(features).transpose(2, 1, 3, 0, 4, 5).reshape(devices, own, -1)
    relative = me - me % feats + my_feat % (feats // 2)
    blocks = [lax.dynamic_index_in_dim(features, i ^ relative, 0) for i in range(devices)]
    features = jnp.concatenate(blocks, axis=0).reshape(devices * own, -1)
    return (features, reconstruction)


def solution(mesh):
    return jax.shard_map(
        shards,
        mesh=mesh,
        in_specs=(
            P("expert", None),
            P(("expert", "feat"), None),
            P(("expert", "feat"), None),
            P(("expert", "feat"), None, None),
            P(("expert", "feat"), None, None),
            P(("expert", "feat"), None, None),
            P(None, "feat"),
            P(None, "feat"),
            P("feat", None),
            P(None, ("expert", "feat")),
            P(("expert", "feat")),
            P(("expert", "feat"), None),
            P(),
        ),
        out_specs=(P(None, ("expert", "feat")), P(("expert", "feat"), None)),
        check_vma=False,
    )
```

```python
import functools

import jax
import jax.numpy as jnp
from jax import lax
from jax.experimental import pallas as pl
from jax.experimental.pallas import tpu as pltpu
from jax.sharding import PartitionSpec as P

CHUNKS = 2
LANES = 128
MIB = 1024 * 1024
LOAD_MIB = 36
VMEM_SPEC = pl.BlockSpec(memory_space=pltpu.VMEM)
SMEM_SPEC = pl.BlockSpec(memory_space=pltpu.SMEM)
HBM_SPEC = pl.BlockSpec(memory_space=pltpu.HBM)


def swap(value, axis, r):
    return lax.ppermute(value, axis, [(i, i ^ r) for i in range(lax.axis_size(axis))])


def dot(a, b):
    return jnp.dot(a, b, preferred_element_type=jnp.float32)


def half(value):
    return value.astype(jnp.bfloat16)


def full(value):
    return value.astype(jnp.float32)


def silu(value):
    return value / (1.0 + jnp.exp(-value))


def bits_of(count):
    assert count & (count - 1) == 0
    return [1 << b for b in range(count.bit_length() - 1)]


def take(value, index, dim):
    return lax.dynamic_index_in_dim(value, index, dim, keepdims=False)


def gather_pairs(value):
    pairs = lax.axis_size("expert") // 2
    return jnp.stack([value] + [swap(value, "expert", 2 * p) for p in range(1, pairs)])


def call(body, operands, specs, outs, scratch, mib, cost):
    flops, moved = cost
    return pl.pallas_call(
        body,
        in_specs=specs,
        out_specs=[VMEM_SPEC] * len(outs),
        out_shape=[jax.ShapeDtypeStruct(shape, dtype) for shape, dtype in outs],
        scratch_shapes=scratch,
        compiler_params=pltpu.CompilerParams(vmem_limit_bytes=mib * MIB),
        cost_estimate=pl.CostEstimate(flops=flops, bytes_accessed=moved, transcendentals=0),
    )(*operands)


def start_all(pairs, sems):
    copies = [pltpu.make_async_copy(a, b, sems.at[i]) for i, (a, b) in enumerate(pairs)]
    for copy in copies:
        copy.start()
    return copies


def pack_kernel(feats, feat, ids, weights, out):
    top, own = ids.shape
    lane = lax.broadcasted_iota(jnp.int32, (top, LANES), 1)
    row = lax.broadcasted_iota(jnp.int32, (top, LANES), 0)
    high = half(weights[...])
    low = half(weights[...] - full(high))
    values = jnp.zeros((own, LANES), jnp.float32)
    for i, part in enumerate([half(full(ids[...])), high, low]):
        places = half(jnp.where(lane == row + i * top, 1.0, 0.0))
        values += lax.dot_general(
            part, places, (((0,), (0,)), ((), ())), preferred_element_type=jnp.float32
        )
    for f in range(feats):
        out[f * own : (f + 1) * own, :] = half(jnp.where(feat[0] == f, values, 0.0))


def run_pack(feat, expert_ids, gate_weights, feats):
    own, top = expert_ids.shape
    return call(
        functools.partial(pack_kernel, feats),
        [feat.reshape(1), expert_ids.T, gate_weights.T],
        [SMEM_SPEC, VMEM_SPEC, VMEM_SPEC],
        [((feats * own, LANES), jnp.bfloat16)],
        [],
        2,
        (6 * own * top * LANES, 2 * feats * own * LANES),
    )[0]


def load_kernel(count, *refs):
    copies = start_all(list(zip(refs[:count], refs[count:-1])), refs[-1])
    for copy in copies:
        copy.wait()


def run_load(values, mib):
    count = len(values)
    return call(
        functools.partial(load_kernel, count),
        values,
        [HBM_SPEC] * count,
        [(value.shape, value.dtype) for value in values],
        [pltpu.SemaphoreType.DMA((count,))],
        mib,
        (0, 4 * sum(value.size for value in values)),
    )


def hidden_kernel(count, e, tile, *refs):
    pieces, (gate, up, out, rows) = refs[:count], refs[count:]
    size = pieces[0].shape[0]
    for i in range(count):
        rows[i * size : (i + 1) * size, :] = pieces[i][...]
    for j in range(0, out.shape[1], tile):
        cut = slice(j, j + tile)
        value = silu(dot(rows[...], gate[e, :, cut]))
        out[:, cut] = half(value * dot(rows[...], up[e, :, cut]))


def run_hidden(pieces, gate, up, e):
    count, (size, width) = len(pieces), pieces[0].shape
    units = gate.shape[2]
    return call(
        functools.partial(hidden_kernel, count, e, min(256, units)),
        [*pieces, gate, up],
        [VMEM_SPEC] * (count + 2),
        [((count * size, units), jnp.bfloat16)],
        [pltpu.VMEM((count * size, width), jnp.bfloat16)],
        8,
        (4 * count * size * width * units, 4 * width * units),
    )[0]


def down_kernel(top, e, start, tile, more, me, hidden, down, table, *refs):
    arrived, outs = refs[:more], refs[more:]
    entries = full(table[...])
    lane = lax.broadcasted_iota(jnp.int32, entries.shape, 1)
    expert = (me[0] * down.shape[0] + e).astype(jnp.float32)
    chosen = jnp.where((entries == expert) & (lane < top), 1.0, 0.0)
    chosen = pltpu.roll(chosen, top, 1) + pltpu.roll(chosen, 2 * top, 1)
    scale = jnp.sum(chosen * entries, axis=1, keepdims=True)
    size, columns = outs[0].shape
    for j in range(0, columns, tile):
        cut = slice(j, j + tile)
        value = dot(hidden[...], down[e, :, start + j : start + j + tile]) * scale
        if more:
            value += full(arrived[0][:, cut])
        for p, out in enumerate(outs):
            out[:, cut] = value[p * size : (p + 1) * size].astype(out.dtype)


def run_down(hidden, down, e, c, table, me, top, arrived=None, pairs=None):
    rows, units = hidden.shape
    columns = down.shape[2] // CHUNKS
    tile = max(t for t in range(128, 513, 128) if columns % t == 0)
    outs = [((rows, columns), jnp.bfloat16)]
    if pairs is not None:
        outs = [
            ((rows // pairs, columns), jnp.bfloat16 if p else jnp.float32) for p in range(pairs)
        ]
    more = [] if arrived is None else [arrived]
    result = call(
        functools.partial(down_kernel, top, e, c * columns, tile, len(more)),
        [me.reshape(1), hidden, down, table, *more],
        [SMEM_SPEC] + [VMEM_SPEC] * (3 + len(more)),
        outs,
        [],
        8,
        (2 * rows * units * columns, 2 * units * columns),
    )
    return result if pairs is not None else result[0]


def shared_kernel(x, gate, up, down, *outs):
    hidden = half(silu(dot(x[...], gate[...])) * dot(x[...], up[...]))
    columns = outs[0].shape[1]
    for c, out in enumerate(outs):
        out[...] = dot(hidden, down[:, c * columns : (c + 1) * columns])


def run_shared(x, gate, up, down):
    rows, width = x.shape
    return call(
        shared_kernel,
        [x, gate, up, down],
        [VMEM_SPEC] * 4,
        [((rows, width // CHUNKS), jnp.float32)] * CHUNKS,
        [],
        8,
        (6 * rows * gate.size, 6 * gate.size),
    )


def sum_kernel(step, place, *refs):
    parts, (kept, sent) = refs[:-2], refs[-2:]
    total = sum(full(part[...]) for part in parts)
    rows, width = total.shape
    total = total.reshape(rows // step // 2, 2, step, width)
    low, high = total[:, 0].reshape(-1, width), total[:, 1].reshape(-1, width)
    kept[...] = jnp.where(place[0] == 0, low, high)
    sent[...] = half(jnp.where(place[0] == 0, high, low))


def run_sum(parts, place, step):
    rows, width = parts[0].shape
    return call(
        functools.partial(sum_kernel, step),
        [place.reshape(1), *parts],
        [SMEM_SPEC] + [VMEM_SPEC] * len(parts),
        [((rows // 2, width), jnp.float32), ((rows // 2, width), jnp.bfloat16)],
        [],
        6,
        (rows * width * len(parts), 2 * rows * width),
    )


def encode_kernel(*refs):
    parts, (encoder, bias, out) = refs[:-3], refs[-3:]
    columns = parts[0].shape[1]
    total = bias[...]
    for c, part in enumerate(parts):
        total = total + dot(part[...], encoder[c * columns : (c + 1) * columns, :])
    out[...] = half(jnp.maximum(total, 0.0))


def run_encode(parts, encoder, bias):
    rows = parts[0].shape[0]
    return call(
        encode_kernel,
        [*parts, encoder, bias[None, :]],
        [VMEM_SPEC] * (len(parts) + 2),
        [((rows, encoder.shape[1]), jnp.bfloat16)],
        [],
        8,
        (2 * rows * encoder.size, 2 * encoder.size),
    )[0]


def decode_kernel(c, more, features, decoder, *refs):
    arrived, outs = refs[:more], refs[more:]
    size, columns = outs[0].shape
    value = dot(features[...], decoder[:, c * columns : (c + 1) * columns])
    if more:
        value += full(arrived[0][...])
    for p, out in enumerate(outs):
        out[...] = value[p * size : (p + 1) * size].astype(out.dtype)


def run_decode(features, decoder, c, arrived=None, pairs=None):
    rows, columns = features.shape[0], decoder.shape[1] // CHUNKS
    outs = [((rows, columns), jnp.bfloat16)]
    if pairs is not None:
        outs = [
            ((rows // pairs, columns), jnp.bfloat16 if p else jnp.float32) for p in range(pairs)
        ]
    more = [] if arrived is None else [arrived]
    result = call(
        functools.partial(decode_kernel, c, len(more)),
        [features, decoder, *more],
        [VMEM_SPEC] * (2 + len(more)),
        outs,
        [],
        8,
        (2 * rows * decoder.size // CHUNKS, 2 * decoder.size // CHUNKS),
    )
    return result if pairs is not None else result[0]


def shards(
    tokens,
    expert_ids,
    gate_weights,
    expert_gate,
    expert_up,
    expert_down,
    shared_gate,
    shared_up,
    shared_down,
    encoder,
    encoder_bias,
    decoder,
    decoder_bias,
):
    own, top = expert_ids.shape
    width = tokens.shape[1]
    feats = lax.axis_size("feat")
    pairs = lax.axis_size("expert") // 2
    devices = 2 * pairs * feats
    local_experts = range(expert_gate.shape[0])
    chunks = range(CHUNKS)
    me = lax.axis_index(("expert", "feat"))
    my_feat = lax.axis_index("feat")
    feat_bits = bits_of(feats)
    place = [(my_feat // bit) % 2 for bit in feat_bits]

    table = run_pack(my_feat, expert_ids, gate_weights, feats)
    for bit in feat_bits:
        table = table + swap(table, "feat", bit)
    for bit in bits_of(pairs):
        table = jnp.concatenate([table, swap(table, "expert", 2 * bit)], axis=0)
    table_far = swap(table, "expert", 1)

    near = [tokens] + [swap(tokens, "expert", 2 * p) for p in range(1, pairs)]
    far = [swap(piece, "expert", 1) for piece in near]
    near[0], expert_gate, expert_up, expert_down = run_load(
        [tokens, expert_gate, expert_up, expert_down], LOAD_MIB
    )
    shared_out = run_shared(far[0], shared_gate, shared_up, shared_down)

    hidden_near = [run_hidden(near, expert_gate, expert_up, e) for e in local_experts]
    hidden_far = [run_hidden(far, expert_gate, expert_up, e) for e in local_experts]

    def over_experts(hidden, rows_table, c, total, last_pairs):
        for e in local_experts:
            last = last_pairs if e == local_experts[-1] else None
            total = run_down(hidden[e], expert_down, e, c, rows_table, me, top, total, last)
        return total

    arrived = [swap(over_experts(hidden_near, table, c, None, None), "expert", 1) for c in chunks]
    blocks = [over_experts(hidden_far, table_far, c, arrived[c], pairs) for c in chunks]

    near = []
    for c in chunks:
        arrived = [swap(blocks[c][p], "expert", 2 * p) for p in range(1, pairs)]
        total, sent = run_sum([blocks[c][0], shared_out[c]] + arrived, place[0], own)
        total = total + full(swap(sent, "feat", feat_bits[0]))
        total = total.reshape((2,) * (len(feat_bits) - 1) + (own, -1))
        for i, bit in enumerate(feat_bits[1:-1]):
            dim = len(feat_bits) - 2 - i
            arrived = swap(half(take(total, 1 - place[i + 1], dim)), "feat", bit)
            total = take(total, place[i + 1], dim) + full(arrived)
        total = half(total)
        moe_out = half(full(total) + full(swap(total, "feat", feat_bits[-1])))
        for bit in feat_bits[-2::-1]:
            moe_out = jnp.stack([moe_out, swap(moe_out, "feat", bit)], axis=moe_out.ndim - 2)
        near.append(gather_pairs(moe_out).reshape(pairs * feats * own, -1))

    far = [swap(part, "expert", 1) for part in near]
    features_near = run_encode(near, encoder, encoder_bias)
    arrived = [swap(run_decode(features_near, decoder, c), "expert", 1) for c in chunks]
    features_far = run_encode(far, encoder, encoder_bias)
    blocks = [run_decode(features_far, decoder, c, arrived[c], pairs) for c in chunks]

    reconstruction = []
    for c in chunks:
        arrived = [swap(blocks[c][p], "expert", 2 * p) for p in range(1, pairs)]
        total = blocks[c][0] + sum(full(a) for a in arrived)
        total = total.reshape((2,) * len(feat_bits) + (own, -1))
        for bit in feat_bits[:-1]:
            dim = len(total.shape) - 3
            arrived = swap(half(lax.index_in_dim(total, 1, dim, False)), "feat", bit)
            total = lax.index_in_dim(total, 0, dim, False) + full(arrived)
        arrived = swap(half(take(total, 1 - place[-1], 0)), "feat", feat_bits[-1])
        reconstruction.append(take(total, place[-1], 0) + full(arrived))
    reconstruction = jnp.concatenate(reconstruction, axis=1) + decoder_bias[None, :]

    features = jnp.stack([features_far, features_near]).reshape(2, pairs, feats, own, -1)
    features = features.transpose(1, 0, 2, 3, 4).reshape(devices, own, -1)
    relative = me - me % feats + my_feat % (feats // 2)
    blocks = [lax.dynamic_index_in_dim(features, i ^ relative, 0) for i in range(devices)]
    features = jnp.concatenate(blocks, axis=0).reshape(devices * own, -1)
    return (features, reconstruction)


def solution(mesh):
    return jax.shard_map(
        shards,
        mesh=mesh,
        in_specs=(
            P("expert", None),
            P(("expert", "feat"), None),
            P(("expert", "feat"), None),
            P(("expert", "feat"), None, None),
            P(("expert", "feat"), None, None),
            P(("expert", "feat"), None, None),
            P(None, "feat"),
            P(None, "feat"),
            P("feat", None),
            P(None, ("expert", "feat")),
            P(("expert", "feat")),
            P(("expert", "feat"), None),
            P(),
        ),
        out_specs=(P(None, ("expert", "feat")), P(("expert", "feat"), None)),
        check_vma=False,
    )
```

```python
import functools

import jax
import jax.numpy as jnp
from jax import lax
from jax.experimental import pallas as pl
from jax.experimental.pallas import tpu as pltpu
from jax.sharding import PartitionSpec as P

LANES = 128
MIB = 1024 * 1024
LOAD_MIB = 34
VMEM_SPEC = pl.BlockSpec(memory_space=pltpu.VMEM)
SMEM_SPEC = pl.BlockSpec(memory_space=pltpu.SMEM)
HBM_SPEC = pl.BlockSpec(memory_space=pltpu.HBM)


def swap(value, axis, r):
    return lax.ppermute(value, axis, [(i, i ^ r) for i in range(lax.axis_size(axis))])


def dot(a, b):
    return jnp.dot(a, b, preferred_element_type=jnp.float32)


def half(value):
    return value.astype(jnp.bfloat16)


def full(value):
    return value.astype(jnp.float32)


def silu(value):
    return value / (1.0 + jnp.exp(-value))


def bits_of(count):
    assert count & (count - 1) == 0
    return [1 << b for b in range(count.bit_length() - 1)]


def take(value, index, dim):
    return lax.dynamic_index_in_dim(value, index, dim, keepdims=False)


def call(body, operands, specs, outs, scratch, mib, cost):
    flops, moved = cost
    return pl.pallas_call(
        body,
        in_specs=specs,
        out_specs=[VMEM_SPEC] * len(outs),
        out_shape=[jax.ShapeDtypeStruct(shape, dtype) for shape, dtype in outs],
        scratch_shapes=scratch,
        compiler_params=pltpu.CompilerParams(vmem_limit_bytes=mib * MIB),
        cost_estimate=pl.CostEstimate(flops=flops, bytes_accessed=moved, transcendentals=0),
    )(*operands)


def start_all(pairs, sems):
    copies = [pltpu.make_async_copy(a, b, sems.at[i]) for i, (a, b) in enumerate(pairs)]
    for copy in copies:
        copy.start()
    return copies


def pack_kernel(feats, feat, ids, weights, out):
    top, own = ids.shape
    lane = lax.broadcasted_iota(jnp.int32, (top, LANES), 1)
    row = lax.broadcasted_iota(jnp.int32, (top, LANES), 0)
    high = half(weights[...])
    low = half(weights[...] - full(high))
    values = jnp.zeros((own, LANES), jnp.float32)
    for i, part in enumerate([half(full(ids[...])), high, low]):
        places = half(jnp.where(lane == row + i * top, 1.0, 0.0))
        values += lax.dot_general(
            part, places, (((0,), (0,)), ((), ())), preferred_element_type=jnp.float32
        )
    for f in range(feats):
        out[f * own : (f + 1) * own, :] = half(jnp.where(feat[0] == f, values, 0.0))


def run_pack(feat, expert_ids, gate_weights, feats):
    own, top = expert_ids.shape
    return call(
        functools.partial(pack_kernel, feats),
        [feat.reshape(1), expert_ids.T, gate_weights.T],
        [SMEM_SPEC, VMEM_SPEC, VMEM_SPEC],
        [((feats * own, LANES), jnp.bfloat16)],
        [],
        2,
        (6 * own * top * LANES, 2 * feats * own * LANES),
    )[0]


def load_kernel(count, x, table, *refs):
    sources, refs = refs[: count + 3], refs[count + 3 :]
    (shared_out, table_out), loaded = refs[:2], refs[2 : 2 + count]
    gate, up, down, sems = refs[2 + count :]
    copies = start_all(list(zip(sources, (gate, up, down) + loaded)), sems)
    table_out[...] = table[...]
    copies[0].wait()
    value = silu(dot(x[...], gate[...]))
    copies[1].wait()
    hidden = half(value * dot(x[...], up[...]))
    copies[2].wait()
    for j in range(0, shared_out.shape[1], 256):
        shared_out[:, j : j + 256] = dot(hidden, down[:, j : j + 256])
    for copy in copies[3:]:
        copy.wait()


def run_load(x, table, shared, values):
    count = len(values)
    outs = [((x.shape[0], shared[2].shape[1]), jnp.float32)]
    outs += [(value.shape, value.dtype) for value in [table] + values]
    return call(
        functools.partial(load_kernel, count),
        [x, table, *shared, *values],
        [VMEM_SPEC] * 2 + [HBM_SPEC] * (3 + count),
        outs,
        [pltpu.VMEM(w.shape, jnp.bfloat16) for w in shared]
        + [pltpu.SemaphoreType.DMA((3 + count,))],
        LOAD_MIB,
        (6 * x.shape[0] * shared[0].size, 4 * sum(value.size for value in values)),
    )


def hidden_kernel(count, e, tile, *refs):
    pieces, (gate, up, out, rows) = refs[:count], refs[count:]
    size = pieces[0].shape[0]
    for i in range(count):
        rows[i * size : (i + 1) * size, :] = pieces[i][...]
    for j in range(0, out.shape[1], tile):
        cut = slice(j, j + tile)
        value = silu(dot(rows[...], gate[e, :, cut]))
        out[:, cut] = half(value * dot(rows[...], up[e, :, cut]))


def run_hidden(pieces, gate, up, e):
    count, (size, width) = len(pieces), pieces[0].shape
    units = gate.shape[2]
    return call(
        functools.partial(hidden_kernel, count, e, min(256, units)),
        [*pieces, gate, up],
        [VMEM_SPEC] * (count + 2),
        [((count * size, units), jnp.bfloat16)],
        [pltpu.VMEM((count * size, width), jnp.bfloat16)],
        8,
        (4 * count * size * width * units, 4 * width * units),
    )[0]


def down_kernel(top, e, tile, kind, scalars, hidden, down, table, *refs):
    count = 1 if kind is None else 2 * kind[0]
    more, outs = refs[:-count], refs[-count:]
    entries = full(table[...])
    lane = lax.broadcasted_iota(jnp.int32, entries.shape, 1)
    expert = (scalars[0] * down.shape[0] + e).astype(jnp.float32)
    chosen = jnp.where((entries == expert) & (lane < top), 1.0, 0.0)
    chosen = pltpu.roll(chosen, top, 1) + pltpu.roll(chosen, 2 * top, 1)
    scale = jnp.sum(chosen * entries, axis=1, keepdims=True)
    for j in range(0, down.shape[2], tile):
        cut = slice(j, j + tile)
        value = dot(hidden[...], down[e, :, cut]) * scale
        if more:
            value += full(more[0][:, cut])
        if kind is None:
            outs[0][:, cut] = half(value)
            continue
        pairs, own = kind
        size = value.shape[0] // pairs
        for p in range(pairs):
            block = value[p * size : (p + 1) * size]
            if p == 0:
                block += more[1][:, cut]
            block = block.reshape(size // own // 2, 2, own, tile)
            low, high = block[:, 0].reshape(-1, tile), block[:, 1].reshape(-1, tile)
            outs[p][:, cut] = half(jnp.where(scalars[1] == 0, low, high))
            outs[pairs + p][:, cut] = half(jnp.where(scalars[1] == 0, high, low))


def run_down(hidden, down, e, scalars, table, top, more=(), kind=None):
    rows, units = hidden.shape
    width = down.shape[2]
    tile = 256 if width % 256 == 0 else 128
    outs = [((rows, width), jnp.bfloat16)]
    if kind is not None:
        outs = [((rows // kind[0] // 2, width), jnp.bfloat16)] * (2 * kind[0])
    return call(
        functools.partial(down_kernel, top, e, tile, kind),
        [scalars, hidden, down, table, *more],
        [SMEM_SPEC] + [VMEM_SPEC] * (3 + len(more)),
        outs,
        [],
        8,
        (2 * rows * units * width, 2 * units * width),
    )


def shards(
    tokens,
    expert_ids,
    gate_weights,
    expert_gate,
    expert_up,
    expert_down,
    shared_gate,
    shared_up,
    shared_down,
    encoder,
    encoder_bias,
    decoder,
    decoder_bias,
):
    own, top = expert_ids.shape
    width = tokens.shape[1]
    feats = lax.axis_size("feat")
    pairs = lax.axis_size("expert") // 2
    devices = 2 * pairs * feats
    local_experts = range(expert_gate.shape[0])
    me = lax.axis_index(("expert", "feat"))
    my_feat = lax.axis_index("feat")
    feat_bits = bits_of(feats)
    place = [(my_feat // bit) % 2 for bit in feat_bits]
    scalars = jnp.stack([me, place[0]])
    chunk_rows = pairs * feats // 2 * own

    table = run_pack(my_feat, expert_ids, gate_weights, feats)
    for bit in feat_bits:
        table = table + swap(table, "feat", bit)

    near = [tokens] + [swap(tokens, "expert", 2 * p) for p in range(1, pairs)]
    far = [swap(piece, "expert", 1) for piece in near]
    arrived = swap(table, "expert", 2)
    shared_out, table, near[0], expert_gate, expert_up, expert_down = run_load(
        far[0],
        table,
        [shared_gate, shared_up, shared_down],
        [tokens, expert_gate, expert_up, expert_down],
    )
    table = jnp.concatenate([table, arrived], axis=0)
    for bit in bits_of(pairs)[1:]:
        table = jnp.concatenate([table, swap(table, "expert", 2 * bit)], axis=0)
    table_far = swap(table, "expert", 1)

    arrived = None
    for e in local_experts:
        hidden = run_hidden(near, expert_gate, expert_up, e)
        more = [] if arrived is None else [arrived]
        arrived = run_down(hidden, expert_down, e, scalars, table, top, more)[0]
    arrived = swap(arrived, "expert", 1)
    for e in local_experts:
        hidden = run_hidden(far, expert_gate, expert_up, e)
        if e < local_experts[-1]:
            more = [arrived]
            arrived = run_down(hidden, expert_down, e, scalars, table_far, top, more)[0]
    blocks = run_down(
        hidden, expert_down, e, scalars, table_far, top, [arrived, shared_out], (pairs, own)
    )

    def reduce_pairs(parts):
        arrived = [swap(parts[p], "expert", 2 * p) for p in range(1, pairs)]
        return sum(full(part) for part in [parts[0]] + arrived)

    def gather_pairs(value):
        parts = [value] + [swap(value, "expert", 2 * p) for p in range(1, pairs)]
        return jnp.stack(parts).reshape(chunk_rows, width)

    arrived = swap(half(reduce_pairs(blocks[:pairs])), "feat", feat_bits[0])
    total = reduce_pairs(blocks[pairs:]) + full(arrived)
    total = total.reshape((2,) * (len(feat_bits) - 1) + (own, width))
    for i, bit in enumerate(feat_bits[1:-1]):
        dim = len(feat_bits) - 2 - i
        arrived = swap(half(take(total, 1 - place[i + 1], dim)), "feat", bit)
        total = take(total, place[i + 1], dim) + full(arrived)
    total = half(total)
    moe_out = half(full(total) + full(swap(total, "feat", feat_bits[-1])))
    for bit in feat_bits[-2:0:-1]:
        moe_out = jnp.stack([moe_out, swap(moe_out, "feat", bit)], axis=moe_out.ndim - 2)
    moe_out = moe_out.reshape(-1, width)
    near = [None, gather_pairs(moe_out)]
    near[0] = gather_pairs(swap(moe_out, "feat", feat_bits[0]))

    def encode(x):
        return half(jax.nn.relu(dot(x, encoder) + encoder_bias[None, :]))

    features = [None, None]
    arrived = None
    for chunk in (1, 0):
        far = swap(near[chunk], "expert", 1)
        features_near = encode(near[chunk])
        decoded = swap(half(dot(features_near, decoder)), "expert", 1)
        features_far = encode(far)
        total = dot(features_far, decoder) + full(decoded)
        total = total.reshape(pairs, feats // 2 * own, width)
        total = reduce_pairs([total[0]] + [half(total[p]) for p in range(1, pairs)])
        both = jnp.stack([features_far, features_near])
        features[chunk] = both.reshape(2, pairs, feats // 2, 1, own, -1)
        if chunk == 1:
            arrived = swap(half(total), "feat", feat_bits[0])
    total = (total + full(arrived)).reshape((2,) * (len(feat_bits) - 1) + (own, width))
    for bit in feat_bits[1:-1]:
        dim = len(total.shape) - 3
        arrived = swap(half(lax.index_in_dim(total, 1, dim, False)), "feat", bit)
        total = lax.index_in_dim(total, 0, dim, False) + full(arrived)
    arrived = swap(half(take(total, 1 - place[-1], 0)), "feat", feat_bits[-1])
    reconstruction = take(total, place[-1], 0) + full(arrived) + decoder_bias[None, :]

    features = jnp.concatenate(features, axis=3).transpose(1, 0, 2, 3, 4, 5)
    features = features.reshape(devices, own, -1)
    relative = me - me % feats + my_feat % (feats // 2)
    blocks = [lax.dynamic_index_in_dim(features, i ^ relative, 0) for i in range(devices)]
    features = jnp.concatenate(blocks, axis=0).reshape(devices * own, -1)
    return (features, reconstruction)


def solution(mesh):
    return jax.shard_map(
        shards,
        mesh=mesh,
        in_specs=(
            P("expert", None),
            P(("expert", "feat"), None),
            P(("expert", "feat"), None),
            P(("expert", "feat"), None, None),
            P(("expert", "feat"), None, None),
            P(("expert", "feat"), None, None),
            P(None, "feat"),
            P(None, "feat"),
            P("feat", None),
            P(None, ("expert", "feat")),
            P(("expert", "feat")),
            P(("expert", "feat"), None),
            P(),
        ),
        out_specs=(P(None, ("expert", "feat")), P(("expert", "feat"), None)),
        check_vma=False,
    )
```

```python
import functools

import jax
import jax.numpy as jnp
from jax import lax
from jax.experimental import pallas as pl
from jax.experimental.pallas import tpu as pltpu
from jax.sharding import PartitionSpec as P

LANES = 128
MIB = 1024 * 1024
LOAD_MIB = 40
VMEM_SPEC = pl.BlockSpec(memory_space=pltpu.VMEM)
SMEM_SPEC = pl.BlockSpec(memory_space=pltpu.SMEM)
HBM_SPEC = pl.BlockSpec(memory_space=pltpu.HBM)


def swap(value, axis, r):
    return lax.ppermute(value, axis, [(i, i ^ r) for i in range(lax.axis_size(axis))])


def dot(a, b):
    return jnp.dot(a, b, preferred_element_type=jnp.float32)


def half(value):
    return value.astype(jnp.bfloat16)


def full(value):
    return value.astype(jnp.float32)


def silu(value):
    return value / (1.0 + jnp.exp(-value))


def bits_of(count):
    assert count & (count - 1) == 0
    return [1 << b for b in range(count.bit_length() - 1)]


def take(value, index, dim):
    return lax.dynamic_index_in_dim(value, index, dim, keepdims=False)


def call(body, operands, specs, outs, scratch, mib, cost):
    flops, moved = cost
    return pl.pallas_call(
        body,
        in_specs=specs,
        out_specs=[VMEM_SPEC] * len(outs),
        out_shape=[jax.ShapeDtypeStruct(shape, dtype) for shape, dtype in outs],
        scratch_shapes=scratch,
        compiler_params=pltpu.CompilerParams(vmem_limit_bytes=mib * MIB),
        cost_estimate=pl.CostEstimate(flops=flops, bytes_accessed=moved, transcendentals=0),
    )(*operands)


def start_all(pairs, sems):
    copies = [pltpu.make_async_copy(a, b, sems.at[i]) for i, (a, b) in enumerate(pairs)]
    for copy in copies:
        copy.start()
    return copies


def pack_kernel(feats, feat, ids, weights, out):
    top, own = ids.shape
    lane = lax.broadcasted_iota(jnp.int32, (top, LANES), 1)
    row = lax.broadcasted_iota(jnp.int32, (top, LANES), 0)
    high = half(weights[...])
    low = half(weights[...] - full(high))
    values = jnp.zeros((own, LANES), jnp.float32)
    for i, part in enumerate([half(full(ids[...])), high, low]):
        places = half(jnp.where(lane == row + i * top, 1.0, 0.0))
        values += lax.dot_general(
            part, places, (((0,), (0,)), ((), ())), preferred_element_type=jnp.float32
        )
    for f in range(feats):
        out[f * own : (f + 1) * own, :] = half(jnp.where(feat[0] == f, values, 0.0))


def run_pack(feat, expert_ids, gate_weights, feats):
    own, top = expert_ids.shape
    return call(
        functools.partial(pack_kernel, feats),
        [feat.reshape(1), expert_ids.T, gate_weights.T],
        [SMEM_SPEC, VMEM_SPEC, VMEM_SPEC],
        [((feats * own, LANES), jnp.bfloat16)],
        [],
        2,
        (6 * own * top * LANES, 2 * feats * own * LANES),
    )[0]


def load_kernel(table, *refs):
    count = (len(refs) - 2) // 2
    copies = start_all(list(zip(refs[:count], refs[count + 1 : -1])), refs[-1])
    refs[count][...] = table[...]
    for copy in copies:
        copy.wait()


def run_load(table, values):
    count = len(values)
    return call(
        load_kernel,
        [table, *values],
        [VMEM_SPEC] + [HBM_SPEC] * count,
        [(value.shape, value.dtype) for value in [table] + values],
        [pltpu.SemaphoreType.DMA((count,))],
        LOAD_MIB,
        (550 * sum(value.size for value in values), 4 * sum(value.size for value in values)),
    )


def shared_kernel(own, scalars, x, gate, up, down, kept, sent):
    hidden = half(silu(dot(x[...], gate[...])) * dot(x[...], up[...]))
    rows, width = x.shape
    for j in range(0, width, 256):
        cut = slice(j, j + 256)
        value = dot(hidden, down[:, cut]).reshape(rows // own // 2, 2, own, -1)
        low, high = [value[:, i].reshape(rows // 2, -1) for i in range(2)]
        kept[:, cut] = jnp.where(scalars[1] == 0, low, high)
        sent[:, cut] = jnp.where(scalars[1] == 0, high, low)


def run_shared(scalars, x, weights, own):
    rows, width = x.shape
    return call(
        functools.partial(shared_kernel, own),
        [scalars, x, *weights],
        [SMEM_SPEC] + [VMEM_SPEC] * 4,
        [((rows // 2, width), jnp.float32)] * 2,
        [],
        6,
        (6 * rows * weights[0].size, 6 * weights[0].size),
    )


def hidden_kernel(count, e, tile, *refs):
    pieces, (gate, up, out, rows) = refs[:count], refs[count:]
    size = pieces[0].shape[0]
    for i in range(count):
        rows[i * size : (i + 1) * size, :] = pieces[i][...]
    for j in range(0, out.shape[1], tile):
        cut = slice(j, j + tile)
        value = silu(dot(rows[...], gate[e, :, cut]))
        out[:, cut] = half(value * dot(rows[...], up[e, :, cut]))


def run_hidden(pieces, gate, up, e):
    count, (size, width) = len(pieces), pieces[0].shape
    units = gate.shape[2]
    return call(
        functools.partial(hidden_kernel, count, e, min(256, units)),
        [*pieces, gate, up],
        [VMEM_SPEC] * (count + 2),
        [((count * size, units), jnp.bfloat16)],
        [pltpu.VMEM((count * size, width), jnp.bfloat16)],
        8,
        (4 * count * size * width * units, 4 * width * units),
    )[0]


def down_kernel(top, e, tile, kind, scalars, hidden, down, table, *refs):
    count = 1 if kind is None else 2 * kind[0]
    more, outs = refs[:-count], refs[-count:]
    entries = full(table[...])
    lane = lax.broadcasted_iota(jnp.int32, entries.shape, 1)
    expert = (scalars[0] * down.shape[0] + e).astype(jnp.float32)
    chosen = jnp.where((entries == expert) & (lane < top), 1.0, 0.0)
    chosen = pltpu.roll(chosen, top, 1) + pltpu.roll(chosen, 2 * top, 1)
    scale = jnp.sum(chosen * entries, axis=1, keepdims=True)
    for j in range(0, down.shape[2], tile):
        cut = slice(j, j + tile)
        value = dot(hidden[...], down[e, :, cut]) * scale
        if more:
            value += full(more[0][:, cut])
        if kind is None:
            outs[0][:, cut] = half(value)
            continue
        pairs, own = kind
        size = value.shape[0] // pairs
        for p in range(pairs):
            block = value[p * size : (p + 1) * size]
            block = block.reshape(size // own // 2, 2, own, tile)
            low, high = block[:, 0].reshape(-1, tile), block[:, 1].reshape(-1, tile)
            outs[p][:, cut] = half(jnp.where(scalars[1] == 0, low, high))
            outs[pairs + p][:, cut] = half(jnp.where(scalars[1] == 0, high, low))


def run_down(hidden, down, e, scalars, table, top, more=(), kind=None):
    rows, units = hidden.shape
    width = down.shape[2]
    tile = 256 if width % 256 == 0 else 128
    outs = [((rows, width), jnp.bfloat16)]
    if kind is not None:
        outs = [((rows // kind[0] // 2, width), jnp.bfloat16)] * (2 * kind[0])
    return call(
        functools.partial(down_kernel, top, e, tile, kind),
        [scalars, hidden, down, table, *more],
        [SMEM_SPEC] + [VMEM_SPEC] * (3 + len(more)),
        outs,
        [],
        8,
        (2 * rows * units * width, 2 * units * width),
    )


def shards(
    tokens,
    expert_ids,
    gate_weights,
    expert_gate,
    expert_up,
    expert_down,
    shared_gate,
    shared_up,
    shared_down,
    encoder,
    encoder_bias,
    decoder,
    decoder_bias,
):
    own, top = expert_ids.shape
    width = tokens.shape[1]
    feats = lax.axis_size("feat")
    pairs = lax.axis_size("expert") // 2
    devices = 2 * pairs * feats
    local_experts = range(expert_gate.shape[0])
    me = lax.axis_index(("expert", "feat"))
    my_feat = lax.axis_index("feat")
    feat_bits = bits_of(feats)
    place = [(my_feat // bit) % 2 for bit in feat_bits]
    scalars = jnp.stack([me, place[0]])
    chunk_rows = pairs * feats // 2 * own

    table = run_pack(my_feat, expert_ids, gate_weights, feats)
    for bit in feat_bits:
        table = table + swap(table, "feat", bit)

    near = [tokens] + [swap(tokens, "expert", 2 * p) for p in range(1, pairs)]
    far = [swap(piece, "expert", 1) for piece in near]
    arrived = swap(table, "expert", 2)
    table, near[0], expert_gate, expert_up = run_load(
        table, [tokens, expert_gate, expert_up]
    )
    shared_out = run_shared(scalars, far[0], [shared_gate, shared_up, shared_down], own)
    table = jnp.concatenate([table, arrived], axis=0)
    for bit in bits_of(pairs)[1:]:
        table = jnp.concatenate([table, swap(table, "expert", 2 * bit)], axis=0)
    table_far = swap(table, "expert", 1)

    table, *far = lax.optimization_barrier((table, *far))
    arrived = None
    for e in local_experts:
        hidden = run_hidden(near, expert_gate, expert_up, e)
        more = [] if arrived is None else [arrived]
        arrived = run_down(hidden, expert_down, e, scalars, table, top, more)[0]
    arrived = swap(arrived, "expert", 1)
    for e in local_experts:
        hidden = run_hidden(far, expert_gate, expert_up, e)
        if e < local_experts[-1]:
            more = [arrived]
            arrived = run_down(hidden, expert_down, e, scalars, table_far, top, more)[0]
    blocks = run_down(
        hidden, expert_down, e, scalars, table_far, top, [arrived], (pairs, own)
    )

    def reduce_pairs(parts, *more):
        arrived = [swap(parts[p], "expert", 2 * p) for p in range(1, pairs)]
        return sum(full(part) for part in [parts[0], *more] + arrived)

    arrived = swap(half(reduce_pairs(blocks[:pairs], shared_out[0])), "feat", feat_bits[0])
    total = reduce_pairs(blocks[pairs:], shared_out[1]) + full(arrived)
    total = total.reshape((2,) * (len(feat_bits) - 1) + (own, width))
    for i, bit in enumerate(feat_bits[1:-1]):
        dim = len(feat_bits) - 2 - i
        arrived = swap(half(take(total, 1 - place[i + 1], dim)), "feat", bit)
        total = take(total, place[i + 1], dim) + full(arrived)
    total = half(total)
    moe_out = half(full(total) + full(swap(total, "feat", feat_bits[-1])))
    for bit in feat_bits[-2:0:-1]:
        moe_out = jnp.stack([moe_out, swap(moe_out, "feat", bit)], axis=moe_out.ndim - 2)
    moe_out = moe_out.reshape(-1, width)
    other = swap(moe_out, "feat", feat_bits[0])
    parts = [moe_out] + [swap(moe_out, "expert", 2 * p) for p in range(1, pairs - 1)]
    mine, other = lax.optimization_barrier((moe_out, other))
    parts.append(swap(mine, "expert", 2 * (pairs - 1)))
    sides = [[other] + [swap(other, "expert", 2 * p) for p in range(1, pairs)], parts]
    near = [jnp.stack(parts).reshape(chunk_rows, width) for parts in sides]

    def encode(x):
        return half(jax.nn.relu(dot(x, encoder) + encoder_bias[None, :]))

    features, blocks = [None, None], [None, None]
    for chunk in (1, 0):
        far = swap(near[chunk], "expert", 1)
        features_near = encode(near[chunk])
        decoded = swap(half(dot(features_near, decoder)), "expert", 1)
        features_far = encode(far)
        total = dot(features_far, decoder) + full(decoded)
        total = total.reshape(pairs, feats // 2 * own, width)
        blocks[chunk] = [total[0]]
        blocks[chunk] += [swap(half(total[p]), "expert", 2 * p) for p in range(1, pairs)]
        both = jnp.stack([features_far, features_near])
        features[chunk] = both.reshape(2, pairs, feats // 2, 1, own, -1)
    arrived = swap(half(sum(full(block) for block in blocks[1])), "feat", feat_bits[0])
    total = sum(full(block) for block in blocks[0])
    total = (total + full(arrived)).reshape((2,) * (len(feat_bits) - 1) + (own, width))
    for bit in feat_bits[1:-1]:
        dim = len(total.shape) - 3
        arrived = swap(half(lax.index_in_dim(total, 1, dim, False)), "feat", bit)
        total = lax.index_in_dim(total, 0, dim, False) + full(arrived)
    arrived = swap(half(take(total, 1 - place[-1], 0)), "feat", feat_bits[-1])
    reconstruction = take(total, place[-1], 0) + full(arrived) + decoder_bias[None, :]

    features = jnp.concatenate(features, axis=3).transpose(1, 0, 2, 3, 4, 5)
    features = features.reshape(devices, own, -1)
    relative = me - me % feats + my_feat % (feats // 2)
    blocks = [lax.dynamic_index_in_dim(features, i ^ relative, 0) for i in range(devices)]
    features = jnp.concatenate(blocks, axis=0).reshape(devices * own, -1)
    return (features, reconstruction)


def solution(mesh):
    return jax.shard_map(
        shards,
        mesh=mesh,
        in_specs=(
            P("expert", None),
            P(("expert", "feat"), None),
            P(("expert", "feat"), None),
            P(("expert", "feat"), None, None),
            P(("expert", "feat"), None, None),
            P(("expert", "feat"), None, None),
            P(None, "feat"),
            P(None, "feat"),
            P("feat", None),
            P(None, ("expert", "feat")),
            P(("expert", "feat")),
            P(("expert", "feat"), None),
            P(),
        ),
        out_specs=(P(None, ("expert", "feat")), P(("expert", "feat"), None)),
        check_vma=False,
    )
```

```python
import functools

import jax
import jax.numpy as jnp
from jax import lax
from jax.experimental import pallas as pl
from jax.experimental.pallas import tpu as pltpu
from jax.sharding import PartitionSpec as P

LANES = 128
MIB = 1024 * 1024
STREAM_MIB = 40
VMEM_SPEC = pl.BlockSpec(memory_space=pltpu.VMEM)
SMEM_SPEC = pl.BlockSpec(memory_space=pltpu.SMEM)
HBM_SPEC = pl.BlockSpec(memory_space=pltpu.HBM)


def swap(value, axis, r):
    return lax.ppermute(value, axis, [(i, i ^ r) for i in range(lax.axis_size(axis))])


def dot(a, b):
    return jnp.dot(a, b, preferred_element_type=jnp.float32)


def half(value):
    return value.astype(jnp.bfloat16)


def full(value):
    return value.astype(jnp.float32)


def silu(value):
    return value / (1.0 + jnp.exp(-value))


def bits_of(count):
    assert count & (count - 1) == 0
    return [1 << b for b in range(count.bit_length() - 1)]


def take(value, index, dim):
    return lax.dynamic_index_in_dim(value, index, dim, keepdims=False)


def call(body, operands, specs, outs, scratch, mib, cost):
    flops, moved = cost
    return pl.pallas_call(
        body,
        in_specs=specs,
        out_specs=[VMEM_SPEC] * len(outs),
        out_shape=[jax.ShapeDtypeStruct(shape, dtype) for shape, dtype in outs],
        scratch_shapes=scratch,
        compiler_params=pltpu.CompilerParams(vmem_limit_bytes=mib * MIB),
        cost_estimate=pl.CostEstimate(flops=flops, bytes_accessed=moved, transcendentals=0),
    )(*operands)


def start_all(pairs, sems):
    copies = [pltpu.make_async_copy(a, b, sems.at[i]) for i, (a, b) in enumerate(pairs)]
    for copy in copies:
        copy.start()
    return copies


def pack_kernel(feats, feat, ids, weights, out):
    top, own = ids.shape
    lane = lax.broadcasted_iota(jnp.int32, (top, LANES), 1)
    row = lax.broadcasted_iota(jnp.int32, (top, LANES), 0)
    high = half(weights[...])
    low = half(weights[...] - full(high))
    values = jnp.zeros((own, LANES), jnp.float32)
    for i, part in enumerate([half(full(ids[...])), high, low]):
        places = half(jnp.where(lane == row + i * top, 1.0, 0.0))
        values += lax.dot_general(
            part, places, (((0,), (0,)), ((), ())), preferred_element_type=jnp.float32
        )
    for f in range(feats):
        out[f * own : (f + 1) * own, :] = half(jnp.where(feat[0] == f, values, 0.0))


def run_pack(feat, expert_ids, gate_weights, feats):
    own, top = expert_ids.shape
    return call(
        functools.partial(pack_kernel, feats),
        [feat.reshape(1), expert_ids.T, gate_weights.T],
        [SMEM_SPEC, VMEM_SPEC, VMEM_SPEC],
        [((feats * own, LANES), jnp.bfloat16)],
        [],
        2,
        (6 * own * top * LANES, 2 * feats * own * LANES),
    )[0]


def load_kernel(table, tokens, table_out, tokens_out):
    table_out[...] = table[...]
    tokens_out[...] = tokens[...]


def run_load(table, tokens):
    return call(
        load_kernel,
        [table, tokens],
        [VMEM_SPEC] * 2,
        [(value.shape, value.dtype) for value in (table, tokens)],
        [],
        2,
        (0, 4 * tokens.size),
    )


def shared_kernel(own, scalars, x, gate, up, down, kept, sent):
    hidden = half(silu(dot(x[...], gate[...])) * dot(x[...], up[...]))
    rows, width = x.shape
    for j in range(0, width, 256):
        cut = slice(j, j + 256)
        value = dot(hidden, down[:, cut]).reshape(rows // own // 2, 2, own, -1)
        low, high = [value[:, i].reshape(rows // 2, -1) for i in range(2)]
        kept[:, cut] = jnp.where(scalars[1] == 0, low, high)
        sent[:, cut] = jnp.where(scalars[1] == 0, high, low)


def run_shared(scalars, x, weights, own):
    rows, width = x.shape
    return call(
        functools.partial(shared_kernel, own),
        [scalars, x, *weights],
        [SMEM_SPEC] + [VMEM_SPEC] * 4,
        [((rows // 2, width), jnp.float32)] * 2,
        [],
        6,
        (6 * rows * weights[0].size, 6 * weights[0].size),
    )


def hidden_kernel(count, e, tile, stream, *refs):
    pieces, (gate, up, out), refs = refs[:count], refs[count : count + 3], refs[count + 3 :]
    size, units = pieces[0].shape[0], out.shape[1]
    cuts = [slice(j, j + tile) for j in range(0, units, tile)]
    if stream:
        gate_held, up_held, rows, sems = refs
        pairs = []
        for cut in cuts:
            pairs.append((gate.at[e, :, cut], gate_held.at[0, :, cut]))
            pairs.append((up.at[e, :, cut], up_held.at[0, :, cut]))
        copies = start_all(pairs, sems)
    else:
        gate_held, up_held, rows = gate, up, refs[0]
    for i in range(count):
        rows[i * size : (i + 1) * size, :] = pieces[i][...]
    for i, cut in enumerate(cuts):
        if stream:
            copies[2 * i].wait()
        value = silu(dot(rows[...], gate_held[0, :, cut]))
        if stream:
            copies[2 * i + 1].wait()
        out[:, cut] = half(value * dot(rows[...], up_held[0, :, cut]))


def run_hidden(pieces, gate, up, e, stream):
    count, (size, width) = len(pieces), pieces[0].shape
    units = gate.shape[2]
    tile = min(256, units)
    outs = [((count * size, units), jnp.bfloat16)]
    scratch = [pltpu.VMEM((count * size, width), jnp.bfloat16)]
    if stream:
        outs += [((1, width, units), jnp.bfloat16)] * 2
        scratch.append(pltpu.SemaphoreType.DMA((2 * (units // tile),)))
    return call(
        functools.partial(hidden_kernel, count, e, tile, stream),
        [*pieces, gate, up],
        [VMEM_SPEC] * count + [HBM_SPEC if stream else VMEM_SPEC] * 2,
        outs,
        scratch,
        STREAM_MIB if stream else 8,
        (4 * count * size * width * units, 4 * width * units),
    )


def down_kernel(top, e, tile, kind, scalars, hidden, down, table, *refs):
    count = 1 if kind is None else 2 * kind[0]
    more, outs = refs[:-count], refs[-count:]
    entries = full(table[...])
    lane = lax.broadcasted_iota(jnp.int32, entries.shape, 1)
    expert = (scalars[0] * down.shape[0] + e).astype(jnp.float32)
    chosen = jnp.where((entries == expert) & (lane < top), 1.0, 0.0)
    chosen = pltpu.roll(chosen, top, 1) + pltpu.roll(chosen, 2 * top, 1)
    scale = jnp.sum(chosen * entries, axis=1, keepdims=True)
    for j in range(0, down.shape[2], tile):
        cut = slice(j, j + tile)
        value = dot(hidden[...], down[e, :, cut]) * scale
        if more:
            value += full(more[0][:, cut])
        if kind is None:
            outs[0][:, cut] = half(value)
            continue
        pairs, own = kind
        size = value.shape[0] // pairs
        for p in range(pairs):
            block = value[p * size : (p + 1) * size]
            block = block.reshape(size // own // 2, 2, own, tile)
            low, high = block[:, 0].reshape(-1, tile), block[:, 1].reshape(-1, tile)
            outs[p][:, cut] = half(jnp.where(scalars[1] == 0, low, high))
            outs[pairs + p][:, cut] = half(jnp.where(scalars[1] == 0, high, low))


def run_down(hidden, down, e, scalars, table, top, more=(), kind=None):
    rows, units = hidden.shape
    width = down.shape[2]
    tile = 256 if width % 256 == 0 else 128
    outs = [((rows, width), jnp.bfloat16)]
    if kind is not None:
        outs = [((rows // kind[0] // 2, width), jnp.bfloat16)] * (2 * kind[0])
    return call(
        functools.partial(down_kernel, top, e, tile, kind),
        [scalars, hidden, down, table, *more],
        [SMEM_SPEC] + [VMEM_SPEC] * (3 + len(more)),
        outs,
        [],
        8,
        (2 * rows * units * width, 2 * units * width),
    )


def shards(
    tokens,
    expert_ids,
    gate_weights,
    expert_gate,
    expert_up,
    expert_down,
    shared_gate,
    shared_up,
    shared_down,
    encoder,
    encoder_bias,
    decoder,
    decoder_bias,
):
    own, top = expert_ids.shape
    width = tokens.shape[1]
    feats = lax.axis_size("feat")
    pairs = lax.axis_size("expert") // 2
    devices = 2 * pairs * feats
    local_experts = range(expert_gate.shape[0])
    me = lax.axis_index(("expert", "feat"))
    my_feat = lax.axis_index("feat")
    feat_bits = bits_of(feats)
    place = [(my_feat // bit) % 2 for bit in feat_bits]
    scalars = jnp.stack([me, place[0]])
    chunk_rows = pairs * feats // 2 * own

    table = run_pack(my_feat, expert_ids, gate_weights, feats)
    for bit in feat_bits:
        table = table + swap(table, "feat", bit)
    tables = [swap(table, "expert", 2 * p) for p in range(1, pairs)]

    near = [swap(tokens, "expert", 2 * p) for p in range(1, pairs)]
    far = [swap(piece, "expert", 1) for piece in [tokens] + near]
    table, mine = run_load(table, tokens)
    near = [mine] + near

    hidden = [list(run_hidden(near, expert_gate, expert_up, e, True)) for e in local_experts]
    hidden[0][0], *rest = lax.optimization_barrier((hidden[0][0], *tables, *far))
    table = jnp.concatenate([table] + rest[: pairs - 1], axis=0)
    far = rest[pairs - 1 :]
    table_far = swap(table, "expert", 1)
    arrived = None
    for e in local_experts:
        more = [] if arrived is None else [arrived]
        arrived = run_down(hidden[e][0], expert_down, e, scalars, table, top, more)[0]
    arrived = swap(arrived, "expert", 1)
    for e in local_experts:
        hidden_far = run_hidden(far, hidden[e][1], hidden[e][2], e, False)[0]
        if e < local_experts[-1]:
            more = [arrived]
            arrived = run_down(hidden_far, expert_down, e, scalars, table_far, top, more)[0]
    blocks = run_down(
        hidden_far, expert_down, e, scalars, table_far, top, [arrived], (pairs, own)
    )
    blocks = [blocks[:pairs], blocks[pairs:]]
    blocks = [
        [mine[0]] + [swap(mine[p], "expert", 2 * p) for p in range(1, pairs)] for mine in blocks
    ]
    scalars, blocks[0][-1] = lax.optimization_barrier((scalars, blocks[0][-1]))
    shared_out = run_shared(scalars, far[0], [shared_gate, shared_up, shared_down], own)
    totals = [sum(full(part) for part in blocks[i] + [shared_out[i]]) for i in range(2)]

    total = totals[1] + full(swap(half(totals[0]), "feat", feat_bits[0]))
    total = total.reshape((2,) * (len(feat_bits) - 1) + (own, width))
    for i, bit in enumerate(feat_bits[1:-1]):
        dim = len(feat_bits) - 2 - i
        arrived = swap(half(take(total, 1 - place[i + 1], dim)), "feat", bit)
        total = take(total, place[i + 1], dim) + full(arrived)
    total = half(total)
    moe_out = half(full(total) + full(swap(total, "feat", feat_bits[-1])))
    for bit in feat_bits[-2:0:-1]:
        moe_out = jnp.stack([moe_out, swap(moe_out, "feat", bit)], axis=moe_out.ndim - 2)
    moe_out = moe_out.reshape(-1, width)
    other = swap(moe_out, "feat", feat_bits[0])
    parts = [moe_out] + [swap(moe_out, "expert", 2 * p) for p in range(1, pairs - 1)]
    mine, other = lax.optimization_barrier((moe_out, other))
    parts.append(swap(mine, "expert", 2 * (pairs - 1)))
    sides = [[other] + [swap(other, "expert", 2 * p) for p in range(1, pairs)], parts]

    def encode(x):
        return half(jax.nn.relu(dot(x, encoder) + encoder_bias[None, :]))

    features, blocks = [None, None], [None, None]
    for chunk in (1, 0):
        near = jnp.stack(sides[chunk]).reshape(chunk_rows, width)
        far = swap(near, "expert", 1)
        features_near = encode(near)
        decoded = swap(half(dot(features_near, decoder)), "expert", 1)
        features_far = encode(far)
        total = half(dot(features_far, decoder) + full(decoded))
        total = total.reshape(pairs, feats // 2 * own, width)
        blocks[chunk] = [total[0]] + [swap(total[p], "expert", 2 * p) for p in range(1, pairs)]
        both = jnp.stack([features_far, features_near])
        features[chunk] = both.reshape(2, pairs, feats // 2, 1, own, -1)
    arrived = swap(half(sum(full(block) for block in blocks[1])), "feat", feat_bits[0])
    total = sum(full(block) for block in blocks[0])
    total = (total + full(arrived)).reshape((2,) * (len(feat_bits) - 1) + (own, width))
    for bit in feat_bits[1:-1]:
        dim = len(total.shape) - 3
        arrived = swap(half(lax.index_in_dim(total, 1, dim, False)), "feat", bit)
        total = lax.index_in_dim(total, 0, dim, False) + full(arrived)
    arrived = swap(half(take(total, 1 - place[-1], 0)), "feat", feat_bits[-1])
    reconstruction = take(total, place[-1], 0) + full(arrived) + decoder_bias[None, :]

    features = jnp.concatenate(features, axis=3).transpose(1, 0, 2, 3, 4, 5)
    features = features.reshape(devices, own, -1)
    relative = me - me % feats + my_feat % (feats // 2)
    blocks = [lax.dynamic_index_in_dim(features, i ^ relative, 0) for i in range(devices)]
    features = jnp.concatenate(blocks, axis=0).reshape(devices * own, -1)
    return (features, reconstruction)


def solution(mesh):
    return jax.shard_map(
        shards,
        mesh=mesh,
        in_specs=(
            P("expert", None),
            P(("expert", "feat"), None),
            P(("expert", "feat"), None),
            P(("expert", "feat"), None, None),
            P(("expert", "feat"), None, None),
            P(("expert", "feat"), None, None),
            P(None, "feat"),
            P(None, "feat"),
            P("feat", None),
            P(None, ("expert", "feat")),
            P(("expert", "feat")),
            P(("expert", "feat"), None),
            P(),
        ),
        out_specs=(P(None, ("expert", "feat")), P(("expert", "feat"), None)),
        check_vma=False,
    )
```

```python
import functools

import jax
import jax.numpy as jnp
from jax import lax
from jax.experimental import pallas as pl
from jax.experimental.pallas import tpu as pltpu
from jax.sharding import PartitionSpec as P

LANES = 128
MIB = 1024 * 1024
LOAD_MIB = 40
VMEM_SPEC = pl.BlockSpec(memory_space=pltpu.VMEM)
SMEM_SPEC = pl.BlockSpec(memory_space=pltpu.SMEM)
HBM_SPEC = pl.BlockSpec(memory_space=pltpu.HBM)


def swap(value, axis, r):
    return lax.ppermute(value, axis, [(i, i ^ r) for i in range(lax.axis_size(axis))])


def dot(a, b):
    return jnp.dot(a, b, preferred_element_type=jnp.float32)


def half(value):
    return value.astype(jnp.bfloat16)


def full(value):
    return value.astype(jnp.float32)


def silu(value):
    return value / (1.0 + jnp.exp(-value))


def bits_of(count):
    assert count & (count - 1) == 0
    return [1 << b for b in range(count.bit_length() - 1)]


def take(value, index, dim):
    return lax.dynamic_index_in_dim(value, index, dim, keepdims=False)


def call(body, operands, specs, outs, scratch, mib, cost):
    flops, moved = cost
    return pl.pallas_call(
        body,
        in_specs=specs,
        out_specs=[VMEM_SPEC] * len(outs),
        out_shape=[jax.ShapeDtypeStruct(shape, dtype) for shape, dtype in outs],
        scratch_shapes=scratch,
        compiler_params=pltpu.CompilerParams(vmem_limit_bytes=mib * MIB),
        cost_estimate=pl.CostEstimate(flops=flops, bytes_accessed=moved, transcendentals=0),
    )(*operands)


def start_all(pairs, sems):
    copies = [pltpu.make_async_copy(a, b, sems.at[i]) for i, (a, b) in enumerate(pairs)]
    for copy in copies:
        copy.start()
    return copies


def pack_kernel(ids, weights, out):
    top, own = ids.shape
    lane = lax.broadcasted_iota(jnp.int32, (top, LANES), 1)
    row = lax.broadcasted_iota(jnp.int32, (top, LANES), 0)
    high = half(weights[...])
    low = half(weights[...] - full(high))
    values = jnp.zeros((own, LANES), jnp.float32)
    for i, part in enumerate([half(full(ids[...])), high, low]):
        places = half(jnp.where(lane == row + i * top, 1.0, 0.0))
        values += lax.dot_general(
            part, places, (((0,), (0,)), ((), ())), preferred_element_type=jnp.float32
        )
    out[...] = half(values)


def run_pack(expert_ids, gate_weights):
    own, top = expert_ids.shape
    return call(
        pack_kernel,
        [expert_ids.T, gate_weights.T],
        [VMEM_SPEC] * 2,
        [((own, LANES), jnp.bfloat16)],
        [],
        2,
        (6 * own * top * LANES, 2 * own * LANES),
    )[0]


def load_kernel(*refs):
    count = (len(refs) - 1) // 2
    copies = start_all(list(zip(refs[:count], refs[count:-1])), refs[-1])
    for copy in copies:
        copy.wait()


def run_load(values):
    count = len(values)
    return call(
        load_kernel,
        values,
        [HBM_SPEC] * count,
        [(value.shape, value.dtype) for value in values],
        [pltpu.SemaphoreType.DMA((count,))],
        LOAD_MIB,
        (550 * sum(value.size for value in values), 4 * sum(value.size for value in values)),
    )


def shared_kernel(own, scalars, x, gate, up, down, kept, sent):
    hidden = half(silu(dot(x[...], gate[...])) * dot(x[...], up[...]))
    rows, width = x.shape
    for j in range(0, width, 256):
        cut = slice(j, j + 256)
        value = dot(hidden, down[:, cut]).reshape(rows // own // 2, 2, own, -1)
        low, high = [value[:, i].reshape(rows // 2, -1) for i in range(2)]
        kept[:, cut] = jnp.where(scalars[1] == 0, low, high)
        sent[:, cut] = jnp.where(scalars[1] == 0, high, low)


def run_shared(scalars, x, weights, own):
    rows, width = x.shape
    return call(
        functools.partial(shared_kernel, own),
        [scalars, x, *weights],
        [SMEM_SPEC] + [VMEM_SPEC] * 4,
        [((rows // 2, width), jnp.float32)] * 2,
        [],
        6,
        (6 * rows * weights[0].size, 6 * weights[0].size),
    )


def hidden_kernel(count, e, tile, *refs):
    pieces, (gate, up, out, rows) = refs[:count], refs[count:]
    size = pieces[0].shape[0]
    for i in range(count):
        rows[i * size : (i + 1) * size, :] = pieces[i][...]
    for j in range(0, out.shape[1], tile):
        cut = slice(j, j + tile)
        value = silu(dot(rows[...], gate[e, :, cut]))
        out[:, cut] = half(value * dot(rows[...], up[e, :, cut]))


def run_hidden(pieces, gate, up, e):
    count, (size, width) = len(pieces), pieces[0].shape
    units = gate.shape[2]
    return call(
        functools.partial(hidden_kernel, count, e, min(256, units)),
        [*pieces, gate, up],
        [VMEM_SPEC] * (count + 2),
        [((count * size, units), jnp.bfloat16)],
        [pltpu.VMEM((count * size, width), jnp.bfloat16)],
        8,
        (4 * count * size * width * units, 4 * width * units),
    )[0]


def down_kernel(top, e, tile, pairs, flip, kind, scalars, hidden, down, table, *refs):
    count = 1 if kind is None else 2 * kind[0]
    more, outs = refs[:-count], refs[-count:]
    size = hidden.shape[0] // pairs
    entries = []
    for p in range(pairs):
        owner = 2 * jnp.bitwise_xor(scalars[2], p) + jnp.bitwise_xor(scalars[3], flip)
        entries.append(full(table[pl.ds(pl.multiple_of(owner * size, size), size), :]))
    entries = jnp.concatenate(entries, axis=0)
    lane = lax.broadcasted_iota(jnp.int32, entries.shape, 1)
    expert = (scalars[0] * down.shape[0] + e).astype(jnp.float32)
    chosen = jnp.where((entries == expert) & (lane < top), 1.0, 0.0)
    chosen = pltpu.roll(chosen, top, 1) + pltpu.roll(chosen, 2 * top, 1)
    scale = jnp.sum(chosen * entries, axis=1, keepdims=True)
    for j in range(0, down.shape[2], tile):
        cut = slice(j, j + tile)
        value = dot(hidden[...], down[e, :, cut]) * scale
        if more:
            value += full(more[0][:, cut])
        if kind is None:
            outs[0][:, cut] = half(value)
            continue
        own = kind[1]
        for p in range(pairs):
            block = value[p * size : (p + 1) * size]
            block = block.reshape(size // own // 2, 2, own, tile)
            low, high = block[:, 0].reshape(-1, tile), block[:, 1].reshape(-1, tile)
            outs[p][:, cut] = half(jnp.where(scalars[1] == 0, low, high))
            outs[pairs + p][:, cut] = half(jnp.where(scalars[1] == 0, high, low))


def run_down(hidden, down, e, scalars, table, top, pairs, flip, more=(), kind=None):
    rows, units = hidden.shape
    width = down.shape[2]
    tile = 256 if width % 256 == 0 else 128
    outs = [((rows, width), jnp.bfloat16)]
    if kind is not None:
        outs = [((rows // kind[0] // 2, width), jnp.bfloat16)] * (2 * kind[0])
    return call(
        functools.partial(down_kernel, top, e, tile, pairs, flip, kind),
        [scalars, hidden, down, table, *more],
        [SMEM_SPEC] + [VMEM_SPEC] * (3 + len(more)),
        outs,
        [],
        8,
        (2 * rows * units * width, 2 * units * width),
    )


def shards(
    tokens,
    expert_ids,
    gate_weights,
    expert_gate,
    expert_up,
    expert_down,
    shared_gate,
    shared_up,
    shared_down,
    encoder,
    encoder_bias,
    decoder,
    decoder_bias,
):
    own, top = expert_ids.shape
    width = tokens.shape[1]
    feats = lax.axis_size("feat")
    pairs = lax.axis_size("expert") // 2
    devices = 2 * pairs * feats
    local_experts = range(expert_gate.shape[0])
    me = lax.axis_index(("expert", "feat"))
    my_feat = lax.axis_index("feat")
    feat_bits = bits_of(feats)
    place = [(my_feat // bit) % 2 for bit in feat_bits]
    my_expert = lax.axis_index("expert")
    scalars = jnp.stack([me, place[0], my_expert // 2, my_expert % 2])
    chunk_rows = pairs * feats // 2 * own

    table = run_pack(expert_ids, gate_weights)
    table = lax.all_gather(table, ("expert", "feat"), axis=0, tiled=True)

    near = [swap(tokens, "expert", 2 * p) for p in range(1, pairs)]
    far = [swap(piece, "expert", 1) for piece in [tokens] + near]
    mine, expert_gate, expert_up = run_load([tokens, expert_gate, expert_up])
    near = [mine] + near

    hidden = [run_hidden(near, expert_gate, expert_up, e) for e in local_experts]
    hidden[0], *far = lax.optimization_barrier((hidden[0], *far))
    arrived = None
    for e in local_experts:
        more = [] if arrived is None else [arrived]
        arrived = run_down(hidden[e], expert_down, e, scalars, table, top, pairs, 0, more)[0]
    arrived = swap(arrived, "expert", 1)
    for e in local_experts:
        hidden = run_hidden(far, expert_gate, expert_up, e)
        if e < local_experts[-1]:
            more = [arrived]
            arrived = run_down(hidden, expert_down, e, scalars, table, top, pairs, 1, more)[0]
    blocks = run_down(
        hidden, expert_down, e, scalars, table, top, pairs, 1, [arrived], (pairs, own)
    )
    blocks = [blocks[:pairs], blocks[pairs:]]
    blocks = [
        [mine[0]] + [swap(mine[p], "expert", 2 * p) for p in range(1, pairs)] for mine in blocks
    ]
    scalars, blocks[0][-1] = lax.optimization_barrier((scalars, blocks[0][-1]))
    shared_out = run_shared(scalars, far[0], [shared_gate, shared_up, shared_down], own)
    totals = [sum(full(part) for part in blocks[i] + [shared_out[i]]) for i in range(2)]

    total = totals[1] + full(swap(half(totals[0]), "feat", feat_bits[0]))
    total = total.reshape((2,) * (len(feat_bits) - 1) + (own, width))
    for i, bit in enumerate(feat_bits[1:-1]):
        dim = len(feat_bits) - 2 - i
        arrived = swap(half(take(total, 1 - place[i + 1], dim)), "feat", bit)
        total = take(total, place[i + 1], dim) + full(arrived)
    total = half(total)
    moe_out = half(full(total) + full(swap(total, "feat", feat_bits[-1])))
    for bit in feat_bits[-2:0:-1]:
        moe_out = jnp.stack([moe_out, swap(moe_out, "feat", bit)], axis=moe_out.ndim - 2)
    moe_out = moe_out.reshape(-1, width)
    other = swap(moe_out, "feat", feat_bits[0])
    parts = [moe_out] + [swap(moe_out, "expert", 2 * p) for p in range(1, pairs - 1)]
    mine, other = lax.optimization_barrier((moe_out, other))
    parts.append(swap(mine, "expert", 2 * (pairs - 1)))
    sides = [[other] + [swap(other, "expert", 2 * p) for p in range(1, pairs)], parts]

    def encode(x):
        return half(jax.nn.relu(dot(x, encoder) + encoder_bias[None, :]))

    features, blocks = [None, None], [None, None]
    for chunk in (1, 0):
        near = jnp.stack(sides[chunk]).reshape(chunk_rows, width)
        far = swap(near, "expert", 1)
        features_near = encode(near)
        decoded = swap(half(dot(features_near, decoder)), "expert", 1)
        features_far = encode(far)
        total = half(dot(features_far, decoder) + full(decoded))
        total = total.reshape(pairs, feats // 2 * own, width)
        blocks[chunk] = [total[0]] + [swap(total[p], "expert", 2 * p) for p in range(1, pairs)]
        both = jnp.stack([features_far, features_near])
        features[chunk] = both.reshape(2, pairs, feats // 2, 1, own, -1)
    arrived = swap(half(sum(full(block) for block in blocks[1])), "feat", feat_bits[0])
    total = sum(full(block) for block in blocks[0])
    total = (total + full(arrived)).reshape((2,) * (len(feat_bits) - 1) + (own, width))
    for bit in feat_bits[1:-1]:
        dim = len(total.shape) - 3
        arrived = swap(half(lax.index_in_dim(total, 1, dim, False)), "feat", bit)
        total = lax.index_in_dim(total, 0, dim, False) + full(arrived)
    arrived = swap(half(take(total, 1 - place[-1], 0)), "feat", feat_bits[-1])
    reconstruction = take(total, place[-1], 0) + full(arrived) + decoder_bias[None, :]

    features = jnp.concatenate(features, axis=3).transpose(1, 0, 2, 3, 4, 5)
    features = features.reshape(devices, own, -1)
    relative = me - me % feats + my_feat % (feats // 2)
    blocks = [lax.dynamic_index_in_dim(features, i ^ relative, 0) for i in range(devices)]
    features = jnp.concatenate(blocks, axis=0).reshape(devices * own, -1)
    return (features, reconstruction)


def solution(mesh):
    return jax.shard_map(
        shards,
        mesh=mesh,
        in_specs=(
            P("expert", None),
            P(("expert", "feat"), None),
            P(("expert", "feat"), None),
            P(("expert", "feat"), None, None),
            P(("expert", "feat"), None, None),
            P(("expert", "feat"), None, None),
            P(None, "feat"),
            P(None, "feat"),
            P("feat", None),
            P(None, ("expert", "feat")),
            P(("expert", "feat")),
            P(("expert", "feat"), None),
            P(),
        ),
        out_specs=(P(None, ("expert", "feat")), P(("expert", "feat"), None)),
        check_vma=False,
    )
```

```python
import functools

import jax
import jax.numpy as jnp
from jax import lax
from jax.experimental import pallas as pl
from jax.experimental.pallas import tpu as pltpu
from jax.sharding import PartitionSpec as P

LANES = 128
MIB = 1024 * 1024
LOAD_MIB = 40
VMEM_SPEC = pl.BlockSpec(memory_space=pltpu.VMEM)
SMEM_SPEC = pl.BlockSpec(memory_space=pltpu.SMEM)
HBM_SPEC = pl.BlockSpec(memory_space=pltpu.HBM)


def swap(value, axis, r):
    return lax.ppermute(value, axis, [(i, i ^ r) for i in range(lax.axis_size(axis))])


def dot(a, b):
    return jnp.dot(a, b, preferred_element_type=jnp.float32)


def half(value):
    return value.astype(jnp.bfloat16)


def full(value):
    return value.astype(jnp.float32)


def silu(value):
    return value / (1.0 + jnp.exp(-value))


def bits_of(count):
    assert count & (count - 1) == 0
    return [1 << b for b in range(count.bit_length() - 1)]


def take(value, index, dim):
    return lax.dynamic_index_in_dim(value, index, dim, keepdims=False)


def call(body, operands, specs, outs, scratch, mib, cost):
    flops, moved = cost
    return pl.pallas_call(
        body,
        in_specs=specs,
        out_specs=[VMEM_SPEC] * len(outs),
        out_shape=[jax.ShapeDtypeStruct(shape, dtype) for shape, dtype in outs],
        scratch_shapes=scratch,
        compiler_params=pltpu.CompilerParams(vmem_limit_bytes=mib * MIB),
        cost_estimate=pl.CostEstimate(flops=flops, bytes_accessed=moved, transcendentals=0),
    )(*operands)


def start_all(pairs, sems):
    copies = [pltpu.make_async_copy(a, b, sems.at[i]) for i, (a, b) in enumerate(pairs)]
    for copy in copies:
        copy.start()
    return copies


def pack_kernel(ids, weights, out):
    top, own = ids.shape
    lane = lax.broadcasted_iota(jnp.int32, (top, LANES), 1)
    row = lax.broadcasted_iota(jnp.int32, (top, LANES), 0)
    high = half(weights[...])
    low = half(weights[...] - full(high))
    values = jnp.zeros((own, LANES), jnp.float32)
    for i, part in enumerate([half(full(ids[...])), high, low]):
        places = half(jnp.where(lane == row + i * top, 1.0, 0.0))
        values += lax.dot_general(
            part, places, (((0,), (0,)), ((), ())), preferred_element_type=jnp.float32
        )
    out[...] = half(values)


def run_pack(expert_ids, gate_weights):
    own, top = expert_ids.shape
    return call(
        pack_kernel,
        [expert_ids.T, gate_weights.T],
        [VMEM_SPEC] * 2,
        [((own, LANES), jnp.bfloat16)],
        [],
        2,
        (6 * own * top * LANES, 2 * own * LANES),
    )[0]


def load_kernel(*refs):
    count = (len(refs) - 1) // 2
    copies = start_all(list(zip(refs[:count], refs[count:-1])), refs[-1])
    for copy in copies:
        copy.wait()


def run_load(values):
    count = len(values)
    return call(
        load_kernel,
        values,
        [HBM_SPEC] * count,
        [(value.shape, value.dtype) for value in values],
        [pltpu.SemaphoreType.DMA((count,))],
        LOAD_MIB,
        (550 * sum(value.size for value in values), 4 * sum(value.size for value in values)),
    )


def shared_kernel(own, scalars, x, gate, up, down, kept, sent):
    hidden = half(silu(dot(x[...], gate[...])) * dot(x[...], up[...]))
    rows, width = x.shape
    for j in range(0, width, 256):
        cut = slice(j, j + 256)
        value = dot(hidden, down[:, cut]).reshape(rows // own // 2, 2, own, -1)
        low, high = [value[:, i].reshape(rows // 2, -1) for i in range(2)]
        kept[:, cut] = jnp.where(scalars[1] == 0, low, high)
        sent[:, cut] = jnp.where(scalars[1] == 0, high, low)


def run_shared(scalars, x, weights, own):
    rows, width = x.shape
    return call(
        functools.partial(shared_kernel, own),
        [scalars, x, *weights],
        [SMEM_SPEC] + [VMEM_SPEC] * 4,
        [((rows // 2, width), jnp.float32)] * 2,
        [],
        6,
        (6 * rows * weights[0].size, 6 * weights[0].size),
    )


def hidden_kernel(count, e, tile, *refs):
    pieces, (gate, up, out, rows) = refs[:count], refs[count:]
    size = pieces[0].shape[0]
    for i in range(count):
        rows[i * size : (i + 1) * size, :] = pieces[i][...]
    for j in range(0, out.shape[1], tile):
        cut = slice(j, j + tile)
        value = silu(dot(rows[...], gate[e, :, cut]))
        out[:, cut] = half(value * dot(rows[...], up[e, :, cut]))


def run_hidden(pieces, gate, up, e):
    count, (size, width) = len(pieces), pieces[0].shape
    units = gate.shape[2]
    return call(
        functools.partial(hidden_kernel, count, e, min(256, units)),
        [*pieces, gate, up],
        [VMEM_SPEC] * (count + 2),
        [((count * size, units), jnp.bfloat16)],
        [pltpu.VMEM((count * size, width), jnp.bfloat16)],
        8,
        (4 * count * size * width * units, 4 * width * units),
    )[0]


def down_kernel(top, e, tile, feats, pairs, kind, scalars, hidden, down, table, *refs):
    count = 1 if kind is None else 2 * kind[0]
    more, outs = refs[:-count], refs[-count:]
    size = hidden.shape[0] // pairs
    own = size // feats
    entries = []
    for p in range(pairs):
        for f in range(feats):
            start = (jnp.bitwise_xor(scalars[2], f) * pairs + p) * own
            entries.append(full(table[pl.ds(pl.multiple_of(start, own), own), :]))
    entries = jnp.concatenate(entries, axis=0)
    lane = lax.broadcasted_iota(jnp.int32, entries.shape, 1)
    expert = (scalars[0] * down.shape[0] + e).astype(jnp.float32)
    chosen = jnp.where((entries == expert) & (lane < top), 1.0, 0.0)
    chosen = pltpu.roll(chosen, top, 1) + pltpu.roll(chosen, 2 * top, 1)
    scale = jnp.sum(chosen * entries, axis=1, keepdims=True)
    for j in range(0, down.shape[2], tile):
        cut = slice(j, j + tile)
        value = dot(hidden[...], down[e, :, cut]) * scale
        if more:
            value += full(more[0][:, cut])
        if kind is None:
            outs[0][:, cut] = half(value)
            continue
        for p in range(pairs):
            block = value[p * size : (p + 1) * size]
            block = block.reshape(size // own // 2, 2, own, tile)
            low, high = block[:, 0].reshape(-1, tile), block[:, 1].reshape(-1, tile)
            outs[p][:, cut] = half(jnp.where(scalars[1] == 0, low, high))
            outs[pairs + p][:, cut] = half(jnp.where(scalars[1] == 0, high, low))


def run_down(hidden, down, e, scalars, table, top, feats, pairs, more=(), kind=None):
    rows, units = hidden.shape
    width = down.shape[2]
    tile = 256 if width % 256 == 0 else 128
    outs = [((rows, width), jnp.bfloat16)]
    if kind is not None:
        outs = [((rows // kind[0] // 2, width), jnp.bfloat16)] * (2 * kind[0])
    return call(
        functools.partial(down_kernel, top, e, tile, feats, pairs, kind),
        [scalars, hidden, down, table, *more],
        [SMEM_SPEC] + [VMEM_SPEC] * (3 + len(more)),
        outs,
        [],
        8,
        (2 * rows * units * width, 2 * units * width),
    )


def shards(
    tokens,
    expert_ids,
    gate_weights,
    expert_gate,
    expert_up,
    expert_down,
    shared_gate,
    shared_up,
    shared_down,
    encoder,
    encoder_bias,
    decoder,
    decoder_bias,
):
    own, top = expert_ids.shape
    width = tokens.shape[1]
    feats = lax.axis_size("feat")
    pairs = lax.axis_size("expert") // 2
    devices = 2 * pairs * feats
    local_experts = range(expert_gate.shape[0])
    me = lax.axis_index(("expert", "feat"))
    my_feat = lax.axis_index("feat")
    feat_bits = bits_of(feats)
    place = [(my_feat // bit) % 2 for bit in feat_bits]
    scalars = jnp.stack([me, place[0], my_feat])
    chunk_rows = pairs * feats // 2 * own

    table = run_pack(expert_ids, gate_weights)
    table = [table] + [swap(table, "expert", 2 * p) for p in range(1, pairs)]
    sent, table[1] = lax.optimization_barrier((tokens, table[1]))
    table = jnp.concatenate(table, axis=0)
    mine, table = lax.optimization_barrier((tokens, table))
    for bit in feat_bits:
        table = jnp.concatenate([table, swap(table, "feat", bit)], axis=0)
    table_far = swap(table, "expert", 1)

    near = [swap(sent, "expert", 2 * p) for p in range(1, pairs)]
    far = [swap(piece, "expert", 1) for piece in [sent] + near]
    mine, expert_gate, expert_up = run_load([mine, expert_gate, expert_up])
    near = [mine] + near

    hidden = [run_hidden(near, expert_gate, expert_up, e) for e in local_experts]
    hidden[0], *far = lax.optimization_barrier((hidden[0], *far))
    arrived = None
    for e in local_experts:
        more = [] if arrived is None else [arrived]
        arrived = run_down(hidden[e], expert_down, e, scalars, table, top, feats, pairs, more)[0]
    arrived = swap(arrived, "expert", 1)
    for e in local_experts:
        hidden = run_hidden(far, expert_gate, expert_up, e)
        if e < local_experts[-1]:
            more = [arrived]
            arrived = run_down(hidden, expert_down, e, scalars, table_far, top, feats, pairs, more)[0]
    blocks = run_down(
        hidden, expert_down, e, scalars, table_far, top, feats, pairs, [arrived], (pairs, own)
    )
    blocks = [blocks[:pairs], blocks[pairs:]]
    blocks = [
        [mine[0]] + [swap(mine[p], "expert", 2 * p) for p in range(1, pairs)] for mine in blocks
    ]
    scalars, blocks[0][-1] = lax.optimization_barrier((scalars, blocks[0][-1]))
    shared_out = run_shared(scalars, far[0], [shared_gate, shared_up, shared_down], own)
    totals = [sum(full(part) for part in blocks[i] + [shared_out[i]]) for i in range(2)]

    total = totals[1] + full(swap(half(totals[0]), "feat", feat_bits[0]))
    total = total.reshape((2,) * (len(feat_bits) - 1) + (own, width))
    for i, bit in enumerate(feat_bits[1:-1]):
        dim = len(feat_bits) - 2 - i
        arrived = swap(half(take(total, 1 - place[i + 1], dim)), "feat", bit)
        total = take(total, place[i + 1], dim) + full(arrived)
    total = half(total)
    moe_out = half(full(total) + full(swap(total, "feat", feat_bits[-1])))
    for bit in feat_bits[-2:0:-1]:
        moe_out = jnp.stack([moe_out, swap(moe_out, "feat", bit)], axis=moe_out.ndim - 2)
    moe_out = moe_out.reshape(-1, width)
    other = swap(moe_out, "feat", feat_bits[0])
    parts = [moe_out] + [swap(moe_out, "expert", 2 * p) for p in range(1, pairs - 1)]
    mine, other = lax.optimization_barrier((moe_out, other))
    parts.append(swap(mine, "expert", 2 * (pairs - 1)))
    sides = [[other] + [swap(other, "expert", 2 * p) for p in range(1, pairs)], parts]

    def encode(x):
        return half(jax.nn.relu(dot(x, encoder) + encoder_bias[None, :]))

    features, blocks = [None, None], [None, None]
    for chunk in (1, 0):
        near = jnp.stack(sides[chunk]).reshape(chunk_rows, width)
        far = swap(near, "expert", 1)
        features_near = encode(near)
        decoded = swap(half(dot(features_near, decoder)), "expert", 1)
        features_far = encode(far)
        total = half(dot(features_far, decoder) + full(decoded))
        total = total.reshape(pairs, feats // 2 * own, width)
        blocks[chunk] = [total[0]] + [swap(total[p], "expert", 2 * p) for p in range(1, pairs)]
        both = jnp.stack([features_far, features_near])
        features[chunk] = both.reshape(2, pairs, feats // 2, 1, own, -1)
    arrived = swap(half(sum(full(block) for block in blocks[1])), "feat", feat_bits[0])
    total = sum(full(block) for block in blocks[0])
    total = (total + full(arrived)).reshape((2,) * (len(feat_bits) - 1) + (own, width))
    for bit in feat_bits[1:-1]:
        dim = len(total.shape) - 3
        arrived = swap(half(lax.index_in_dim(total, 1, dim, False)), "feat", bit)
        total = lax.index_in_dim(total, 0, dim, False) + full(arrived)
    arrived = swap(half(take(total, 1 - place[-1], 0)), "feat", feat_bits[-1])
    reconstruction = take(total, place[-1], 0) + full(arrived) + decoder_bias[None, :]

    features = jnp.concatenate(features, axis=3).transpose(1, 0, 2, 3, 4, 5)
    features = features.reshape(devices, own, -1)
    relative = me - me % feats + my_feat % (feats // 2)
    blocks = [lax.dynamic_index_in_dim(features, i ^ relative, 0) for i in range(devices)]
    features = jnp.concatenate(blocks, axis=0).reshape(devices * own, -1)
    return (features, reconstruction)


def solution(mesh):
    return jax.shard_map(
        shards,
        mesh=mesh,
        in_specs=(
            P("expert", None),
            P(("expert", "feat"), None),
            P(("expert", "feat"), None),
            P(("expert", "feat"), None, None),
            P(("expert", "feat"), None, None),
            P(("expert", "feat"), None, None),
            P(None, "feat"),
            P(None, "feat"),
            P("feat", None),
            P(None, ("expert", "feat")),
            P(("expert", "feat")),
            P(("expert", "feat"), None),
            P(),
        ),
        out_specs=(P(None, ("expert", "feat")), P(("expert", "feat"), None)),
        check_vma=False,
    )
```

```python
import functools

import jax
import jax.numpy as jnp
from jax import lax
from jax.experimental import pallas as pl
from jax.experimental.pallas import tpu as pltpu
from jax.sharding import PartitionSpec as P

LANES = 128
MIB = 1024 * 1024
LOAD_MIB = 40
VMEM_SPEC = pl.BlockSpec(memory_space=pltpu.VMEM)
SMEM_SPEC = pl.BlockSpec(memory_space=pltpu.SMEM)
HBM_SPEC = pl.BlockSpec(memory_space=pltpu.HBM)


def swap(value, axis, r):
    return lax.ppermute(value, axis, [(i, i ^ r) for i in range(lax.axis_size(axis))])


def dot(a, b):
    return jnp.dot(a, b, preferred_element_type=jnp.float32)


def half(value):
    return value.astype(jnp.bfloat16)


def full(value):
    return value.astype(jnp.float32)


def silu(value):
    return value / (1.0 + jnp.exp(-value))


def bits_of(count):
    assert count & (count - 1) == 0
    return [1 << b for b in range(count.bit_length() - 1)]


def take(value, index, dim):
    return lax.dynamic_index_in_dim(value, index, dim, keepdims=False)


def call(body, operands, specs, outs, scratch, mib, cost):
    flops, moved = cost
    return pl.pallas_call(
        body,
        in_specs=specs,
        out_specs=[VMEM_SPEC] * len(outs),
        out_shape=[jax.ShapeDtypeStruct(shape, dtype) for shape, dtype in outs],
        scratch_shapes=scratch,
        compiler_params=pltpu.CompilerParams(vmem_limit_bytes=mib * MIB),
        cost_estimate=pl.CostEstimate(flops=flops, bytes_accessed=moved, transcendentals=0),
    )(*operands)


def start_all(pairs, sems):
    copies = [pltpu.make_async_copy(a, b, sems.at[i]) for i, (a, b) in enumerate(pairs)]
    for copy in copies:
        copy.start()
    return copies


def pack_kernel(ids, weights, out):
    top, own = ids.shape
    lane = lax.broadcasted_iota(jnp.int32, (top, LANES), 1)
    row = lax.broadcasted_iota(jnp.int32, (top, LANES), 0)
    high = half(weights[...])
    low = half(weights[...] - full(high))
    values = jnp.zeros((own, LANES), jnp.float32)
    for i, part in enumerate([half(full(ids[...])), high, low]):
        places = half(jnp.where(lane == row + i * top, 1.0, 0.0))
        values += lax.dot_general(
            part, places, (((0,), (0,)), ((), ())), preferred_element_type=jnp.float32
        )
    out[...] = half(values)


def run_pack(expert_ids, gate_weights):
    own, top = expert_ids.shape
    return call(
        pack_kernel,
        [expert_ids.T, gate_weights.T],
        [VMEM_SPEC] * 2,
        [((own, LANES), jnp.bfloat16)],
        [],
        2,
        (6 * own * top * LANES, 2 * own * LANES),
    )[0]


def load_kernel(*refs):
    count = (len(refs) - 1) // 2
    copies = start_all(list(zip(refs[:count], refs[count:-1])), refs[-1])
    for copy in copies:
        copy.wait()


def run_load(values):
    count = len(values)
    return call(
        load_kernel,
        values,
        [HBM_SPEC] * count,
        [(value.shape, value.dtype) for value in values],
        [pltpu.SemaphoreType.DMA((count,))],
        LOAD_MIB,
        (550 * sum(value.size for value in values), 4 * sum(value.size for value in values)),
    )


def shared_kernel(own, scalars, x, gate, up, down, kept, sent):
    hidden = half(silu(dot(x[...], gate[...])) * dot(x[...], up[...]))
    rows, width = x.shape
    for j in range(0, width, 256):
        cut = slice(j, j + 256)
        value = dot(hidden, down[:, cut]).reshape(rows // own // 2, 2, own, -1)
        low, high = [value[:, i].reshape(rows // 2, -1) for i in range(2)]
        kept[:, cut] = jnp.where(scalars[1] == 0, low, high)
        sent[:, cut] = jnp.where(scalars[1] == 0, high, low)


def run_shared(scalars, x, weights, own):
    rows, width = x.shape
    return call(
        functools.partial(shared_kernel, own),
        [scalars, x, *weights],
        [SMEM_SPEC] + [VMEM_SPEC] * 4,
        [((rows // 2, width), jnp.float32)] * 2,
        [],
        6,
        (6 * rows * weights[0].size, 6 * weights[0].size),
    )


def hidden_kernel(count, e, tile, *refs):
    pieces, (gate, up, out, rows) = refs[:count], refs[count:]
    size = pieces[0].shape[0]
    for i in range(count):
        rows[i * size : (i + 1) * size, :] = pieces[i][...]
    for j in range(0, out.shape[1], tile):
        cut = slice(j, j + tile)
        value = silu(dot(rows[...], gate[e, :, cut]))
        out[:, cut] = half(value * dot(rows[...], up[e, :, cut]))


def run_hidden(pieces, gate, up, e):
    count, (size, width) = len(pieces), pieces[0].shape
    units = gate.shape[2]
    return call(
        functools.partial(hidden_kernel, count, e, min(256, units)),
        [*pieces, gate, up],
        [VMEM_SPEC] * (count + 2),
        [((count * size, units), jnp.bfloat16)],
        [pltpu.VMEM((count * size, width), jnp.bfloat16)],
        8,
        (4 * count * size * width * units, 4 * width * units),
    )[0]


def down_kernel(top, e, tile, feats, pairs, kind, scalars, hidden, down, table, *refs):
    count = 1 if kind is None else 2 * kind[0]
    more, outs = refs[:-count], refs[-count:]
    size = hidden.shape[0] // pairs
    own = size // feats
    entries = []
    for p in range(pairs):
        for f in range(feats):
            start = (jnp.bitwise_xor(scalars[2], f) * pairs + p) * own
            entries.append(full(table[pl.ds(pl.multiple_of(start, own), own), :]))
    entries = jnp.concatenate(entries, axis=0)
    lane = lax.broadcasted_iota(jnp.int32, entries.shape, 1)
    expert = (scalars[0] * down.shape[0] + e).astype(jnp.float32)
    chosen = jnp.where((entries == expert) & (lane < top), 1.0, 0.0)
    chosen = pltpu.roll(chosen, top, 1) + pltpu.roll(chosen, 2 * top, 1)
    scale = jnp.sum(chosen * entries, axis=1, keepdims=True)
    for j in range(0, down.shape[2], tile):
        cut = slice(j, j + tile)
        value = dot(hidden[...], down[e, :, cut]) * scale
        if more:
            value += full(more[0][:, cut])
        if kind is None:
            outs[0][:, cut] = half(value)
            continue
        for p in range(pairs):
            block = value[p * size : (p + 1) * size]
            block = block.reshape(size // own // 2, 2, own, tile)
            low, high = block[:, 0].reshape(-1, tile), block[:, 1].reshape(-1, tile)
            outs[p][:, cut] = half(jnp.where(scalars[1] == 0, low, high))
            outs[pairs + p][:, cut] = half(jnp.where(scalars[1] == 0, high, low))


def run_down(hidden, down, e, scalars, table, top, feats, pairs, more=(), kind=None):
    rows, units = hidden.shape
    width = down.shape[2]
    tile = 256 if width % 256 == 0 else 128
    outs = [((rows, width), jnp.bfloat16)]
    if kind is not None:
        outs = [((rows // kind[0] // 2, width), jnp.bfloat16)] * (2 * kind[0])
    return call(
        functools.partial(down_kernel, top, e, tile, feats, pairs, kind),
        [scalars, hidden, down, table, *more],
        [SMEM_SPEC] + [VMEM_SPEC] * (3 + len(more)),
        outs,
        [],
        8,
        (2 * rows * units * width, 2 * units * width),
    )


def shards(
    tokens,
    expert_ids,
    gate_weights,
    expert_gate,
    expert_up,
    expert_down,
    shared_gate,
    shared_up,
    shared_down,
    encoder,
    encoder_bias,
    decoder,
    decoder_bias,
):
    own, top = expert_ids.shape
    width = tokens.shape[1]
    feats = lax.axis_size("feat")
    pairs = lax.axis_size("expert") // 2
    devices = 2 * pairs * feats
    local_experts = range(expert_gate.shape[0])
    me = lax.axis_index(("expert", "feat"))
    my_feat = lax.axis_index("feat")
    feat_bits = bits_of(feats)
    place = [(my_feat // bit) % 2 for bit in feat_bits]
    scalars = jnp.stack([me, place[0], my_feat])
    chunk_rows = pairs * feats // 2 * own

    table = run_pack(expert_ids, gate_weights)
    table = [table] + [swap(table, "expert", 2 * p) for p in range(1, pairs)]
    sent, table[1] = lax.optimization_barrier((tokens, table[1]))
    table = jnp.concatenate(table, axis=0)
    mine, table = lax.optimization_barrier((tokens, table))
    for bit in feat_bits:
        table = jnp.concatenate([table, swap(table, "feat", bit)], axis=0)
    table_far = swap(table, "expert", 1)

    near = [swap(sent, "expert", 2 * p) for p in range(1, pairs)]
    far = [swap(piece, "expert", 1) for piece in [sent] + near]
    mine, expert_gate, expert_up = run_load([mine, expert_gate, expert_up])
    near = [mine] + near

    hidden = [run_hidden(near, expert_gate, expert_up, e) for e in local_experts]
    hidden[0], *far = lax.optimization_barrier((hidden[0], *far))
    arrived = None
    for e in local_experts:
        more = [] if arrived is None else [arrived]
        arrived = run_down(hidden[e], expert_down, e, scalars, table, top, feats, pairs, more)[0]
    arrived = swap(arrived, "expert", 1)
    for e in local_experts:
        hidden = run_hidden(far, expert_gate, expert_up, e)
        if e < local_experts[-1]:
            more = [arrived]
            arrived = run_down(hidden, expert_down, e, scalars, table_far, top, feats, pairs, more)[0]
    blocks = run_down(
        hidden, expert_down, e, scalars, table_far, top, feats, pairs, [arrived], (pairs, own)
    )
    blocks = [blocks[:pairs], blocks[pairs:]]
    blocks = [
        [mine[0]] + [swap(mine[p], "expert", 2 * p) for p in range(1, pairs)] for mine in blocks
    ]
    scalars, blocks[0][-1] = lax.optimization_barrier((scalars, blocks[0][-1]))
    shared_out = run_shared(scalars, far[0], [shared_gate, shared_up, shared_down], own)
    totals = [sum(full(part) for part in blocks[i] + [shared_out[i]]) for i in range(2)]

    total = totals[1] + full(swap(half(totals[0]), "feat", feat_bits[0]))
    total = total.reshape((2,) * (len(feat_bits) - 1) + (own, width))
    for i, bit in enumerate(feat_bits[1:-1]):
        dim = len(feat_bits) - 2 - i
        arrived = swap(half(take(total, 1 - place[i + 1], dim)), "feat", bit)
        total = take(total, place[i + 1], dim) + full(arrived)
    total = half(total)
    moe_out = half(full(total) + full(swap(total, "feat", feat_bits[-1])))
    for bit in feat_bits[-2:0:-1]:
        moe_out = jnp.stack([moe_out, swap(moe_out, "feat", bit)], axis=moe_out.ndim - 2)
    moe_out = moe_out.reshape(-1, width)
    other = swap(moe_out, "feat", feat_bits[0])
    parts = [moe_out] + [swap(moe_out, "expert", 2 * p) for p in range(1, pairs - 1)]
    mine, other = lax.optimization_barrier((moe_out, other))
    parts.append(swap(mine, "expert", 2 * (pairs - 1)))
    sides = [[other] + [swap(other, "expert", 2 * p) for p in range(1, pairs)], parts]

    def encode(x):
        return half(jax.nn.relu(dot(x, encoder) + encoder_bias[None, :]))

    features, blocks, zero = [None, None], [None, None], 0.0
    for chunk in (1, 0):
        near = jnp.stack(sides[chunk]).reshape(chunk_rows, width)
        far = swap(near, "expert", 1)
        features_near = encode(near)
        decoded = swap(half(dot(features_near, decoder)), "expert", 1)
        features_far = encode(far)
        total = half(dot(features_far, decoder) + full(decoded) + zero)
        total = total.reshape(pairs, feats // 2 * own, width)
        blocks[chunk] = [total[0]] + [swap(total[p], "expert", 2 * p) for p in range(1, pairs)]
        zero = 0.0 * full(blocks[chunk][1][0, 0])
        both = jnp.stack([features_far, features_near])
        features[chunk] = both.reshape(2, pairs, feats // 2, 1, own, -1)
    arrived = swap(half(sum(full(block) for block in blocks[1])), "feat", feat_bits[0])
    total = sum(full(block) for block in blocks[0])
    total = (total + full(arrived)).reshape((2,) * (len(feat_bits) - 1) + (own, width))
    for bit in feat_bits[1:-1]:
        dim = len(total.shape) - 3
        arrived = swap(half(lax.index_in_dim(total, 1, dim, False)), "feat", bit)
        total = lax.index_in_dim(total, 0, dim, False) + full(arrived)
    arrived = swap(half(take(total, 1 - place[-1], 0)), "feat", feat_bits[-1])
    reconstruction = take(total, place[-1], 0) + full(arrived) + decoder_bias[None, :]

    features = jnp.concatenate(features, axis=3).transpose(1, 0, 2, 3, 4, 5)
    features = features.reshape(devices, own, -1)
    relative = me - me % feats + my_feat % (feats // 2)
    blocks = [lax.dynamic_index_in_dim(features, i ^ relative, 0) for i in range(devices)]
    features = jnp.concatenate(blocks, axis=0).reshape(devices * own, -1)
    return (features, reconstruction)


def solution(mesh):
    return jax.shard_map(
        shards,
        mesh=mesh,
        in_specs=(
            P("expert", None),
            P(("expert", "feat"), None),
            P(("expert", "feat"), None),
            P(("expert", "feat"), None, None),
            P(("expert", "feat"), None, None),
            P(("expert", "feat"), None, None),
            P(None, "feat"),
            P(None, "feat"),
            P("feat", None),
            P(None, ("expert", "feat")),
            P(("expert", "feat")),
            P(("expert", "feat"), None),
            P(),
        ),
        out_specs=(P(None, ("expert", "feat")), P(("expert", "feat"), None)),
        check_vma=False,
    )
```

```python
import functools

import jax
import jax.numpy as jnp
from jax import lax
from jax.experimental import pallas as pl
from jax.experimental.pallas import tpu as pltpu
from jax.sharding import PartitionSpec as P

LANES = 128
MIB = 1024 * 1024
LOAD_MIB = 40
VMEM_SPEC = pl.BlockSpec(memory_space=pltpu.VMEM)
SMEM_SPEC = pl.BlockSpec(memory_space=pltpu.SMEM)
HBM_SPEC = pl.BlockSpec(memory_space=pltpu.HBM)


def swap(value, axis, r):
    return lax.ppermute(value, axis, [(i, i ^ r) for i in range(lax.axis_size(axis))])


def dot(a, b):
    return jnp.dot(a, b, preferred_element_type=jnp.float32)


def half(value):
    return value.astype(jnp.bfloat16)


def full(value):
    return value.astype(jnp.float32)


def silu(value):
    return value / (1.0 + jnp.exp(-value))


def bits_of(count):
    assert count & (count - 1) == 0
    return [1 << b for b in range(count.bit_length() - 1)]


def take(value, index, dim):
    return lax.dynamic_index_in_dim(value, index, dim, keepdims=False)


def call(body, operands, specs, outs, scratch, mib, cost):
    flops, moved = cost
    return pl.pallas_call(
        body,
        in_specs=specs,
        out_specs=[VMEM_SPEC] * len(outs),
        out_shape=[jax.ShapeDtypeStruct(shape, dtype) for shape, dtype in outs],
        scratch_shapes=scratch,
        compiler_params=pltpu.CompilerParams(vmem_limit_bytes=mib * MIB),
        cost_estimate=pl.CostEstimate(flops=flops, bytes_accessed=moved, transcendentals=0),
    )(*operands)


def start_all(pairs, sems):
    copies = [pltpu.make_async_copy(a, b, sems.at[i]) for i, (a, b) in enumerate(pairs)]
    for copy in copies:
        copy.start()
    return copies


def pack_kernel(ids, weights, out):
    top, own = ids.shape
    lane = lax.broadcasted_iota(jnp.int32, (top, LANES), 1)
    row = lax.broadcasted_iota(jnp.int32, (top, LANES), 0)
    high = half(weights[...])
    low = half(weights[...] - full(high))
    values = jnp.zeros((own, LANES), jnp.float32)
    for i, part in enumerate([half(full(ids[...])), high, low]):
        places = half(jnp.where(lane == row + i * top, 1.0, 0.0))
        values += lax.dot_general(
            part, places, (((0,), (0,)), ((), ())), preferred_element_type=jnp.float32
        )
    out[...] = half(values)


def run_pack(expert_ids, gate_weights):
    own, top = expert_ids.shape
    return call(
        pack_kernel,
        [expert_ids.T, gate_weights.T],
        [VMEM_SPEC] * 2,
        [((own, LANES), jnp.bfloat16)],
        [],
        2,
        (6 * own * top * LANES, 2 * own * LANES),
    )[0]


def load_kernel(*refs):
    count = (len(refs) - 1) // 2
    copies = start_all(list(zip(refs[:count], refs[count:-1])), refs[-1])
    for copy in copies:
        copy.wait()


def run_load(values):
    count = len(values)
    return call(
        load_kernel,
        values,
        [HBM_SPEC] * count,
        [(value.shape, value.dtype) for value in values],
        [pltpu.SemaphoreType.DMA((count,))],
        LOAD_MIB,
        (550 * sum(value.size for value in values), 4 * sum(value.size for value in values)),
    )


def shared_kernel(own, scalars, x, gate, up, down, extra, kept, sent, extra_out, sem):
    copy = pltpu.make_async_copy(extra, extra_out, sem)
    copy.start()
    hidden = half(silu(dot(x[...], gate[...])) * dot(x[...], up[...]))
    rows, width = x.shape
    for j in range(0, width, 256):
        cut = slice(j, j + 256)
        value = dot(hidden, down[:, cut]).reshape(rows // own // 2, 2, own, -1)
        low, high = [value[:, i].reshape(rows // 2, -1) for i in range(2)]
        kept[:, cut] = jnp.where(scalars[1] == 0, low, high)
        sent[:, cut] = jnp.where(scalars[1] == 0, high, low)
    copy.wait()


def run_shared(scalars, x, weights, extra, own):
    rows, width = x.shape
    return call(
        functools.partial(shared_kernel, own),
        [scalars, x, *weights, extra],
        [SMEM_SPEC] + [VMEM_SPEC] * 4 + [HBM_SPEC],
        [((rows // 2, width), jnp.float32)] * 2 + [(extra.shape, extra.dtype)],
        [pltpu.SemaphoreType.DMA],
        6,
        (6 * rows * weights[0].size, 6 * weights[0].size),
    )


def hidden_kernel(count, e, tile, *refs):
    pieces, (gate, up, out, rows) = refs[:count], refs[count:]
    size = pieces[0].shape[0]
    for i in range(count):
        rows[i * size : (i + 1) * size, :] = pieces[i][...]
    for j in range(0, out.shape[1], tile):
        cut = slice(j, j + tile)
        value = silu(dot(rows[...], gate[e, :, cut]))
        out[:, cut] = half(value * dot(rows[...], up[e, :, cut]))


def run_hidden(pieces, gate, up, e):
    count, (size, width) = len(pieces), pieces[0].shape
    units = gate.shape[2]
    return call(
        functools.partial(hidden_kernel, count, e, min(256, units)),
        [*pieces, gate, up],
        [VMEM_SPEC] * (count + 2),
        [((count * size, units), jnp.bfloat16)],
        [pltpu.VMEM((count * size, width), jnp.bfloat16)],
        8,
        (4 * count * size * width * units, 4 * width * units),
    )[0]


def down_kernel(top, e, tile, feats, pairs, kind, scalars, hidden, down, table, *refs):
    count = 1 if kind is None else 2 * kind[0]
    more, outs = refs[:-count], refs[-count:]
    size = hidden.shape[0] // pairs
    own = size // feats
    entries = []
    for p in range(pairs):
        for f in range(feats):
            start = (jnp.bitwise_xor(scalars[2], f) * pairs + p) * own
            entries.append(full(table[pl.ds(pl.multiple_of(start, own), own), :]))
    entries = jnp.concatenate(entries, axis=0)
    lane = lax.broadcasted_iota(jnp.int32, entries.shape, 1)
    expert = (scalars[0] * down.shape[0] + e).astype(jnp.float32)
    chosen = jnp.where((entries == expert) & (lane < top), 1.0, 0.0)
    chosen = pltpu.roll(chosen, top, 1) + pltpu.roll(chosen, 2 * top, 1)
    scale = jnp.sum(chosen * entries, axis=1, keepdims=True)
    for j in range(0, down.shape[2], tile):
        cut = slice(j, j + tile)
        value = dot(hidden[...], down[e, :, cut]) * scale
        if more:
            value += full(more[0][:, cut])
        if kind is None:
            outs[0][:, cut] = half(value)
            continue
        for p in range(pairs):
            block = value[p * size : (p + 1) * size]
            block = block.reshape(size // own // 2, 2, own, tile)
            low, high = block[:, 0].reshape(-1, tile), block[:, 1].reshape(-1, tile)
            outs[p][:, cut] = half(jnp.where(scalars[1] == 0, low, high))
            outs[pairs + p][:, cut] = half(jnp.where(scalars[1] == 0, high, low))


def run_down(hidden, down, e, scalars, table, top, feats, pairs, more=(), kind=None):
    rows, units = hidden.shape
    width = down.shape[2]
    tile = 256 if width % 256 == 0 else 128
    outs = [((rows, width), jnp.bfloat16)]
    if kind is not None:
        outs = [((rows // kind[0] // 2, width), jnp.bfloat16)] * (2 * kind[0])
    return call(
        functools.partial(down_kernel, top, e, tile, feats, pairs, kind),
        [scalars, hidden, down, table, *more],
        [SMEM_SPEC] + [VMEM_SPEC] * (3 + len(more)),
        outs,
        [],
        8,
        (2 * rows * units * width, 2 * units * width),
    )


def shards(
    tokens,
    expert_ids,
    gate_weights,
    expert_gate,
    expert_up,
    expert_down,
    shared_gate,
    shared_up,
    shared_down,
    encoder,
    encoder_bias,
    decoder,
    decoder_bias,
):
    own, top = expert_ids.shape
    width = tokens.shape[1]
    feats = lax.axis_size("feat")
    pairs = lax.axis_size("expert") // 2
    devices = 2 * pairs * feats
    local_experts = range(expert_gate.shape[0])
    me = lax.axis_index(("expert", "feat"))
    my_feat = lax.axis_index("feat")
    feat_bits = bits_of(feats)
    place = [(my_feat // bit) % 2 for bit in feat_bits]
    scalars = jnp.stack([me, place[0], my_feat])
    chunk_rows = pairs * feats // 2 * own

    table = run_pack(expert_ids, gate_weights)
    table = [table] + [swap(table, "expert", 2 * p) for p in range(1, pairs)]
    sent, table[1] = lax.optimization_barrier((tokens, table[1]))
    table = jnp.concatenate(table, axis=0)
    mine, table = lax.optimization_barrier((tokens, table))
    for bit in feat_bits:
        table = jnp.concatenate([table, swap(table, "feat", bit)], axis=0)
    table_far = swap(table, "expert", 1)

    near = [swap(sent, "expert", 2 * p) for p in range(1, pairs)]
    far = [swap(piece, "expert", 1) for piece in [sent] + near]
    mine, expert_gate, expert_up = run_load([mine, expert_gate, expert_up])
    near = [mine] + near

    hidden = [run_hidden(near, expert_gate, expert_up, e) for e in local_experts]
    hidden[0], *far = lax.optimization_barrier((hidden[0], *far))
    arrived = None
    for e in local_experts:
        more = [] if arrived is None else [arrived]
        arrived = run_down(hidden[e], expert_down, e, scalars, table, top, feats, pairs, more)[0]
    arrived = swap(arrived, "expert", 1)
    for e in local_experts:
        hidden = run_hidden(far, expert_gate, expert_up, e)
        if e < local_experts[-1]:
            more = [arrived]
            arrived = run_down(hidden, expert_down, e, scalars, table_far, top, feats, pairs, more)[0]
    blocks = run_down(
        hidden, expert_down, e, scalars, table_far, top, feats, pairs, [arrived], (pairs, own)
    )
    blocks = [blocks[:pairs], blocks[pairs:]]
    blocks = [
        [mine[0]] + [swap(mine[p], "expert", 2 * p) for p in range(1, pairs)] for mine in blocks
    ]
    scalars, blocks[0][-1] = lax.optimization_barrier((scalars, blocks[0][-1]))
    shared_out = run_shared(
        scalars, far[0], [shared_gate, shared_up, shared_down], encoder, own
    )
    encoder = shared_out[2]
    totals = [sum(full(part) for part in blocks[i] + [shared_out[i]]) for i in range(2)]

    total = totals[1] + full(swap(half(totals[0]), "feat", feat_bits[0]))
    total = total.reshape((2,) * (len(feat_bits) - 1) + (own, width))
    for i, bit in enumerate(feat_bits[1:-1]):
        dim = len(feat_bits) - 2 - i
        arrived = swap(half(take(total, 1 - place[i + 1], dim)), "feat", bit)
        total = take(total, place[i + 1], dim) + full(arrived)
    total = half(total)
    moe_out = half(full(total) + full(swap(total, "feat", feat_bits[-1])))
    for bit in feat_bits[-2:0:-1]:
        moe_out = jnp.stack([moe_out, swap(moe_out, "feat", bit)], axis=moe_out.ndim - 2)
    moe_out = moe_out.reshape(-1, width)
    other = swap(moe_out, "feat", feat_bits[0])
    parts = [moe_out] + [swap(moe_out, "expert", 2 * p) for p in range(1, pairs - 1)]
    mine, other = lax.optimization_barrier((moe_out, other))
    parts.append(swap(mine, "expert", 2 * (pairs - 1)))
    sides = [[other] + [swap(other, "expert", 2 * p) for p in range(1, pairs)], parts]

    def encode(x):
        return half(jax.nn.relu(dot(x, encoder) + encoder_bias[None, :]))

    features, blocks, zero = [None, None], [None, None], 0.0
    for chunk in (1, 0):
        near = jnp.stack(sides[chunk]).reshape(chunk_rows, width)
        far = swap(near, "expert", 1)
        features_near = encode(near)
        decoded = swap(half(dot(features_near, decoder)), "expert", 1)
        features_far = encode(far)
        total = half(dot(features_far, decoder) + full(decoded) + zero)
        total = total.reshape(pairs, feats // 2 * own, width)
        blocks[chunk] = [total[0]] + [swap(total[p], "expert", 2 * p) for p in range(1, pairs)]
        zero = 0.0 * full(blocks[chunk][1][0, 0])
        both = jnp.stack([features_far, features_near])
        features[chunk] = both.reshape(2, pairs, feats // 2, 1, own, -1)
    arrived = swap(half(sum(full(block) for block in blocks[1])), "feat", feat_bits[0])
    total = sum(full(block) for block in blocks[0])
    total = (total + full(arrived)).reshape((2,) * (len(feat_bits) - 1) + (own, width))
    for bit in feat_bits[1:-1]:
        dim = len(total.shape) - 3
        arrived = swap(half(lax.index_in_dim(total, 1, dim, False)), "feat", bit)
        total = lax.index_in_dim(total, 0, dim, False) + full(arrived)
    arrived = swap(half(take(total, 1 - place[-1], 0)), "feat", feat_bits[-1])
    reconstruction = take(total, place[-1], 0) + full(arrived) + decoder_bias[None, :]

    features = jnp.concatenate(features, axis=3).transpose(1, 0, 2, 3, 4, 5)
    features = features.reshape(devices, own, -1)
    relative = me - me % feats + my_feat % (feats // 2)
    blocks = [lax.dynamic_index_in_dim(features, i ^ relative, 0) for i in range(devices)]
    features = jnp.concatenate(blocks, axis=0).reshape(devices * own, -1)
    return (features, reconstruction)


def solution(mesh):
    return jax.shard_map(
        shards,
        mesh=mesh,
        in_specs=(
            P("expert", None),
            P(("expert", "feat"), None),
            P(("expert", "feat"), None),
            P(("expert", "feat"), None, None),
            P(("expert", "feat"), None, None),
            P(("expert", "feat"), None, None),
            P(None, "feat"),
            P(None, "feat"),
            P("feat", None),
            P(None, ("expert", "feat")),
            P(("expert", "feat")),
            P(("expert", "feat"), None),
            P(),
        ),
        out_specs=(P(None, ("expert", "feat")), P(("expert", "feat"), None)),
        check_vma=False,
    )
```

```python
import functools

import jax
import jax.numpy as jnp
from jax import lax
from jax.experimental import pallas as pl
from jax.experimental.pallas import tpu as pltpu
from jax.sharding import PartitionSpec as P

LANES = 128
MIB = 1024 * 1024
LOAD_MIB = 40
VMEM_SPEC = pl.BlockSpec(memory_space=pltpu.VMEM)
SMEM_SPEC = pl.BlockSpec(memory_space=pltpu.SMEM)
HBM_SPEC = pl.BlockSpec(memory_space=pltpu.HBM)


def swap(value, axis, r):
    return lax.ppermute(value, axis, [(i, i ^ r) for i in range(lax.axis_size(axis))])


def dot(a, b):
    return jnp.dot(a, b, preferred_element_type=jnp.float32)


def half(value):
    return value.astype(jnp.bfloat16)


def full(value):
    return value.astype(jnp.float32)


def silu(value):
    return value / (1.0 + jnp.exp(-value))


def bits_of(count):
    assert count & (count - 1) == 0
    return [1 << b for b in range(count.bit_length() - 1)]


def take(value, index, dim):
    return lax.dynamic_index_in_dim(value, index, dim, keepdims=False)


def call(body, operands, specs, outs, scratch, mib, cost):
    flops, moved = cost
    return pl.pallas_call(
        body,
        in_specs=specs,
        out_specs=[VMEM_SPEC] * len(outs),
        out_shape=[jax.ShapeDtypeStruct(shape, dtype) for shape, dtype in outs],
        scratch_shapes=scratch,
        compiler_params=pltpu.CompilerParams(vmem_limit_bytes=mib * MIB),
        cost_estimate=pl.CostEstimate(flops=flops, bytes_accessed=moved, transcendentals=0),
    )(*operands)


def start_all(pairs, sems):
    copies = [pltpu.make_async_copy(a, b, sems.at[i]) for i, (a, b) in enumerate(pairs)]
    for copy in copies:
        copy.start()
    return copies


def pack_kernel(ids, weights, out):
    top, own = ids.shape
    lane = lax.broadcasted_iota(jnp.int32, (top, LANES), 1)
    row = lax.broadcasted_iota(jnp.int32, (top, LANES), 0)
    high = half(weights[...])
    low = half(weights[...] - full(high))
    values = jnp.zeros((own, LANES), jnp.float32)
    for i, part in enumerate([half(full(ids[...])), high, low]):
        places = half(jnp.where(lane == row + i * top, 1.0, 0.0))
        values += lax.dot_general(
            part, places, (((0,), (0,)), ((), ())), preferred_element_type=jnp.float32
        )
    out[...] = half(values)


def run_pack(expert_ids, gate_weights):
    own, top = expert_ids.shape
    return call(
        pack_kernel,
        [expert_ids.T, gate_weights.T],
        [VMEM_SPEC] * 2,
        [((own, LANES), jnp.bfloat16)],
        [],
        2,
        (6 * own * top * LANES, 2 * own * LANES),
    )[0]


def load_kernel(*refs):
    count = (len(refs) - 1) // 2
    copies = start_all(list(zip(refs[:count], refs[count:-1])), refs[-1])
    for copy in copies:
        copy.wait()


def run_load(values):
    count = len(values)
    return call(
        load_kernel,
        values,
        [HBM_SPEC] * count,
        [(value.shape, value.dtype) for value in values],
        [pltpu.SemaphoreType.DMA((count,))],
        LOAD_MIB,
        (550 * sum(value.size for value in values), 4 * sum(value.size for value in values)),
    )


def shared_kernel(own, scalars, x, gate, up, down, kept, sent):
    hidden = half(silu(dot(x[...], gate[...])) * dot(x[...], up[...]))
    rows, width = x.shape
    for j in range(0, width, 256):
        cut = slice(j, j + 256)
        value = dot(hidden, down[:, cut]).reshape(rows // own // 2, 2, own, -1)
        low, high = [value[:, i].reshape(rows // 2, -1) for i in range(2)]
        kept[:, cut] = jnp.where(scalars[1] == 0, low, high)
        sent[:, cut] = jnp.where(scalars[1] == 0, high, low)


def run_shared(scalars, x, weights, own):
    rows, width = x.shape
    return call(
        functools.partial(shared_kernel, own),
        [scalars, x, *weights],
        [SMEM_SPEC] + [VMEM_SPEC] * 4,
        [((rows // 2, width), jnp.float32)] * 2,
        [],
        6,
        (6 * rows * weights[0].size, 6 * weights[0].size),
    )


def hidden_kernel(count, e, tile, *refs):
    pieces, (gate, up, out, rows) = refs[:count], refs[count:]
    size = pieces[0].shape[0]
    for i in range(count):
        rows[i * size : (i + 1) * size, :] = pieces[i][...]
    for j in range(0, out.shape[1], tile):
        cut = slice(j, j + tile)
        value = silu(dot(rows[...], gate[e, :, cut]))
        out[:, cut] = half(value * dot(rows[...], up[e, :, cut]))


def run_hidden(pieces, gate, up, e):
    count, (size, width) = len(pieces), pieces[0].shape
    units = gate.shape[2]
    return call(
        functools.partial(hidden_kernel, count, e, min(256, units)),
        [*pieces, gate, up],
        [VMEM_SPEC] * (count + 2),
        [((count * size, units), jnp.bfloat16)],
        [pltpu.VMEM((count * size, width), jnp.bfloat16)],
        8,
        (4 * count * size * width * units, 4 * width * units),
    )[0]


def down_kernel(top, e, tile, feats, pairs, chunk, scalars, hidden, down, table, *refs):
    count = 1 if chunk is None else pairs
    more, outs = refs[:-count], refs[-count:]
    own = hidden.shape[0] // pairs // feats
    if chunk is None:
        blocks = [(p, f) for p in range(pairs) for f in range(feats)]
    else:
        side = jnp.bitwise_xor(scalars[1], chunk)
        blocks = [(p, 2 * f + side) for p in range(pairs) for f in range(feats // 2)]

    def rows_of(ref):
        if chunk is None:
            return ref[...]
        starts = [pl.multiple_of((p * feats + f) * own, own) for p, f in blocks]
        return jnp.concatenate([ref[pl.ds(start, own), :] for start in starts], axis=0)

    entries = []
    for p, f in blocks:
        start = (jnp.bitwise_xor(scalars[2], f) * pairs + p) * own
        entries.append(full(table[pl.ds(pl.multiple_of(start, own), own), :]))
    entries = jnp.concatenate(entries, axis=0)
    lane = lax.broadcasted_iota(jnp.int32, entries.shape, 1)
    expert = (scalars[0] * down.shape[0] + e).astype(jnp.float32)
    chosen = jnp.where((entries == expert) & (lane < top), 1.0, 0.0)
    chosen = pltpu.roll(chosen, top, 1) + pltpu.roll(chosen, 2 * top, 1)
    scale = jnp.sum(chosen * entries, axis=1, keepdims=True)
    rows = rows_of(hidden)
    arrived = rows_of(more[0]) if more else None
    size = outs[0].shape[0]
    for j in range(0, down.shape[2], tile):
        cut = slice(j, j + tile)
        value = dot(rows, down[e, :, cut]) * scale
        if more:
            value += full(arrived[:, cut])
        for p, out in enumerate(outs):
            out[:, cut] = half(value[p * size : (p + 1) * size])


def run_down(hidden, down, e, scalars, table, top, feats, pairs, more=(), chunk=None):
    rows, units = hidden.shape
    width = down.shape[2]
    tile = 256 if width % 256 == 0 else 128
    outs = [((rows, width), jnp.bfloat16)]
    if chunk is not None:
        outs = [((rows // pairs // 2, width), jnp.bfloat16)] * pairs
    return call(
        functools.partial(down_kernel, top, e, tile, feats, pairs, chunk),
        [scalars, hidden, down, table, *more],
        [SMEM_SPEC] + [VMEM_SPEC] * (3 + len(more)),
        outs,
        [],
        8,
        (2 * rows * units * width, 2 * units * width),
    )


def shards(
    tokens,
    expert_ids,
    gate_weights,
    expert_gate,
    expert_up,
    expert_down,
    shared_gate,
    shared_up,
    shared_down,
    encoder,
    encoder_bias,
    decoder,
    decoder_bias,
):
    own, top = expert_ids.shape
    width = tokens.shape[1]
    feats = lax.axis_size("feat")
    pairs = lax.axis_size("expert") // 2
    devices = 2 * pairs * feats
    local_experts = range(expert_gate.shape[0])
    me = lax.axis_index(("expert", "feat"))
    my_feat = lax.axis_index("feat")
    feat_bits = bits_of(feats)
    place = [(my_feat // bit) % 2 for bit in feat_bits]
    scalars = jnp.stack([me, place[0], my_feat])
    chunk_rows = pairs * feats // 2 * own

    table = run_pack(expert_ids, gate_weights)
    table = [table] + [swap(table, "expert", 2 * p) for p in range(1, pairs)]
    sent, table[1] = lax.optimization_barrier((tokens, table[1]))
    table = jnp.concatenate(table, axis=0)
    mine, table = lax.optimization_barrier((tokens, table))
    for bit in feat_bits:
        table = jnp.concatenate([table, swap(table, "feat", bit)], axis=0)
    table_far = swap(table, "expert", 1)

    near = [swap(sent, "expert", 2 * p) for p in range(1, pairs)]
    far = [swap(piece, "expert", 1) for piece in [sent] + near]
    mine, expert_gate, expert_up = run_load([mine, expert_gate, expert_up])
    near = [mine] + near

    hidden = [run_hidden(near, expert_gate, expert_up, e) for e in local_experts]
    hidden[0], *far = lax.optimization_barrier((hidden[0], *far))
    arrived = None
    for e in local_experts:
        more = [] if arrived is None else [arrived]
        arrived = run_down(hidden[e], expert_down, e, scalars, table, top, feats, pairs, more)[0]
    arrived = swap(arrived, "expert", 1)
    for e in local_experts:
        hidden = run_hidden(far, expert_gate, expert_up, e)
        if e < local_experts[-1]:
            more = [arrived]
            arrived = run_down(hidden, expert_down, e, scalars, table_far, top, feats, pairs, more)[0]
    more = [arrived]
    blocks = [
        run_down(hidden, expert_down, e, scalars, table_far, top, feats, pairs, more, chunk)
        for chunk in range(2)
    ]
    blocks = [
        [mine[0]] + [swap(mine[p], "expert", 2 * p) for p in range(1, pairs)] for mine in blocks
    ]
    scalars, blocks[0][-1] = lax.optimization_barrier((scalars, blocks[0][-1]))
    shared_out = run_shared(scalars, far[0], [shared_gate, shared_up, shared_down], own)
    totals = [sum(full(part) for part in blocks[i] + [shared_out[i]]) for i in range(2)]

    total = totals[1] + full(swap(half(totals[0]), "feat", feat_bits[0]))
    total = total.reshape((2,) * (len(feat_bits) - 1) + (own, width))
    for i, bit in enumerate(feat_bits[1:-1]):
        dim = len(feat_bits) - 2 - i
        arrived = swap(half(take(total, 1 - place[i + 1], dim)), "feat", bit)
        total = take(total, place[i + 1], dim) + full(arrived)
    total = half(total)
    moe_out = half(full(total) + full(swap(total, "feat", feat_bits[-1])))
    for bit in feat_bits[-2:0:-1]:
        moe_out = jnp.stack([moe_out, swap(moe_out, "feat", bit)], axis=moe_out.ndim - 2)
    moe_out = moe_out.reshape(-1, width)
    other = swap(moe_out, "feat", feat_bits[0])
    parts = [moe_out] + [swap(moe_out, "expert", 2 * p) for p in range(1, pairs - 1)]
    mine, other = lax.optimization_barrier((moe_out, other))
    parts.append(swap(mine, "expert", 2 * (pairs - 1)))
    sides = [[other] + [swap(other, "expert", 2 * p) for p in range(1, pairs)], parts]

    def encode(x):
        return half(jax.nn.relu(dot(x, encoder) + encoder_bias[None, :]))

    features, blocks, zero = [None, None], [None, None], 0.0
    for chunk in (1, 0):
        near = jnp.stack(sides[chunk]).reshape(chunk_rows, width)
        far = swap(near, "expert", 1)
        features_near = encode(near)
        decoded = swap(half(dot(features_near, decoder)), "expert", 1)
        features_far = encode(far)
        total = half(dot(features_far, decoder) + full(decoded) + zero)
        total = total.reshape(pairs, feats // 2 * own, width)
        blocks[chunk] = [total[0]] + [swap(total[p], "expert", 2 * p) for p in range(1, pairs)]
        zero = 0.0 * full(blocks[chunk][1][:1])
        both = jnp.stack([features_far, features_near])
        features[chunk] = both.reshape(2, pairs, feats // 2, 1, own, -1)
    arrived = swap(half(sum(full(block) for block in blocks[1])), "feat", feat_bits[0])
    total = sum(full(block) for block in blocks[0])
    total = (total + full(arrived)).reshape((2,) * (len(feat_bits) - 1) + (own, width))
    for bit in feat_bits[1:-1]:
        dim = len(total.shape) - 3
        arrived = swap(half(lax.index_in_dim(total, 1, dim, False)), "feat", bit)
        total = lax.index_in_dim(total, 0, dim, False) + full(arrived)
    arrived = swap(half(take(total, 1 - place[-1], 0)), "feat", feat_bits[-1])
    reconstruction = take(total, place[-1], 0) + full(arrived) + decoder_bias[None, :]

    features = jnp.concatenate(features, axis=3).transpose(1, 0, 2, 3, 4, 5)
    features = features.reshape(devices, own, -1)
    relative = me - me % feats + my_feat % (feats // 2)
    blocks = [lax.dynamic_index_in_dim(features, i ^ relative, 0) for i in range(devices)]
    features = jnp.concatenate(blocks, axis=0).reshape(devices * own, -1)
    return (features, reconstruction)


def solution(mesh):
    return jax.shard_map(
        shards,
        mesh=mesh,
        in_specs=(
            P("expert", None),
            P(("expert", "feat"), None),
            P(("expert", "feat"), None),
            P(("expert", "feat"), None, None),
            P(("expert", "feat"), None, None),
            P(("expert", "feat"), None, None),
            P(None, "feat"),
            P(None, "feat"),
            P("feat", None),
            P(None, ("expert", "feat")),
            P(("expert", "feat")),
            P(("expert", "feat"), None),
            P(),
        ),
        out_specs=(P(None, ("expert", "feat")), P(("expert", "feat"), None)),
        check_vma=False,
    )
```

```python
import functools

import jax
import jax.numpy as jnp
from jax import lax
from jax.experimental import pallas as pl
from jax.experimental.pallas import tpu as pltpu
from jax.sharding import PartitionSpec as P

LANES = 128
MIB = 1024 * 1024
LOAD_MIB = 40
VMEM_SPEC = pl.BlockSpec(memory_space=pltpu.VMEM)
SMEM_SPEC = pl.BlockSpec(memory_space=pltpu.SMEM)
HBM_SPEC = pl.BlockSpec(memory_space=pltpu.HBM)


def swap(value, axis, r):
    return lax.ppermute(value, axis, [(i, i ^ r) for i in range(lax.axis_size(axis))])


def dot(a, b):
    return jnp.dot(a, b, preferred_element_type=jnp.float32)


def half(value):
    return value.astype(jnp.bfloat16)


def full(value):
    return value.astype(jnp.float32)


def silu(value):
    return value / (1.0 + jnp.exp(-value))


def bits_of(count):
    assert count & (count - 1) == 0
    return [1 << b for b in range(count.bit_length() - 1)]


def take(value, index, dim):
    return lax.dynamic_index_in_dim(value, index, dim, keepdims=False)


def call(body, operands, specs, outs, scratch, mib, cost):
    flops, moved = cost
    return pl.pallas_call(
        body,
        in_specs=specs,
        out_specs=[VMEM_SPEC] * len(outs),
        out_shape=[jax.ShapeDtypeStruct(shape, dtype) for shape, dtype in outs],
        scratch_shapes=scratch,
        compiler_params=pltpu.CompilerParams(vmem_limit_bytes=mib * MIB),
        cost_estimate=pl.CostEstimate(flops=flops, bytes_accessed=moved, transcendentals=0),
    )(*operands)


def start_all(pairs, sems):
    copies = [pltpu.make_async_copy(a, b, sems.at[i]) for i, (a, b) in enumerate(pairs)]
    for copy in copies:
        copy.start()
    return copies


def pack_kernel(both, out):
    top, own = both.shape[0] // 2, both.shape[1]
    ids, weights = both[:top], both[top:]
    lane = lax.broadcasted_iota(jnp.int32, (top, LANES), 1)
    row = lax.broadcasted_iota(jnp.int32, (top, LANES), 0)
    high = half(weights)
    low = half(weights - full(high))
    values = jnp.zeros((own, LANES), jnp.float32)
    for i, part in enumerate([half(ids), high, low]):
        places = half(jnp.where(lane == row + i * top, 1.0, 0.0))
        values += lax.dot_general(
            part, places, (((0,), (0,)), ((), ())), preferred_element_type=jnp.float32
        )
    out[...] = half(values)


def run_pack(expert_ids, gate_weights):
    own, top = expert_ids.shape
    ids = jnp.pad(expert_ids.T, ((0, top), (0, 0)))
    weights = jnp.pad(gate_weights.T, ((top, 0), (0, 0)))
    return call(
        pack_kernel,
        [full(ids) + weights],
        [VMEM_SPEC],
        [((own, LANES), jnp.bfloat16)],
        [],
        2,
        (6 * own * top * LANES, 2 * own * LANES),
    )[0]


def load_kernel(*refs):
    count = (len(refs) - 1) // 2
    copies = start_all(list(zip(refs[:count], refs[count:-1])), refs[-1])
    for copy in copies:
        copy.wait()


def run_load(values):
    count = len(values)
    return call(
        load_kernel,
        values,
        [HBM_SPEC] * count,
        [(value.shape, value.dtype) for value in values],
        [pltpu.SemaphoreType.DMA((count,))],
        LOAD_MIB,
        (550 * sum(value.size for value in values), 4 * sum(value.size for value in values)),
    )


def shared_kernel(own, scalars, x, gate, up, down, kept, sent):
    hidden = half(silu(dot(x[...], gate[...])) * dot(x[...], up[...]))
    rows, width = x.shape
    for j in range(0, width, 256):
        cut = slice(j, j + 256)
        value = dot(hidden, down[:, cut]).reshape(rows // own // 2, 2, own, -1)
        low, high = [value[:, i].reshape(rows // 2, -1) for i in range(2)]
        kept[:, cut] = jnp.where(scalars[1] == 0, low, high)
        sent[:, cut] = jnp.where(scalars[1] == 0, high, low)


def run_shared(scalars, x, weights, own):
    rows, width = x.shape
    return call(
        functools.partial(shared_kernel, own),
        [scalars, x, *weights],
        [SMEM_SPEC] + [VMEM_SPEC] * 4,
        [((rows // 2, width), jnp.float32)] * 2,
        [],
        6,
        (6 * rows * weights[0].size, 6 * weights[0].size),
    )


def hidden_kernel(count, e, tile, *refs):
    pieces, (gate, up, out, rows) = refs[:count], refs[count:]
    size = pieces[0].shape[0]
    for i in range(count):
        rows[i * size : (i + 1) * size, :] = pieces[i][...]
    for j in range(0, out.shape[1], tile):
        cut = slice(j, j + tile)
        value = silu(dot(rows[...], gate[e, :, cut]))
        out[:, cut] = half(value * dot(rows[...], up[e, :, cut]))


def run_hidden(pieces, gate, up, e):
    count, (size, width) = len(pieces), pieces[0].shape
    units = gate.shape[2]
    return call(
        functools.partial(hidden_kernel, count, e, min(256, units)),
        [*pieces, gate, up],
        [VMEM_SPEC] * (count + 2),
        [((count * size, units), jnp.bfloat16)],
        [pltpu.VMEM((count * size, width), jnp.bfloat16)],
        8,
        (4 * count * size * width * units, 4 * width * units),
    )[0]


def down_kernel(top, e, tile, feats, pairs, chunk, scalars, hidden, down, table, *refs):
    count = 1 if chunk is None else pairs
    more, outs = refs[:-count], refs[-count:]
    own = hidden.shape[0] // pairs // feats
    if chunk is None:
        blocks = [(p, f) for p in range(pairs) for f in range(feats)]
    else:
        side = jnp.bitwise_xor(scalars[1], chunk)
        blocks = [(p, 2 * f + side) for p in range(pairs) for f in range(feats // 2)]

    def rows_of(ref):
        if chunk is None:
            return ref[...]
        starts = [pl.multiple_of((p * feats + f) * own, own) for p, f in blocks]
        return jnp.concatenate([ref[pl.ds(start, own), :] for start in starts], axis=0)

    entries = []
    for p, f in blocks:
        start = (jnp.bitwise_xor(scalars[2], f) * pairs + p) * own
        entries.append(full(table[pl.ds(pl.multiple_of(start, own), own), :]))
    entries = jnp.concatenate(entries, axis=0)
    lane = lax.broadcasted_iota(jnp.int32, entries.shape, 1)
    expert = (scalars[0] * down.shape[0] + e).astype(jnp.float32)
    chosen = jnp.where((entries == expert) & (lane < top), 1.0, 0.0)
    chosen = pltpu.roll(chosen, top, 1) + pltpu.roll(chosen, 2 * top, 1)
    scale = jnp.sum(chosen * entries, axis=1, keepdims=True)
    rows = rows_of(hidden)
    arrived = rows_of(more[0]) if more else None
    size = outs[0].shape[0]
    for j in range(0, down.shape[2], tile):
        cut = slice(j, j + tile)
        value = dot(rows, down[e, :, cut]) * scale
        if more:
            value += full(arrived[:, cut])
        for p, out in enumerate(outs):
            out[:, cut] = half(value[p * size : (p + 1) * size])


def run_down(hidden, down, e, scalars, table, top, feats, pairs, more=(), chunk=None):
    rows, units = hidden.shape
    width = down.shape[2]
    tile = 256 if width % 256 == 0 else 128
    outs = [((rows, width), jnp.bfloat16)]
    if chunk is not None:
        outs = [((rows // pairs // 2, width), jnp.bfloat16)] * pairs
    return call(
        functools.partial(down_kernel, top, e, tile, feats, pairs, chunk),
        [scalars, hidden, down, table, *more],
        [SMEM_SPEC] + [VMEM_SPEC] * (3 + len(more)),
        outs,
        [],
        8,
        (2 * rows * units * width, 2 * units * width),
    )


def shards(
    tokens,
    expert_ids,
    gate_weights,
    expert_gate,
    expert_up,
    expert_down,
    shared_gate,
    shared_up,
    shared_down,
    encoder,
    encoder_bias,
    decoder,
    decoder_bias,
):
    own, top = expert_ids.shape
    width = tokens.shape[1]
    feats = lax.axis_size("feat")
    pairs = lax.axis_size("expert") // 2
    devices = 2 * pairs * feats
    local_experts = range(expert_gate.shape[0])
    me = lax.axis_index(("expert", "feat"))
    my_feat = lax.axis_index("feat")
    feat_bits = bits_of(feats)
    place = [(my_feat // bit) % 2 for bit in feat_bits]
    scalars = jnp.stack([me, place[0], my_feat])
    chunk_rows = pairs * feats // 2 * own

    table = run_pack(expert_ids, gate_weights)
    table = [table] + [swap(table, "expert", 2 * p) for p in range(1, pairs)]
    sent, table[1] = lax.optimization_barrier((tokens, table[1]))
    table = jnp.concatenate(table, axis=0)
    mine, table = lax.optimization_barrier((tokens, table))
    for bit in feat_bits:
        table = jnp.concatenate([table, swap(table, "feat", bit)], axis=0)
    table_far = swap(table, "expert", 1)

    near = [swap(sent, "expert", 2 * p) for p in range(1, pairs)]
    far = [swap(piece, "expert", 1) for piece in [sent] + near]
    mine, expert_gate, expert_up = run_load([mine, expert_gate, expert_up])
    near = [mine] + near

    hidden = [run_hidden(near, expert_gate, expert_up, e) for e in local_experts]
    hidden[0], *far = lax.optimization_barrier((hidden[0], *far))
    arrived = None
    for e in local_experts:
        more = [] if arrived is None else [arrived]
        arrived = run_down(hidden[e], expert_down, e, scalars, table, top, feats, pairs, more)[0]
    arrived = swap(arrived, "expert", 1)
    for e in local_experts:
        hidden = run_hidden(far, expert_gate, expert_up, e)
        if e < local_experts[-1]:
            more = [arrived]
            arrived = run_down(hidden, expert_down, e, scalars, table_far, top, feats, pairs, more)[0]
    more = [arrived]
    blocks = [
        run_down(hidden, expert_down, e, scalars, table_far, top, feats, pairs, more, chunk)
        for chunk in range(2)
    ]
    blocks = [
        [mine[0]] + [swap(mine[p], "expert", 2 * p) for p in range(1, pairs)] for mine in blocks
    ]
    scalars, blocks[0][-1] = lax.optimization_barrier((scalars, blocks[0][-1]))
    shared_out = run_shared(scalars, far[0], [shared_gate, shared_up, shared_down], own)
    totals = [sum(full(part) for part in blocks[i] + [shared_out[i]]) for i in range(2)]

    total = totals[1] + full(swap(half(totals[0]), "feat", feat_bits[0]))
    total = total.reshape((2,) * (len(feat_bits) - 1) + (own, width))
    for i, bit in enumerate(feat_bits[1:-1]):
        dim = len(feat_bits) - 2 - i
        arrived = swap(half(take(total, 1 - place[i + 1], dim)), "feat", bit)
        total = take(total, place[i + 1], dim) + full(arrived)
    total = half(total)
    moe_out = half(full(total) + full(swap(total, "feat", feat_bits[-1])))
    for bit in feat_bits[-2:0:-1]:
        moe_out = jnp.stack([moe_out, swap(moe_out, "feat", bit)], axis=moe_out.ndim - 2)
    moe_out = moe_out.reshape(-1, width)
    other = swap(moe_out, "feat", feat_bits[0])
    parts = [moe_out] + [swap(moe_out, "expert", 2 * p) for p in range(1, pairs - 1)]
    mine, other = lax.optimization_barrier((moe_out, other))
    parts.append(swap(mine, "expert", 2 * (pairs - 1)))
    sides = [[other] + [swap(other, "expert", 2 * p) for p in range(1, pairs)], parts]

    def encode(x):
        return half(jax.nn.relu(dot(x, encoder) + encoder_bias[None, :]))

    features, blocks, zero = [None, None], [None, None], 0.0
    for chunk in (1, 0):
        near = jnp.stack(sides[chunk]).reshape(chunk_rows, width)
        far = swap(near, "expert", 1)
        features_near = encode(near)
        decoded = swap(half(dot(features_near, decoder)), "expert", 1)
        features_far = encode(far)
        total = half(dot(features_far, decoder) + full(decoded) + zero)
        total = total.reshape(pairs, feats // 2 * own, width)
        blocks[chunk] = [total[0]] + [swap(total[p], "expert", 2 * p) for p in range(1, pairs)]
        zero = 0.0 * full(blocks[chunk][1][:1])
        both = jnp.stack([features_far, features_near])
        features[chunk] = both.reshape(2, pairs, feats // 2, 1, own, -1)
    arrived = swap(half(sum(full(block) for block in blocks[1])), "feat", feat_bits[0])
    total = sum(full(block) for block in blocks[0])
    total = (total + full(arrived)).reshape((2,) * (len(feat_bits) - 1) + (own, width))
    for bit in feat_bits[1:-1]:
        dim = len(total.shape) - 3
        arrived = swap(half(lax.index_in_dim(total, 1, dim, False)), "feat", bit)
        total = lax.index_in_dim(total, 0, dim, False) + full(arrived)
    arrived = swap(half(take(total, 1 - place[-1], 0)), "feat", feat_bits[-1])
    reconstruction = take(total, place[-1], 0) + full(arrived) + decoder_bias[None, :]

    features = jnp.concatenate(features, axis=3).transpose(1, 0, 2, 3, 4, 5)
    features = features.reshape(devices, own, -1)
    relative = me - me % feats + my_feat % (feats // 2)
    blocks = [lax.dynamic_index_in_dim(features, i ^ relative, 0) for i in range(devices)]
    features = jnp.concatenate(blocks, axis=0).reshape(devices * own, -1)
    return (features, reconstruction)


def solution(mesh):
    return jax.shard_map(
        shards,
        mesh=mesh,
        in_specs=(
            P("expert", None),
            P(("expert", "feat"), None),
            P(("expert", "feat"), None),
            P(("expert", "feat"), None, None),
            P(("expert", "feat"), None, None),
            P(("expert", "feat"), None, None),
            P(None, "feat"),
            P(None, "feat"),
            P("feat", None),
            P(None, ("expert", "feat")),
            P(("expert", "feat")),
            P(("expert", "feat"), None),
            P(),
        ),
        out_specs=(P(None, ("expert", "feat")), P(("expert", "feat"), None)),
        check_vma=False,
    )
```

```python
import functools

import jax
import jax.numpy as jnp
from jax import lax
from jax.experimental import pallas as pl
from jax.experimental.pallas import tpu as pltpu
from jax.sharding import PartitionSpec as P

LANES = 128
MIB = 1024 * 1024
LOAD_MIB = 40
VMEM_SPEC = pl.BlockSpec(memory_space=pltpu.VMEM)
SMEM_SPEC = pl.BlockSpec(memory_space=pltpu.SMEM)
HBM_SPEC = pl.BlockSpec(memory_space=pltpu.HBM)


def swap(value, axis, r):
    return lax.ppermute(value, axis, [(i, i ^ r) for i in range(lax.axis_size(axis))])


def dot(a, b):
    return jnp.dot(a, b, preferred_element_type=jnp.float32)


def half(value):
    return value.astype(jnp.bfloat16)


def full(value):
    return value.astype(jnp.float32)


def silu(value):
    return value / (1.0 + jnp.exp(-value))


def bits_of(count):
    assert count & (count - 1) == 0
    return [1 << b for b in range(count.bit_length() - 1)]


def take(value, index, dim):
    return lax.dynamic_index_in_dim(value, index, dim, keepdims=False)


def call(body, operands, specs, outs, scratch, mib, cost):
    flops, moved = cost
    return pl.pallas_call(
        body,
        in_specs=specs,
        out_specs=[VMEM_SPEC] * len(outs),
        out_shape=[jax.ShapeDtypeStruct(shape, dtype) for shape, dtype in outs],
        scratch_shapes=scratch,
        compiler_params=pltpu.CompilerParams(vmem_limit_bytes=mib * MIB),
        cost_estimate=pl.CostEstimate(flops=flops, bytes_accessed=moved, transcendentals=0),
    )(*operands)


def start_all(pairs, sems):
    copies = [pltpu.make_async_copy(a, b, sems.at[i]) for i, (a, b) in enumerate(pairs)]
    for copy in copies:
        copy.start()
    return copies


def pack_kernel(both, out):
    top, own = both.shape[0] // 2, both.shape[1]
    ids, weights = both[:top], both[top:]
    lane = lax.broadcasted_iota(jnp.int32, (top, LANES), 1)
    row = lax.broadcasted_iota(jnp.int32, (top, LANES), 0)
    high = half(weights)
    low = half(weights - full(high))
    values = jnp.zeros((own, LANES), jnp.float32)
    for i, part in enumerate([half(ids), high, low]):
        places = half(jnp.where(lane == row + i * top, 1.0, 0.0))
        values += lax.dot_general(
            part, places, (((0,), (0,)), ((), ())), preferred_element_type=jnp.float32
        )
    out[...] = half(values)


def run_pack(expert_ids, gate_weights):
    own, top = expert_ids.shape
    ids = jnp.pad(expert_ids.T, ((0, top), (0, 0)))
    weights = jnp.pad(gate_weights.T, ((top, 0), (0, 0)))
    return call(
        pack_kernel,
        [full(ids) + weights],
        [VMEM_SPEC],
        [((own, LANES), jnp.bfloat16)],
        [],
        2,
        (6 * own * top * LANES, 2 * own * LANES),
    )[0]


def load_kernel(*refs):
    count = (len(refs) - 1) // 2
    copies = start_all(list(zip(refs[:count], refs[count:-1])), refs[-1])
    for copy in copies:
        copy.wait()


def run_load(values):
    count = len(values)
    return call(
        load_kernel,
        values,
        [HBM_SPEC] * count,
        [(value.shape, value.dtype) for value in values],
        [pltpu.SemaphoreType.DMA((count,))],
        LOAD_MIB,
        (550 * sum(value.size for value in values), 4 * sum(value.size for value in values)),
    )


def shared_kernel(own, scalars, x, gate, up, down, kept, sent):
    hidden = half(silu(dot(x[...], gate[...])) * dot(x[...], up[...]))
    rows, width = x.shape
    for j in range(0, width, 256):
        cut = slice(j, j + 256)
        value = dot(hidden, down[:, cut]).reshape(rows // own // 2, 2, own, -1)
        low, high = [value[:, i].reshape(rows // 2, -1) for i in range(2)]
        kept[:, cut] = jnp.where(scalars[1] == 0, low, high)
        sent[:, cut] = jnp.where(scalars[1] == 0, high, low)


def run_shared(scalars, x, weights, own):
    rows, width = x.shape
    return call(
        functools.partial(shared_kernel, own),
        [scalars, x, *weights],
        [SMEM_SPEC] + [VMEM_SPEC] * 4,
        [((rows // 2, width), jnp.float32)] * 2,
        [],
        6,
        (6 * rows * weights[0].size, 6 * weights[0].size),
    )


def hidden_kernel(count, e, tile, *refs):
    pieces, (gate, up, out, rows) = refs[:count], refs[count:]
    size = pieces[0].shape[0]
    for i in range(count):
        rows[i * size : (i + 1) * size, :] = pieces[i][...]
    for j in range(0, out.shape[1], tile):
        cut = slice(j, j + tile)
        value = silu(dot(rows[...], gate[e, :, cut]))
        out[:, cut] = half(value * dot(rows[...], up[e, :, cut]))


def run_hidden(pieces, gate, up, e):
    count, (size, width) = len(pieces), pieces[0].shape
    units = gate.shape[2]
    return call(
        functools.partial(hidden_kernel, count, e, min(512, units)),
        [*pieces, gate, up],
        [VMEM_SPEC] * (count + 2),
        [((count * size, units), jnp.bfloat16)],
        [pltpu.VMEM((count * size, width), jnp.bfloat16)],
        8,
        (4 * count * size * width * units, 4 * width * units),
    )[0]


def down_kernel(top, e, tile, feats, pairs, chunk, scalars, hidden, down, table, *refs):
    count = 1 if chunk is None else pairs
    more, outs = refs[:-count], refs[-count:]
    own = hidden.shape[0] // pairs // feats
    if chunk is None:
        blocks = [(p, f) for p in range(pairs) for f in range(feats)]
    else:
        side = jnp.bitwise_xor(scalars[1], chunk)
        blocks = [(p, 2 * f + side) for p in range(pairs) for f in range(feats // 2)]

    def rows_of(ref):
        if chunk is None:
            return ref[...]
        starts = [pl.multiple_of((p * feats + f) * own, own) for p, f in blocks]
        return jnp.concatenate([ref[pl.ds(start, own), :] for start in starts], axis=0)

    entries = []
    for p, f in blocks:
        start = (jnp.bitwise_xor(scalars[2], f) * pairs + p) * own
        entries.append(full(table[pl.ds(pl.multiple_of(start, own), own), :]))
    entries = jnp.concatenate(entries, axis=0)
    lane = lax.broadcasted_iota(jnp.int32, entries.shape, 1)
    expert = (scalars[0] * down.shape[0] + e).astype(jnp.float32)
    chosen = jnp.where((entries == expert) & (lane < top), 1.0, 0.0)
    chosen = pltpu.roll(chosen, top, 1) + pltpu.roll(chosen, 2 * top, 1)
    scale = jnp.sum(chosen * entries, axis=1, keepdims=True)
    rows = rows_of(hidden)
    arrived = rows_of(more[0]) if more else None
    size = outs[0].shape[0]
    for j in range(0, down.shape[2], tile):
        cut = slice(j, j + tile)
        value = dot(rows, down[e, :, cut]) * scale
        if more:
            value += full(arrived[:, cut])
        for p, out in enumerate(outs):
            out[:, cut] = half(value[p * size : (p + 1) * size])


def run_down(hidden, down, e, scalars, table, top, feats, pairs, more=(), chunk=None):
    rows, units = hidden.shape
    width = down.shape[2]
    tile = max(t for t in range(128, 769, 128) if width % t == 0)
    outs = [((rows, width), jnp.bfloat16)]
    if chunk is not None:
        outs = [((rows // pairs // 2, width), jnp.bfloat16)] * pairs
    return call(
        functools.partial(down_kernel, top, e, tile, feats, pairs, chunk),
        [scalars, hidden, down, table, *more],
        [SMEM_SPEC] + [VMEM_SPEC] * (3 + len(more)),
        outs,
        [],
        8,
        (2 * rows * units * width, 2 * units * width),
    )


def shards(
    tokens,
    expert_ids,
    gate_weights,
    expert_gate,
    expert_up,
    expert_down,
    shared_gate,
    shared_up,
    shared_down,
    encoder,
    encoder_bias,
    decoder,
    decoder_bias,
):
    own, top = expert_ids.shape
    width = tokens.shape[1]
    feats = lax.axis_size("feat")
    pairs = lax.axis_size("expert") // 2
    devices = 2 * pairs * feats
    local_experts = range(expert_gate.shape[0])
    me = lax.axis_index(("expert", "feat"))
    my_feat = lax.axis_index("feat")
    feat_bits = bits_of(feats)
    place = [(my_feat // bit) % 2 for bit in feat_bits]
    scalars = jnp.stack([me, place[0], my_feat])
    chunk_rows = pairs * feats // 2 * own

    table = run_pack(expert_ids, gate_weights)
    table = [table] + [swap(table, "expert", 2 * p) for p in range(1, pairs)]
    sent, table[1] = lax.optimization_barrier((tokens, table[1]))
    table = jnp.concatenate(table, axis=0)
    mine, table = lax.optimization_barrier((tokens, table))
    for bit in feat_bits:
        table = jnp.concatenate([table, swap(table, "feat", bit)], axis=0)
    table_far = swap(table, "expert", 1)

    near = [swap(sent, "expert", 2 * p) for p in range(1, pairs)]
    far = [swap(piece, "expert", 1) for piece in [sent] + near]
    mine, expert_gate, expert_up = run_load([mine, expert_gate, expert_up])
    near = [mine] + near

    hidden = [run_hidden(near, expert_gate, expert_up, e) for e in local_experts]
    hidden[0], *far = lax.optimization_barrier((hidden[0], *far))
    arrived = None
    for e in local_experts:
        more = [] if arrived is None else [arrived]
        arrived = run_down(hidden[e], expert_down, e, scalars, table, top, feats, pairs, more)[0]
    arrived = swap(arrived, "expert", 1)
    for e in local_experts:
        hidden = run_hidden(far, expert_gate, expert_up, e)
        if e < local_experts[-1]:
            more = [arrived]
            arrived = run_down(hidden, expert_down, e, scalars, table_far, top, feats, pairs, more)[0]
    more = [arrived]
    blocks = [
        run_down(hidden, expert_down, e, scalars, table_far, top, feats, pairs, more, chunk)
        for chunk in range(2)
    ]
    blocks = [
        [mine[0]] + [swap(mine[p], "expert", 2 * p) for p in range(1, pairs)] for mine in blocks
    ]
    scalars, blocks[0][-1] = lax.optimization_barrier((scalars, blocks[0][-1]))
    shared_out = run_shared(scalars, far[0], [shared_gate, shared_up, shared_down], own)
    totals = [sum(full(part) for part in blocks[i] + [shared_out[i]]) for i in range(2)]

    total = totals[1] + full(swap(half(totals[0]), "feat", feat_bits[0]))
    total = total.reshape((2,) * (len(feat_bits) - 1) + (own, width))
    for i, bit in enumerate(feat_bits[1:-1]):
        dim = len(feat_bits) - 2 - i
        arrived = swap(half(take(total, 1 - place[i + 1], dim)), "feat", bit)
        total = take(total, place[i + 1], dim) + full(arrived)
    total = half(total)
    moe_out = half(full(total) + full(swap(total, "feat", feat_bits[-1])))
    for bit in feat_bits[-2:0:-1]:
        moe_out = jnp.stack([moe_out, swap(moe_out, "feat", bit)], axis=moe_out.ndim - 2)
    moe_out = moe_out.reshape(-1, width)
    other = swap(moe_out, "feat", feat_bits[0])
    parts = [moe_out] + [swap(moe_out, "expert", 2 * p) for p in range(1, pairs - 1)]
    mine, other = lax.optimization_barrier((moe_out, other))
    parts.append(swap(mine, "expert", 2 * (pairs - 1)))
    sides = [[other] + [swap(other, "expert", 2 * p) for p in range(1, pairs)], parts]

    def encode(x):
        return half(jax.nn.relu(dot(x, encoder) + encoder_bias[None, :]))

    features, blocks, zero = [None, None], [None, None], 0.0
    for chunk in (1, 0):
        near = jnp.stack(sides[chunk]).reshape(chunk_rows, width)
        far = swap(near, "expert", 1)
        features_near = encode(near)
        decoded = swap(half(dot(features_near, decoder)), "expert", 1)
        features_far = encode(far)
        total = half(dot(features_far, decoder) + full(decoded) + zero)
        total = total.reshape(pairs, feats // 2 * own, width)
        blocks[chunk] = [total[0]] + [swap(total[p], "expert", 2 * p) for p in range(1, pairs)]
        zero = 0.0 * full(blocks[chunk][1][:1])
        both = jnp.stack([features_far, features_near])
        features[chunk] = both.reshape(2, pairs, feats // 2, 1, own, -1)
    arrived = swap(half(sum(full(block) for block in blocks[1])), "feat", feat_bits[0])
    total = sum(full(block) for block in blocks[0])
    total = (total + full(arrived)).reshape((2,) * (len(feat_bits) - 1) + (own, width))
    for bit in feat_bits[1:-1]:
        dim = len(total.shape) - 3
        arrived = swap(half(lax.index_in_dim(total, 1, dim, False)), "feat", bit)
        total = lax.index_in_dim(total, 0, dim, False) + full(arrived)
    arrived = swap(half(take(total, 1 - place[-1], 0)), "feat", feat_bits[-1])
    reconstruction = take(total, place[-1], 0) + full(arrived) + decoder_bias[None, :]

    features = jnp.concatenate(features, axis=3).transpose(1, 0, 2, 3, 4, 5)
    features = features.reshape(devices, own, -1)
    relative = me - me % feats + my_feat % (feats // 2)
    blocks = [lax.dynamic_index_in_dim(features, i ^ relative, 0) for i in range(devices)]
    features = jnp.concatenate(blocks, axis=0).reshape(devices * own, -1)
    return (features, reconstruction)


def solution(mesh):
    return jax.shard_map(
        shards,
        mesh=mesh,
        in_specs=(
            P("expert", None),
            P(("expert", "feat"), None),
            P(("expert", "feat"), None),
            P(("expert", "feat"), None, None),
            P(("expert", "feat"), None, None),
            P(("expert", "feat"), None, None),
            P(None, "feat"),
            P(None, "feat"),
            P("feat", None),
            P(None, ("expert", "feat")),
            P(("expert", "feat")),
            P(("expert", "feat"), None),
            P(),
        ),
        out_specs=(P(None, ("expert", "feat")), P(("expert", "feat"), None)),
        check_vma=False,
    )
```

```python
import functools

import jax
import jax.numpy as jnp
from jax import lax
from jax.experimental import pallas as pl
from jax.experimental.pallas import tpu as pltpu
from jax.sharding import PartitionSpec as P

LANES = 128
MIB = 1024 * 1024
LOAD_MIB = 40
VMEM_SPEC = pl.BlockSpec(memory_space=pltpu.VMEM)
SMEM_SPEC = pl.BlockSpec(memory_space=pltpu.SMEM)
HBM_SPEC = pl.BlockSpec(memory_space=pltpu.HBM)


def swap(value, axis, r):
    return lax.ppermute(value, axis, [(i, i ^ r) for i in range(lax.axis_size(axis))])


def dot(a, b):
    return jnp.dot(a, b, preferred_element_type=jnp.float32)


def half(value):
    return value.astype(jnp.bfloat16)


def full(value):
    return value.astype(jnp.float32)


def silu(value):
    return value / (1.0 + jnp.exp(-value))


def bits_of(count):
    assert count & (count - 1) == 0
    return [1 << b for b in range(count.bit_length() - 1)]


def take(value, index, dim):
    return lax.dynamic_index_in_dim(value, index, dim, keepdims=False)


def call(body, operands, specs, outs, scratch, mib, cost):
    flops, moved = cost
    return pl.pallas_call(
        body,
        in_specs=specs,
        out_specs=[VMEM_SPEC] * len(outs),
        out_shape=[jax.ShapeDtypeStruct(shape, dtype) for shape, dtype in outs],
        scratch_shapes=scratch,
        compiler_params=pltpu.CompilerParams(vmem_limit_bytes=mib * MIB),
        cost_estimate=pl.CostEstimate(flops=flops, bytes_accessed=moved, transcendentals=0),
    )(*operands)


def start_all(pairs, sems):
    copies = [pltpu.make_async_copy(a, b, sems.at[i]) for i, (a, b) in enumerate(pairs)]
    for copy in copies:
        copy.start()
    return copies


def pack_kernel(both, out):
    top, own = both.shape[0] // 2, both.shape[1]
    ids, weights = both[:top], both[top:]
    lane = lax.broadcasted_iota(jnp.int32, (top, LANES), 1)
    row = lax.broadcasted_iota(jnp.int32, (top, LANES), 0)
    high = half(weights)
    low = half(weights - full(high))
    values = jnp.zeros((own, LANES), jnp.float32)
    for i, part in enumerate([half(ids), high, low]):
        places = half(jnp.where(lane == row + i * top, 1.0, 0.0))
        values += lax.dot_general(
            part, places, (((0,), (0,)), ((), ())), preferred_element_type=jnp.float32
        )
    out[...] = half(values)


def run_pack(expert_ids, gate_weights):
    own, top = expert_ids.shape
    ids = jnp.pad(expert_ids.T, ((0, top), (0, 0)))
    weights = jnp.pad(gate_weights.T, ((top, 0), (0, 0)))
    return call(
        pack_kernel,
        [full(ids) + weights],
        [VMEM_SPEC],
        [((own, LANES), jnp.bfloat16)],
        [],
        2,
        (6 * own * top * LANES, 2 * own * LANES),
    )[0]


def load_kernel(*refs):
    count = (len(refs) - 1) // 2
    copies = start_all(list(zip(refs[:count], refs[count:-1])), refs[-1])
    for copy in copies:
        copy.wait()


def run_load(values):
    count = len(values)
    return call(
        load_kernel,
        values,
        [HBM_SPEC] * count,
        [(value.shape, value.dtype) for value in values],
        [pltpu.SemaphoreType.DMA((count,))],
        LOAD_MIB,
        (550 * sum(value.size for value in values), 4 * sum(value.size for value in values)),
    )


def shared_kernel(own, scalars, x, gate, up, down, kept, sent):
    hidden = half(silu(dot(x[...], gate[...])) * dot(x[...], up[...]))
    rows, width = x.shape
    for j in range(0, width, 256):
        cut = slice(j, j + 256)
        value = dot(hidden, down[:, cut]).reshape(rows // own // 2, 2, own, -1)
        low, high = [value[:, i].reshape(rows // 2, -1) for i in range(2)]
        kept[:, cut] = jnp.where(scalars[1] == 0, low, high)
        sent[:, cut] = jnp.where(scalars[1] == 0, high, low)


def run_shared(scalars, x, weights, own):
    rows, width = x.shape
    return call(
        functools.partial(shared_kernel, own),
        [scalars, x, *weights],
        [SMEM_SPEC] + [VMEM_SPEC] * 4,
        [((rows // 2, width), jnp.float32)] * 2,
        [],
        6,
        (6 * rows * weights[0].size, 6 * weights[0].size),
    )


def hidden_kernel(count, e, tile, *refs):
    pieces, (gate, up, out, rows) = refs[:count], refs[count:]
    size = pieces[0].shape[0]
    for i in range(count):
        rows[i * size : (i + 1) * size, :] = pieces[i][...]
    for j in range(0, out.shape[1], tile):
        cut = slice(j, j + tile)
        value = silu(dot(rows[...], gate[e, :, cut]))
        out[:, cut] = half(value * dot(rows[...], up[e, :, cut]))


def run_hidden(pieces, gate, up, e):
    count, (size, width) = len(pieces), pieces[0].shape
    units = gate.shape[2]
    return call(
        functools.partial(hidden_kernel, count, e, min(256, units)),
        [*pieces, gate, up],
        [VMEM_SPEC] * (count + 2),
        [((count * size, units), jnp.bfloat16)],
        [pltpu.VMEM((count * size, width), jnp.bfloat16)],
        8,
        (4 * count * size * width * units, 4 * width * units),
    )[0]


def down_kernel(top, e, tile, feats, pairs, chunk, scalars, hidden, down, table, *refs):
    count = 1 if chunk is None else pairs
    more, outs = refs[:-count], refs[-count:]
    own = hidden.shape[0] // pairs // feats
    if chunk is None:
        blocks = [(p, f) for p in range(pairs) for f in range(feats)]
    else:
        side = jnp.bitwise_xor(scalars[1], chunk)
        blocks = [(p, 2 * f + side) for p in range(pairs) for f in range(feats // 2)]

    def rows_of(ref):
        if chunk is None:
            return ref[...]
        starts = [pl.multiple_of((p * feats + f) * own, own) for p, f in blocks]
        return jnp.concatenate([ref[pl.ds(start, own), :] for start in starts], axis=0)

    entries = []
    for p, f in blocks:
        start = (jnp.bitwise_xor(scalars[2], f) * pairs + p) * own
        entries.append(full(table[pl.ds(pl.multiple_of(start, own), own), :]))
    entries = jnp.concatenate(entries, axis=0)
    lane = lax.broadcasted_iota(jnp.int32, entries.shape, 1)
    expert = (scalars[0] * down.shape[0] + e).astype(jnp.float32)
    chosen = jnp.where((entries == expert) & (lane < top), 1.0, 0.0)
    chosen = pltpu.roll(chosen, top, 1) + pltpu.roll(chosen, 2 * top, 1)
    scale = jnp.sum(chosen * entries, axis=1, keepdims=True)
    rows = rows_of(hidden)
    arrived = rows_of(more[0]) if more else None
    size = outs[0].shape[0]
    for j in range(0, down.shape[2], tile):
        cut = slice(j, j + tile)
        value = dot(rows, down[e, :, cut]) * scale
        if more:
            value += full(arrived[:, cut])
        for p, out in enumerate(outs):
            out[:, cut] = half(value[p * size : (p + 1) * size])


def run_down(hidden, down, e, scalars, table, top, feats, pairs, more=(), chunk=None):
    rows, units = hidden.shape
    width = down.shape[2]
    tile = 256 if width % 256 == 0 else 128
    outs = [((rows, width), jnp.bfloat16)]
    if chunk is not None:
        outs = [((rows // pairs // 2, width), jnp.bfloat16)] * pairs
    return call(
        functools.partial(down_kernel, top, e, tile, feats, pairs, chunk),
        [scalars, hidden, down, table, *more],
        [SMEM_SPEC] + [VMEM_SPEC] * (3 + len(more)),
        outs,
        [],
        8,
        (2 * rows * units * width, 2 * units * width),
    )


def shards(
    tokens,
    expert_ids,
    gate_weights,
    expert_gate,
    expert_up,
    expert_down,
    shared_gate,
    shared_up,
    shared_down,
    encoder,
    encoder_bias,
    decoder,
    decoder_bias,
):
    own, top = expert_ids.shape
    width = tokens.shape[1]
    feats = lax.axis_size("feat")
    pairs = lax.axis_size("expert") // 2
    devices = 2 * pairs * feats
    local_experts = range(expert_gate.shape[0])
    me = lax.axis_index(("expert", "feat"))
    my_feat = lax.axis_index("feat")
    feat_bits = bits_of(feats)
    place = [(my_feat // bit) % 2 for bit in feat_bits]
    scalars = jnp.stack([me, place[0], my_feat])
    chunk_rows = pairs * feats // 2 * own

    table = run_pack(expert_ids, gate_weights)
    table = [table] + [swap(table, "expert", 2 * p) for p in range(1, pairs)]
    sent, table[1] = lax.optimization_barrier((tokens, table[1]))
    table = jnp.concatenate(table, axis=0)
    mine, table = lax.optimization_barrier((tokens, table))
    for bit in feat_bits:
        table = jnp.concatenate([table, swap(table, "feat", bit)], axis=0)
    table_far = swap(table, "expert", 1)

    near = [swap(sent, "expert", 2 * p) for p in range(1, pairs)]
    far = [swap(piece, "expert", 1) for piece in [sent] + near]
    mine, expert_gate, expert_up = run_load([mine, expert_gate, expert_up])
    near = [mine] + near

    hidden = [run_hidden(near, expert_gate, expert_up, e) for e in local_experts]
    hidden[0], *far = lax.optimization_barrier((hidden[0], *far))
    arrived = None
    for e in local_experts:
        more = [] if arrived is None else [arrived]
        arrived = run_down(hidden[e], expert_down, e, scalars, table, top, feats, pairs, more)[0]
    arrived = swap(arrived, "expert", 1)
    for e in local_experts:
        hidden = run_hidden(far, expert_gate, expert_up, e)
        if e < local_experts[-1]:
            more = [arrived]
            arrived = run_down(hidden, expert_down, e, scalars, table_far, top, feats, pairs, more)[0]
    more = [arrived]
    blocks = [
        run_down(hidden, expert_down, e, scalars, table_far, top, feats, pairs, more, chunk)
        for chunk in range(2)
    ]
    blocks = [
        [mine[0]] + [swap(mine[p], "expert", 2 * p) for p in range(1, pairs)] for mine in blocks
    ]
    scalars, blocks[0][-1] = lax.optimization_barrier((scalars, blocks[0][-1]))
    shared_out = run_shared(scalars, far[0], [shared_gate, shared_up, shared_down], own)
    totals = [sum(full(part) for part in blocks[i] + [shared_out[i]]) for i in range(2)]

    total = totals[1] + full(swap(half(totals[0]), "feat", feat_bits[0]))
    total = total.reshape((2,) * (len(feat_bits) - 1) + (own, width))
    for i, bit in enumerate(feat_bits[1:-1]):
        dim = len(feat_bits) - 2 - i
        arrived = swap(half(take(total, 1 - place[i + 1], dim)), "feat", bit)
        total = take(total, place[i + 1], dim) + full(arrived)
    total = half(total)
    moe_out = half(full(total) + full(swap(total, "feat", feat_bits[-1])))
    for bit in feat_bits[-2:0:-1]:
        moe_out = jnp.stack([moe_out, swap(moe_out, "feat", bit)], axis=moe_out.ndim - 2)
    moe_out = moe_out.reshape(-1, width)
    other = swap(moe_out, "feat", feat_bits[0])
    parts = [moe_out] + [swap(moe_out, "expert", 2 * p) for p in range(1, pairs - 1)]
    mine, other = lax.optimization_barrier((moe_out, other))
    parts.append(swap(mine, "expert", 2 * (pairs - 1)))
    sides = [[other] + [swap(other, "expert", 2 * p) for p in range(1, pairs)], parts]

    def encode(x):
        return half(jax.nn.relu(dot(x, encoder) + encoder_bias[None, :]))

    features, blocks, zero = [None, None], [None, None], 0.0
    for chunk in (1, 0):
        near = jnp.stack(sides[chunk]).reshape(chunk_rows, width)
        far = swap(near, "expert", 1)
        features_near = encode(near)
        decoded = swap(half(dot(features_near, decoder)), "expert", 1)
        features_far = encode(far)
        total = half(dot(features_far, decoder) + full(decoded) + zero)
        total = total.reshape(pairs, feats // 2 * own, width)
        blocks[chunk] = [total[0]] + [swap(total[p], "expert", 2 * p) for p in range(1, pairs)]
        zero = 0.0 * full(swap(total[1, :own, :LANES], "expert", 1)[:1, :1])
        both = jnp.stack([features_far, features_near])
        features[chunk] = both.reshape(2, pairs, feats // 2, 1, own, -1)
    arrived = swap(half(sum(full(block) for block in blocks[1])), "feat", feat_bits[0])
    total = sum(full(block) for block in blocks[0])
    total = (total + full(arrived)).reshape((2,) * (len(feat_bits) - 1) + (own, width))
    for bit in feat_bits[1:-1]:
        dim = len(total.shape) - 3
        arrived = swap(half(lax.index_in_dim(total, 1, dim, False)), "feat", bit)
        total = lax.index_in_dim(total, 0, dim, False) + full(arrived)
    arrived = swap(half(take(total, 1 - place[-1], 0)), "feat", feat_bits[-1])
    reconstruction = take(total, place[-1], 0) + full(arrived) + decoder_bias[None, :]

    features = jnp.concatenate(features, axis=3).transpose(1, 0, 2, 3, 4, 5)
    features = features.reshape(devices, own, -1)
    relative = me - me % feats + my_feat % (feats // 2)
    blocks = [lax.dynamic_index_in_dim(features, i ^ relative, 0) for i in range(devices)]
    features = jnp.concatenate(blocks, axis=0).reshape(devices * own, -1)
    return (features, reconstruction)


def solution(mesh):
    return jax.shard_map(
        shards,
        mesh=mesh,
        in_specs=(
            P("expert", None),
            P(("expert", "feat"), None),
            P(("expert", "feat"), None),
            P(("expert", "feat"), None, None),
            P(("expert", "feat"), None, None),
            P(("expert", "feat"), None, None),
            P(None, "feat"),
            P(None, "feat"),
            P("feat", None),
            P(None, ("expert", "feat")),
            P(("expert", "feat")),
            P(("expert", "feat"), None),
            P(),
        ),
        out_specs=(P(None, ("expert", "feat")), P(("expert", "feat"), None)),
        check_vma=False,
    )
```
